32 devices in a mesh: sec: 4 (over x, core), col: 8 (over z, y).
Axes of the slice: x: 2, y: 2, z: 4, core: 2. Of those that a mesh axis runs over, the one named last changes fastest.
Arguments:
- rhs: bfloat16 [256, 64, 256], P(('sec', 'col')), may hold values from -6 to 6
- diag_inv: bfloat16 [256, 64, 64], P(('sec', 'col')), may hold values from -0.5 to 0.5
- off_tiles: bfloat16 [256, 16, 64, 64], P(('sec', 'col')), may hold values from -0.1875 to 0.1875
- targets: int32 [256, 16], P(('sec', 'col')), may hold values from 0 to 63, all different within a row
- row_slot: int32 [4, 64], P('sec'), may hold values from 0 to 63, each once within a row
Outputs:
- solution: bfloat16 [256, 64, 256], P(('sec', 'col'))
- handed_on: bfloat16 [256, 64, 256], P(('sec', 'col'))
The draws below stay inside these ranges and needn't reach their ends.
Inputs may be any that keep to these rules, and one draw needn't show every extreme that they name: The 16 targets of one block are distinct. `row_slot`: each row is a permutation.
All inputs are finite; a program needn't handle non-finite values.
Results may differ from the reference program's by a relative error of at most 0.03.
Values may be sent and summed in bfloat16 or wider, within the bound.
A program may use at most 64 MiB of HBM per device.

```python
import jax
import jax.numpy as jnp
from jax import lax

W = 64
NRHS = 256
NOFF = 16
BPD = 8
NB_SEC = 64
NBLK = 256
N_SEC = 4
N_COL = 8


def level_of(rng, dims, pieces, low, largest):
    gain, own = 1.0, jax.random.fold_in(rng, 6)
    for dim, shards_of in pieces:
        steps = jnp.exp(jax.random.uniform(jax.random.fold_in(own, dim), (shards_of,), jnp.float32, low / len(pieces), largest / len(pieces)))
        gain = gain * jnp.repeat(steps, dims[dim] // shards_of).reshape([-1 if axis == dim else 1 for axis in range(len(dims))])
    return gain


def distinct(rng, rows, amount, top, lift):
    order = jax.random.permutation(jax.random.fold_in(rng, 1), amount)
    favour = order
    for power in range(3):
        favour = favour * favour // amount
    favour = favour * lift // amount
    lots = jax.random.randint(jax.random.fold_in(rng, 2), (rows, amount), 0, 4096) + favour
    holders = jax.random.permutation(jax.random.fold_in(rng, 3), rows)[jnp.arange(amount) % rows]
    lots = jnp.where(jnp.arange(rows)[:, None] == holders[None, :], 1 << 14, lots)
    score = lots * amount + jnp.arange(amount)
    return lax.top_k(score.astype(jnp.int32), top)[1].astype(jnp.int32)


def scatter_about(stream_key, dims, scale, bound, cuts=(), dtype=jnp.bfloat16):
    result = jax.random.normal(stream_key, dims, jnp.float32) * scale
    if len(cuts) > 0:
        result = level_of(stream_key, dims, cuts, -0.22, 0.18) * result
    return jnp.clip(result, min=-bound, max=bound).astype(dtype)


def setup_inputs(seed: int = 0) -> dict:
    seeds = jax.random.split(jax.random.key(seed), 6)
    rhs = scatter_about(seeds[0], (NBLK, W, NRHS), 1.0, 6.0, ((0, 32),))
    diag_inv = scatter_about(seeds[1], (NBLK, W, W), (2 * W) ** -0.5, 0.5, ((0, 32),))
    off_tiles = scatter_about(seeds[2], (NBLK, NOFF, W, W), (W * NOFF) ** -0.5, 0.1875, ((0, 32),))
    targets = distinct(seeds[3], NBLK, NB_SEC, NOFF, 4096)
    row_slot = jax.vmap(lambda own: jax.random.permutation(own, NB_SEC))(jax.random.split(seeds[4], N_SEC)).reshape((N_SEC, NB_SEC)).astype(jnp.int32)
    return dict(rhs=rhs, diag_inv=diag_inv, off_tiles=off_tiles, targets=targets, row_slot=row_slot)


def reference(rhs, diag_inv, off_tiles, targets, row_slot):
    count = NB_SEC
    incoming = jnp.zeros((count, W, NRHS), jnp.bfloat16)
    solved_all = []
    handed_all = []
    for section in range(N_SEC):
        start = section * count
        residual = (rhs[start:start + count].astype(jnp.float32) - incoming.astype(jnp.float32)).astype(jnp.bfloat16)
        solved = jnp.einsum("kab,kbn->kan", diag_inv[start:start + count].astype(jnp.float32), residual.astype(jnp.float32)).astype(jnp.bfloat16)
        tiles = jnp.einsum("kpab,kbn->kpan", off_tiles[start:start + count].astype(jnp.float32), solved.astype(jnp.float32)).astype(jnp.bfloat16)
        dest_slot = row_slot[section][targets[start:start + count]]
        tiles = tiles.reshape(N_COL, BPD * NOFF, W, NRHS)
        dest_slot = dest_slot.reshape(N_COL, BPD * NOFF).astype(jnp.int32)

        def device_sum(carry, item):
            piece, slots = item
            partial_value = jnp.zeros((count, W, NRHS), jnp.float32).at[slots].add(piece.astype(jnp.float32))
            rounded = lax.optimization_barrier(partial_value.astype(jnp.bfloat16))
            return carry + rounded.astype(jnp.float32), None

        total, _ = lax.scan(device_sum, jnp.zeros((count, W, NRHS), jnp.float32), (tiles, dest_slot))
        incoming = total.astype(jnp.bfloat16)
        solved_all.append(solved)
        handed_all.append(incoming)
    return jnp.concatenate(solved_all, 0), jnp.concatenate(handed_all, 0)
```

```python
import functools

import jax
import jax.numpy as jnp
from jax import lax
from jax.experimental import pallas as pl
from jax.experimental.pallas import tpu as pltpu
from jax.sharding import PartitionSpec as P

MESH = pl.DeviceIdType.MESH
OWN, MIRROR, OTHER = 0, 1, 2


def low_size(n_col):
    low = 1
    while (2 * low) ** 2 <= n_col:
        low *= 2
    return low


def kernel(
    dims, targets_ref, slot_ref, rhs_hbm, diag_hbm, off_hbm, sol_ref, hand_ref,
    rin, diag_ref, off_ref, pack_own, pack_mirror, idx_vec, idx_ref,
    a_ref, x_ref, inc, send1, recv1, send2, recv2, acc, passed, ret,
    in_sem, fs_sem, fr_sem, s1_sem, r1_sem, s2_sem, r2_sem, sp_sem, rp_sem, sr_sem, rr_sem,
):
    n_sec, n_hi, n_lo = dims
    half = n_sec // 2
    blocks, width = off_hbm.shape[0], off_hbm.shape[2]
    noff = off_hbm.shape[1]
    rows = slot_ref.shape[1]
    lanes = idx_vec.shape[2]
    nc = rin.shape[3]
    size = blocks * width
    pairs = blocks // 2
    sec = lax.axis_index("sec")
    col = lax.axis_index("col")
    plane, place = sec // half, sec % half
    hi, lo = col // n_lo, col % n_lo
    mirror = {"sec": lax.rem(sec + half, n_sec), "col": col}

    def columns_of(which):
        return pl.ds(pl.multiple_of(which * nc, nc), nc)

    loads = [
        pltpu.make_async_copy(off_hbm, off_ref, in_sem.at[0]),
        pltpu.make_async_copy(diag_hbm, diag_ref.at[OWN], in_sem.at[1]),
        pltpu.make_async_copy(rhs_hbm.at[:, :, columns_of(plane)], rin.at[OWN], in_sem.at[2]),
        pltpu.make_async_copy(rhs_hbm.at[:, :, columns_of(1 - plane)], rin.at[OTHER], in_sem.at[3]),
    ]
    for load in loads:
        load.start()

    def lo_peer(o):
        return {"sec": sec, "col": hi * n_lo + lax.rem(lo + o, n_lo)}

    def hi_flip(o):
        value, bit = hi, 1
        while bit < n_hi:
            if o & bit:
                value = value + bit - 2 * bit * ((value // bit) % 2)
            bit *= 2
        return value

    def hi_peer(o):
        return {"sec": sec, "col": hi_flip(o) * n_lo + lo}

    barrier = pltpu.get_barrier_semaphore()
    for o in range(1, n_lo):
        pl.semaphore_signal(barrier, inc=1, device_id=lo_peer(o), device_id_type=MESH)
    for o in range(1, n_hi):
        pl.semaphore_signal(barrier, inc=1, device_id=hi_peer(o), device_id_type=MESH)
    for o in range(1, n_sec):
        pl.semaphore_signal(
            barrier, inc=1, device_id={"sec": lax.rem(sec + o, n_sec), "col": col},
            device_id_type=MESH,
        )

    slot_of_lane = lax.broadcasted_iota(jnp.int32, (1, lanes), 1)
    for k in range(blocks):
        found = jnp.full((1, lanes), noff, jnp.int32)
        for p in range(noff):
            dest = slot_ref[0, targets_ref[k, p]]
            found = jnp.where(slot_of_lane == dest, p, found)
        idx_vec[OWN, k:k + 1, :] = found
    to_scalar = pltpu.make_async_copy(idx_vec.at[OWN], idx_ref.at[OWN], in_sem.at[4])
    to_scalar.start()

    packs = (pack_own, pack_mirror)
    for pack_ref in packs:
        for q in range(pairs):
            pack_ref[q, noff] = jnp.zeros((width, 2 * width), jnp.bfloat16)
    for load in loads:
        load.wait()

    def pack(p, carry):
        for q in range(pairs):
            pack_own[q, p] = jnp.concatenate([off_ref[2 * q, p], off_ref[2 * q + 1, p]], axis=1)
        return carry

    lax.fori_loop(0, noff, pack, 0)
    to_scalar.wait()
    pl.semaphore_wait(barrier, n_lo - 1 + n_hi - 1 + n_sec - 1)

    def factor_copies():
        ends = [
            (idx_vec.at[OWN], idx_vec.at[MIRROR]),
            (diag_ref.at[OWN], diag_ref.at[MIRROR]),
            (rin.at[OTHER], rin.at[MIRROR]),
        ] + [
            (pack_own.at[q, pl.ds(0, noff)], pack_mirror.at[q, pl.ds(0, noff)])
            for q in range(pairs)
        ]
        return [
            pltpu.make_async_remote_copy(
                src_ref=src, dst_ref=dst, send_sem=fs_sem.at[n], recv_sem=fr_sem.at[n],
                device_id=mirror, device_id_type=MESH,
            )
            for n, (src, dst) in enumerate(ends)
        ]

    @pl.when(sec != 0)
    def _():
        for copy in factor_copies():
            copy.start()

    def mirror_factor():
        for copy in factor_copies():
            copy.wait_recv()
        to_scalar = pltpu.make_async_copy(idx_vec.at[MIRROR], idx_ref.at[MIRROR], in_sem.at[5])
        to_scalar.start()
        to_scalar.wait()

    def source(role):
        return lax.rem(role + plane, 2)

    left = lax.broadcasted_iota(jnp.int32, (width, 2 * width), 1) < width

    def build_row(role, src, i):
        pack_ref = packs[src]
        for q in range(pairs):
            a_ref[role, i, :, 2 * q * width:2 * (q + 1) * width] = jnp.where(
                left,
                pack_ref[q, idx_ref[src, 2 * q, i]],
                pack_ref[q, idx_ref[src, 2 * q + 1, i]],
            )

    def build_all(role):
        for src in (OWN, MIRROR):
            @pl.when(source(role) == src)
            def _():
                def step(i, carry):
                    build_row(role, src, i)
                    return carry

                lax.fori_loop(0, rows, step, 0)

    def copy1(j, o, oh):
        return pltpu.make_async_remote_copy(
            src_ref=send1.at[j, o - 1, oh], dst_ref=recv1.at[j, o - 1, oh],
            send_sem=s1_sem.at[j, o - 1, oh], recv_sem=r1_sem.at[j, o - 1, oh],
            device_id=lo_peer(o), device_id_type=MESH,
        )

    def copy2(j, oh):
        return pltpu.make_async_remote_copy(
            src_ref=send2.at[j, oh - 1], dst_ref=recv2.at[j, oh - 1],
            send_sem=s2_sem.at[j, oh - 1], recv_sem=r2_sem.at[j, oh - 1],
            device_id=hi_peer(oh), device_id_type=MESH,
        )

    def copyp(j, to_sec, slot):
        return pltpu.make_async_remote_copy(
            src_ref=passed.at[j], dst_ref=inc.at[slot],
            send_sem=sp_sem.at[j], recv_sem=rp_sem.at[slot],
            device_id={"sec": to_sec, "col": col}, device_id_type=MESH,
        )

    def pass_on(j):
        if j == 0:
            return copyp(0, half + 1, 0)
        more = place + 1 < half
        to_sec = plane * half + jnp.where(more, place + 1, 0)
        if j == 1:
            return copyp(1, to_sec, jnp.where(more, 0, 1))
        return copyp(2, to_sec, 1)

    def give_back(which, j):
        return pltpu.make_async_remote_copy(
            src_ref=(x_ref, passed)[which].at[j], dst_ref=ret.at[which],
            send_sem=sr_sem.at[which], recv_sem=rr_sem.at[which],
            device_id=mirror, device_id_type=MESH,
        )

    order = list(range(n_hi - 1, -1, -1))

    def product(j, oh, o):
        role = max(j - 1, 0)
        dest = hi_flip(oh) * n_lo + lax.rem(lo + o, n_lo)
        if j == 0:
            for r in range(blocks):
                build_row(0, OWN, dest * blocks + r)
        a = a_ref[role, pl.ds(dest * blocks, blocks)].reshape(size, size)
        return jnp.dot(a, x_ref[j], preferred_element_type=jnp.float32)

    def first(j, fresh):
        role = max(j - 1, 0)
        src = source(role)
        which = OTHER if j == 0 else src
        if not fresh:
            copyp(j, sec, role).wait_recv()
        for k in range(blocks):
            part = slice(k * width, (k + 1) * width)
            residual = rin[which, k]
            if not fresh:
                residual = (
                    residual.astype(jnp.float32) - inc[role, part, :].astype(jnp.float32)
                ).astype(jnp.bfloat16)
            x_ref[j, part, :] = jnp.dot(
                diag_ref[src, k], residual, preferred_element_type=jnp.float32
            ).astype(jnp.bfloat16)
        for oh in order:
            for o in range(1, n_lo):
                send1[j, o - 1, oh] = product(j, oh, o).astype(jnp.bfloat16)
                copy1(j, o, oh).start()

    def middle(j):
        for oh in order:
            total = product(j, oh, 0)
            for o in range(1, n_lo):
                copy1(j, o, oh).wait_recv()
                total = total + recv1[j, o - 1, oh].astype(jnp.float32)
            if oh == 0:
                acc[j] = total
            else:
                send2[j, oh - 1] = total.astype(jnp.bfloat16)
                copy2(j, oh).start()

    def last(j):
        total = acc[j]
        for oh in range(1, n_hi):
            copy2(j, oh).wait_recv()
            total = total + recv2[j, oh - 1].astype(jnp.float32)
        passed[j] = total.astype(jnp.bfloat16)
        if j < 2:
            pass_on(j).start()
        else:
            @pl.when(place < half - 1)
            def _():
                pass_on(j).start()

        if j > 0:
            @pl.when(source(j - 1) == MIRROR)
            def _():
                give_back(0, j).start()
                give_back(1, j).start()

    def sent(j):
        for oh in range(n_hi):
            for o in range(1, n_lo):
                copy1(j, o, oh).wait_send()
        for oh in range(1, n_hi):
            copy2(j, oh).wait_send()

    @pl.when(sec == 0)
    def _():
        first(0, True)
        middle(0)
        first(1, True)
        last(0)
        middle(1)
        last(1)
        sent(0)
        sent(1)
        pass_on(0).wait_send()
        pass_on(1).wait_send()

    @pl.when(place > 0)
    def _():
        @pl.when(plane == 1)
        def _():
            mirror_factor()

        build_all(0)
        first(1, False)
        middle(1)
        last(1)
        sent(1)
        pass_on(1).wait_send()

    @pl.when(plane == 0)
    def _():
        mirror_factor()

    build_all(1)
    first(2, False)
    middle(2)
    last(2)
    own = 1 + plane
    sol_ref[:, :, columns_of(plane)] = x_ref[own].reshape(blocks, width, nc)
    hand_ref[:, :, columns_of(plane)] = passed[own].reshape(blocks, width, nc)

    @pl.when(sec == 0)
    def _():
        sol_ref[:, :, nc:2 * nc] = x_ref[0].reshape(blocks, width, nc)
        hand_ref[:, :, nc:2 * nc] = passed[0].reshape(blocks, width, nc)

    @pl.when(sec != 0)
    def _():
        give_back(0, 1).wait_recv()
        sol_ref[:, :, columns_of(1 - plane)] = ret[0].reshape(blocks, width, nc)
        give_back(1, 1).wait_recv()
        hand_ref[:, :, columns_of(1 - plane)] = ret[1].reshape(blocks, width, nc)
        for copy in factor_copies():
            copy.wait_send()

    sent(2)

    @pl.when(place < half - 1)
    def _():
        pass_on(2).wait_send()

    @pl.when(sec != half)
    def _():
        give_back(0, 1).wait_send()
        give_back(1, 1).wait_send()


def mirrored(n_sec, n_col, rhs, diag_inv, off_tiles, targets, row_slot):
    blocks, width, columns = rhs.shape
    noff = off_tiles.shape[1]
    rows = row_slot.shape[1]
    n_lo = low_size(n_col)
    n_hi = n_col // n_lo
    nc = columns // 2
    size = blocks * width
    pairs = blocks // 2
    lanes = -(-rows // 128) * 128

    vmem = pl.BlockSpec(memory_space=pltpu.VMEM)
    smem = pl.BlockSpec(memory_space=pltpu.SMEM)
    hbm = pl.BlockSpec(memory_space=pl.ANY)
    out = jax.ShapeDtypeStruct((blocks, width, columns), jnp.bfloat16)
    dma = pltpu.SemaphoreType.DMA
    bf16 = jnp.bfloat16
    return pl.pallas_call(
        functools.partial(kernel, (n_sec, n_hi, n_lo)),
        out_shape=(out, out),
        in_specs=[smem, smem, hbm, hbm, hbm],
        out_specs=(vmem, vmem),
        scratch_shapes=[
            pltpu.VMEM((3, blocks, width, nc), bf16),
            pltpu.VMEM((2, blocks, width, width), bf16),
            pltpu.VMEM((blocks, noff, width, width), bf16),
            pltpu.VMEM((pairs, noff + 1, width, 2 * width), bf16),
            pltpu.VMEM((pairs, noff + 1, width, 2 * width), bf16),
            pltpu.VMEM((2, blocks, lanes), jnp.int32),
            pltpu.SMEM((2, blocks, lanes), jnp.int32),
            pltpu.VMEM((2, rows, width, size), bf16),
            pltpu.VMEM((3, size, nc), bf16),
            pltpu.VMEM((2, size, nc), bf16),
            pltpu.VMEM((3, n_lo - 1, n_hi, size, nc), bf16),
            pltpu.VMEM((3, n_lo - 1, n_hi, size, nc), bf16),
            pltpu.VMEM((3, n_hi - 1, size, nc), bf16),
            pltpu.VMEM((3, n_hi - 1, size, nc), bf16),
            pltpu.VMEM((3, size, nc), jnp.float32),
            pltpu.VMEM((3, size, nc), bf16),
            pltpu.VMEM((2, size, nc), bf16),
            dma((6,)),
            dma((3 + pairs,)),
            dma((3 + pairs,)),
            dma((3, n_lo - 1, n_hi)),
            dma((3, n_lo - 1, n_hi)),
            dma((3, n_hi - 1)),
            dma((3, n_hi - 1)),
            dma((3,)),
            dma((2,)),
            dma((2,)),
            dma((2,)),
        ],
        compiler_params=pltpu.CompilerParams(
            collective_id=0, has_side_effects=True, vmem_limit_bytes=60 * 1024 * 1024
        ),
    )(targets, row_slot, rhs, diag_inv, off_tiles)


def chains_kernel(
    dims, targets_ref, slot_ref, rhs_hbm, diag_hbm, off_hbm, sol_ref, hand_ref,
    rhs_ref, off_ref, pack_0, pack_1, pack_2, pack_3, diag_ref, idx_vec, idx_ref, rin, a_ref, w_ref,
    send1, recv1, send2, recv2, acc, xs, hs, inc, ret,
    in_sem, fs_sem, fr_sem, rs_sem, rr_sem, s1_sem, r1_sem, s2_sem, r2_sem, p_sem, gs_sem, gr_sem,
):
    n_hi, n_lo = dims
    blocks, noff, width = off_hbm.shape[:3]
    lanes = idx_vec.shape[2]
    pairs = blocks // 2
    size = blocks * width
    packed = pairs * width
    wide = 2 * width
    sec = lax.axis_index("sec")
    col = lax.axis_index("col")
    plane, place = sec // 2, sec % 2
    hi, lo = col // n_lo, col % n_lo
    bf16, f32 = jnp.bfloat16, jnp.float32

    own_idx = pltpu.make_async_copy(idx_vec.at[sec], idx_ref.at[sec], in_sem.at[0])
    load_off = pltpu.make_async_copy(off_hbm, off_ref, in_sem.at[1])
    load_diag = pltpu.make_async_copy(diag_hbm, diag_ref.at[sec], in_sem.at[2])
    load_rhs = pltpu.make_async_copy(rhs_hbm, rhs_ref, in_sem.at[3])
    for load in (load_off, load_diag, load_rhs):
        load.start()

    def hi_flip(o):
        value, bit = hi, 1
        while bit < n_hi:
            value = value + ((o // bit) % 2) * (bit - 2 * bit * ((value // bit) % 2))
            bit *= 2
        return value

    def at_sec(to):
        return {"sec": to, "col": col}

    lo_peer = {"sec": sec, "col": hi * n_lo + 1 - lo}

    def hi_peer(o):
        return {"sec": sec, "col": hi_flip(o) * n_lo + lo}

    barrier = pltpu.get_barrier_semaphore()
    peers = [lo_peer] + [hi_peer(o) for o in range(1, n_hi)]
    peers += [at_sec(lax.rem(sec + o, 4)) for o in range(1, 4)]
    for peer in peers:
        pl.semaphore_signal(barrier, inc=1, device_id=peer, device_id_type=MESH)

    slot_of_lane = lax.broadcasted_iota(jnp.int32, (1, lanes), 1)
    for k in range(blocks):
        found = jnp.full((1, lanes), noff, jnp.int32)
        for p in range(noff):
            dest = slot_ref[0, targets_ref[k, p]]
            found = jnp.where(slot_of_lane == dest, p, found)
        idx_vec[sec, k:k + 1, :] = found
    own_idx.start()
    packs = (pack_0, pack_1, pack_2, pack_3)
    for pack_ref in packs:
        for q in range(pairs):
            pack_ref[q, noff] = jnp.zeros((width, wide), bf16)

    left = lax.broadcasted_iota(jnp.int32, (width, wide), 1) < width

    def swap(x):
        return jnp.concatenate([x[:, width:], x[:, :width]], axis=1)

    load_off.wait()

    def pack_into(pack_ref):
        def step(p, carry):
            for q in range(pairs):
                pack_ref[q, p] = jnp.concatenate([off_ref[2 * q, p], off_ref[2 * q + 1, p]], axis=1)
            return carry

        lax.fori_loop(0, noff, step, 0)

    for s in range(4):
        @pl.when(sec == s)
        def _():
            pack_into(packs[s])

    load_diag.wait()
    load_rhs.wait()
    own_idx.wait()
    pl.semaphore_wait(barrier, len(peers))

    def factor(s, to, step):
        ends = [idx_vec.at[s], diag_ref.at[s]]
        ends += [packs[s].at[q, pl.ds(0, noff)] for q in range(pairs)]
        return [
            pltpu.make_async_remote_copy(
                src_ref=end, dst_ref=end, send_sem=fs_sem.at[step, n], recv_sem=fr_sem.at[s, n],
                device_id=at_sec(to), device_id_type=MESH,
            )
            for n, end in enumerate(ends)
        ]

    def start(copies):
        for copy in copies:
            copy.start()

    def wait_sent(copies):
        for copy in copies:
            copy.wait_send()

    def factor_here(s):
        for copy in factor(s, 0, 0):
            copy.wait_recv()
        to_scalar = pltpu.make_async_copy(idx_vec.at[s], idx_ref.at[s], in_sem.at[0])
        to_scalar.start()
        to_scalar.wait()

    def rhs_copy(s, chain, to, step):
        return pltpu.make_async_remote_copy(
            src_ref=rin.at[s, chain], dst_ref=rin.at[s, chain],
            send_sem=rs_sem.at[step], recv_sem=rr_sem.at[s, chain // 2],
            device_id=at_sec(to), device_id_type=MESH,
        )

    other = plane * 2 + 1 - place
    for s in range(4):
        @pl.when(sec == s)
        def _():
            start(factor(s, other, 0))

    for m in range(2):
        part = slice(m * wide, (m + 1) * wide)
        for q in range(pairs):
            even, odd = rhs_ref[2 * q, :, part], rhs_ref[2 * q + 1, :, part]
            rows = slice(q * width, (q + 1) * width)
            rin[sec, 2 * m, rows] = jnp.where(left, even, swap(odd))
            rin[sec, 2 * m + 1, rows] = jnp.where(left, swap(even), odd)

    def rhs_sends():
        first_set = [rhs_copy(sec, 1 - place, other, 0)]
        return first_set, [rhs_copy(sec, 3 - place, other, 1)], [
            rhs_copy(sec, 2, 0, 1), rhs_copy(sec, 3, 1, 2),
        ]

    start(rhs_sends()[0])

    @pl.when(plane == 0)
    def _():
        start(rhs_sends()[1])

    @pl.when(plane == 1)
    def _():
        start(rhs_sends()[2])
        for s in (2, 3):
            @pl.when(sec == s)
            def _():
                start(factor(s, place, 1))

    def rhs_here(s, m):
        rhs_copy(s, 2 * m + place, 0, 0).wait_recv()

    def build(s, d):
        for r in range(blocks):
            i = d * blocks + r
            for q in range(pairs):
                at = (r % 2) * size + q * wide
                a_ref[s, d * pairs + r // 2, :, at:at + wide] = jnp.where(
                    left, packs[s][q, idx_ref[s, 2 * q, i]], packs[s][q, idx_ref[s, 2 * q + 1, i]]
                )

    def build_range(s, low, high):
        def step(d, carry):
            build(s, d)
            return carry

        lax.fori_loop(low, high, step, 0)

    def copy1(j, oh):
        return pltpu.make_async_remote_copy(
            src_ref=send1.at[j, oh], dst_ref=recv1.at[j, oh],
            send_sem=s1_sem.at[j, oh], recv_sem=r1_sem.at[j, oh],
            device_id=lo_peer, device_id_type=MESH,
        )

    def copy2(j, oh):
        return pltpu.make_async_remote_copy(
            src_ref=send2.at[j, oh - 1], dst_ref=recv2.at[j, oh - 1],
            send_sem=s2_sem.at[j, oh - 1], recv_sem=r2_sem.at[j, oh - 1],
            device_id=hi_peer(oh), device_id_type=MESH,
        )

    def slot(m, s):
        return s % 2 if m == 0 else 2 + s

    def give(which, m, s):
        j = slot(m, s)
        return pltpu.make_async_remote_copy(
            src_ref=(xs, hs)[which].at[j], dst_ref=ret.at[which, 2 * m + place],
            send_sem=gs_sem.at[which, j], recv_sem=gr_sem.at[which, 2 * m + place],
            device_id=at_sec(s), device_id_type=MESH,
        )

    def give_out(which, m, s):
        @pl.when(sec == s)
        def _():
            ret[which, 2 * m + place] = (xs, hs)[which][slot(m, s)]

        @pl.when(sec != s)
        def _():
            give(which, m, s).start()

    def product(m, s, dest):
        a = a_ref[s, pl.ds(dest * pairs, pairs)].reshape(packed, 2 * size)
        return jnp.dot(a, w_ref[m], preferred_element_type=f32)

    def first(m, s, h, fresh=False):
        j = slot(m, s)
        for q in range(pairs):
            rows = slice(q * width, (q + 1) * width)
            residual = rin[s, 2 * m + place, rows]
            if h is not None:
                residual = (residual.astype(f32) - h[rows].astype(f32)).astype(bf16)
            z = jnp.dot(
                diag_ref[s, 2 * q:2 * q + 2].reshape(wide, width), residual,
                preferred_element_type=f32,
            ).astype(bf16)
            top, low = z[:width], z[width:]
            xs[j, rows] = jnp.where(left, top, low)
            zero = jnp.zeros_like(top)
            at = q * wide
            w_ref[m, at:at + width] = jnp.where(left, top, zero)
            w_ref[m, at + width:at + wide] = jnp.where(left, swap(low), zero)
            w_ref[m, size + at:size + at + width] = jnp.where(left, zero, swap(top))
            w_ref[m, size + at + width:size + at + wide] = jnp.where(left, zero, low)

        def step(t, carry):
            oh = n_hi - 1 - t
            dest = hi_flip(oh) * n_lo + 1 - lo
            if fresh:
                build(s, dest)
            send1[j, oh] = product(m, s, dest).astype(bf16)
            copy1(j, oh).start()
            return carry

        lax.fori_loop(0, n_hi, step, 0)
        give_out(0, m, s)

    def middle(m, s, fresh=False, also=None):
        j = slot(m, s)

        def step(t, carry):
            oh = n_hi - 1 - t
            dest = hi_flip(oh) * n_lo + lo
            if fresh:
                build(s, dest)
            total = product(m, s, dest)
            copy1(j, oh).wait_recv()
            total = total + recv1[j, oh].astype(f32)

            @pl.when(oh > 0)
            def _():
                send2[j, oh - 1] = total.astype(bf16)
                copy2(j, oh).start()

            @pl.when(oh == 0)
            def _():
                acc[m] = total

            if also is not None:
                build(also, 2 * t)
                build(also, 2 * t + 1)
            return carry

        lax.fori_loop(0, n_hi, step, 0)

    def last(m, s):
        j = slot(m, s)
        total = acc[m]
        for oh in range(n_hi - 1, 0, -1):
            copy2(j, oh).wait_recv()
            total = total + recv2[j, oh - 1].astype(f32)
        hs[j] = total.astype(bf16)

    def sent(m, s):
        j = slot(m, s)
        for oh in range(n_hi):
            copy1(j, oh).wait_send()
        for oh in range(1, n_hi):
            copy2(j, oh).wait_send()

        @pl.when(sec != s)
        def _():
            give(0, m, s).wait_send()
            give(1, m, s).wait_send()

    def pass_on():
        return pltpu.make_async_remote_copy(
            src_ref=hs.at[1], dst_ref=inc, send_sem=p_sem.at[0], recv_sem=p_sem.at[1],
            device_id=at_sec(2 + place), device_id_type=MESH,
        )

    @pl.when(plane == 0)
    def _():
        @pl.when(place == 1)
        def _():
            factor_here(0)
            rhs_here(0, 0)
            rhs_here(0, 1)

        first(0, 0, None, fresh=True)
        first(1, 0, None)
        middle(0, 0, fresh=True)

        @pl.when(place == 0)
        def _():
            factor_here(1)
            rhs_here(1, 0)
            rhs_here(1, 1)

        middle(1, 0, also=1)
        last(0, 0)
        first(0, 1, hs.at[0])
        give_out(1, 0, 0)
        last(1, 0)
        first(1, 1, hs.at[2])
        give_out(1, 1, 0)
        middle(0, 1)

        @pl.when(place == 0)
        def _():
            factor_here(2)
            start(factor(2, 1, 1))

        @pl.when(place == 1)
        def _():
            factor_here(3)
            start(factor(3, 0, 1))

        last(0, 1)
        pass_on().start()
        give_out(1, 0, 1)

        @pl.when(place == 1)
        def _():
            factor_here(2)

        @pl.when(place == 0)
        def _():
            factor_here(3)

        middle(1, 1, also=2)
        last(1, 1)
        rhs_here(2, 1)
        first(1, 2, hs.at[3])
        give_out(1, 1, 1)
        middle(1, 2, also=3)
        last(1, 2)
        rhs_here(3, 1)
        first(1, 3, hs.at[4])
        give_out(1, 1, 2)
        middle(1, 3)
        last(1, 3)
        give_out(1, 1, 3)
        for s in range(2):
            sent(0, s)
        for s in range(4):
            sent(1, s)
        pass_on().wait_send()

    @pl.when(plane == 1)
    def _():
        @pl.when(place == 0)
        def _():
            factor_here(3)
            rhs_here(3, 0)

        @pl.when(place == 1)
        def _():
            factor_here(2)
            rhs_here(2, 0)

        build_range(2, 0, n_hi * n_lo)
        build_range(3, 0, n_hi * n_lo)
        pass_on().wait_recv()
        first(0, 2, inc)
        middle(0, 2)
        last(0, 2)
        first(0, 3, hs.at[0])
        give_out(1, 0, 2)
        middle(0, 3)
        last(0, 3)
        give_out(1, 0, 3)
        sent(0, 2)
        sent(0, 3)

    def returned(which, chain):
        return pltpu.make_async_remote_copy(
            src_ref=xs.at[0], dst_ref=ret.at[which, chain],
            send_sem=gs_sem.at[which, 0], recv_sem=gr_sem.at[which, chain],
            device_id=at_sec(other), device_id_type=MESH,
        )

    for which, out in ((0, sol_ref), (1, hand_ref)):
        for m in range(2):
            returned(which, 2 * m + 1 - place).wait_recv()
            if m == 1:
                @pl.when(plane == 1)
                def _():
                    returned(which, 2 + place).wait_recv()

            part = slice(m * wide, (m + 1) * wide)
            for q in range(pairs):
                rows = slice(q * width, (q + 1) * width)
                one, two = ret[which, 2 * m, rows], ret[which, 2 * m + 1, rows]
                out[2 * q, :, part] = jnp.where(left, one, swap(two))
                out[2 * q + 1, :, part] = jnp.where(left, swap(one), two)

    wait_sent(factor(0, other, 0))
    wait_sent(factor(0, other, 1))
    wait_sent(rhs_sends()[0])

    @pl.when(plane == 0)
    def _():
        wait_sent(rhs_sends()[1])

    @pl.when(plane == 1)
    def _():
        wait_sent(rhs_sends()[2])


def chains(n_col, rhs, diag_inv, off_tiles, targets, row_slot):
    blocks, width, columns = rhs.shape
    noff = off_tiles.shape[1]
    rows = row_slot.shape[1]
    n_lo = 2
    n_hi = n_col // n_lo
    size = blocks * width
    pairs = blocks // 2
    packed = pairs * width
    wide = 2 * width
    lanes = -(-rows // 128) * 128
    vmem = pl.BlockSpec(memory_space=pltpu.VMEM)
    smem = pl.BlockSpec(memory_space=pltpu.SMEM)
    hbm = pl.BlockSpec(memory_space=pl.ANY)
    out = jax.ShapeDtypeStruct((blocks, width, columns), jnp.bfloat16)
    dma = pltpu.SemaphoreType.DMA
    bf16 = jnp.bfloat16
    return pl.pallas_call(
        functools.partial(chains_kernel, (n_hi, n_lo)),
        out_shape=(out, out),
        in_specs=[smem, smem, hbm, hbm, hbm],
        out_specs=(vmem, vmem),
        scratch_shapes=[
            pltpu.VMEM((blocks, width, columns), bf16),
            pltpu.VMEM((blocks, noff, width, width), bf16),
            pltpu.VMEM((pairs, noff + 1, width, wide), bf16),
            pltpu.VMEM((pairs, noff + 1, width, wide), bf16),
            pltpu.VMEM((pairs, noff + 1, width, wide), bf16),
            pltpu.VMEM((pairs, noff + 1, width, wide), bf16),
            pltpu.VMEM((4, blocks, width, width), bf16),
            pltpu.VMEM((4, blocks, lanes), jnp.int32),
            pltpu.SMEM((4, blocks, lanes), jnp.int32),
            pltpu.VMEM((4, 4, packed, wide), bf16),
            pltpu.VMEM((4, rows // 2, width, 2 * size), bf16),
            pltpu.VMEM((2, 2 * size, wide), bf16),
            pltpu.VMEM((6, n_hi, packed, wide), bf16),
            pltpu.VMEM((6, n_hi, packed, wide), bf16),
            pltpu.VMEM((6, n_hi - 1, packed, wide), bf16),
            pltpu.VMEM((6, n_hi - 1, packed, wide), bf16),
            pltpu.VMEM((2, packed, wide), jnp.float32),
            pltpu.VMEM((6, packed, wide), bf16),
            pltpu.VMEM((6, packed, wide), bf16),
            pltpu.VMEM((packed, wide), bf16),
            pltpu.VMEM((2, 4, packed, wide), bf16),
            dma((4,)),
            dma((2, 2 + pairs)),
            dma((4, 2 + pairs)),
            dma((3,)),
            dma((4, 2)),
            dma((6, n_hi)),
            dma((6, n_hi)),
            dma((6, n_hi - 1)),
            dma((6, n_hi - 1)),
            dma((2,)),
            dma((2, 6)),
            dma((2, 4)),
        ],
        compiler_params=pltpu.CompilerParams(
            collective_id=1, has_side_effects=True, vmem_limit_bytes=60 * 1024 * 1024
        ),
    )(targets, row_slot, rhs, diag_inv, off_tiles)


def fits_chains(n_sec, n_col, rhs, row_slot):
    blocks, width, columns = rhs.shape
    n_hi = n_col // 2
    return (
        n_sec == 4 and n_col % 2 == 0 and n_hi & (n_hi - 1) == 0 and columns == 4 * width and width == 64
        and blocks % 2 == 0 and row_slot.shape[1] == blocks * n_col
    )


def shards(n_sec, n_col, rhs, diag_inv, off_tiles, targets, row_slot):
    if fits_chains(n_sec, n_col, rhs, row_slot):
        return chains(n_col, rhs, diag_inv, off_tiles, targets, row_slot)
    return mirrored(n_sec, n_col, rhs, diag_inv, off_tiles, targets, row_slot)


def solution(mesh):
    return jax.shard_map(
        functools.partial(shards, mesh.shape["sec"], mesh.shape["col"]),
        mesh=mesh,
        in_specs=(
            P(("sec", "col"), None, None),
            P(("sec", "col"), None, None),
            P(("sec", "col"), None, None, None),
            P(("sec", "col"), None),
            P("sec", None),
        ),
        out_specs=(P(("sec", "col"), None, None), P(("sec", "col"), None, None)),
        check_vma=False,
    )
```

```python
import functools

import jax
import jax.numpy as jnp
from jax import lax
from jax.experimental import pallas as pl
from jax.experimental.pallas import tpu as pltpu
from jax.sharding import PartitionSpec as P

MESH = pl.DeviceIdType.MESH
OWN, MIRROR, OTHER = 0, 1, 2


def low_size(n_col):
    low = 1
    while (2 * low) ** 2 <= n_col:
        low *= 2
    return low


def kernel(
    dims, targets_ref, slot_ref, rhs_hbm, diag_hbm, off_hbm, sol_ref, hand_ref,
    rin, diag_ref, off_ref, pack_own, pack_mirror, idx_vec, idx_ref,
    a_ref, x_ref, inc, send1, recv1, send2, recv2, acc, passed, ret,
    in_sem, fs_sem, fr_sem, s1_sem, r1_sem, s2_sem, r2_sem, sp_sem, rp_sem, sr_sem, rr_sem,
):
    n_sec, n_hi, n_lo = dims
    half = n_sec // 2
    blocks, width = off_hbm.shape[0], off_hbm.shape[2]
    noff = off_hbm.shape[1]
    rows = slot_ref.shape[1]
    lanes = idx_vec.shape[2]
    nc = rin.shape[3]
    size = blocks * width
    pairs = blocks // 2
    sec = lax.axis_index("sec")
    col = lax.axis_index("col")
    plane, place = sec // half, sec % half
    hi, lo = col // n_lo, col % n_lo
    mirror = {"sec": lax.rem(sec + half, n_sec), "col": col}

    def columns_of(which):
        return pl.ds(pl.multiple_of(which * nc, nc), nc)

    loads = [
        pltpu.make_async_copy(off_hbm, off_ref, in_sem.at[0]),
        pltpu.make_async_copy(diag_hbm, diag_ref.at[OWN], in_sem.at[1]),
        pltpu.make_async_copy(rhs_hbm.at[:, :, columns_of(plane)], rin.at[OWN], in_sem.at[2]),
        pltpu.make_async_copy(rhs_hbm.at[:, :, columns_of(1 - plane)], rin.at[OTHER], in_sem.at[3]),
    ]
    for load in loads:
        load.start()

    def lo_peer(o):
        return {"sec": sec, "col": hi * n_lo + lax.rem(lo + o, n_lo)}

    def hi_flip(o):
        value, bit = hi, 1
        while bit < n_hi:
            if o & bit:
                value = value + bit - 2 * bit * ((value // bit) % 2)
            bit *= 2
        return value

    def hi_peer(o):
        return {"sec": sec, "col": hi_flip(o) * n_lo + lo}

    barrier = pltpu.get_barrier_semaphore()
    for o in range(1, n_lo):
        pl.semaphore_signal(barrier, inc=1, device_id=lo_peer(o), device_id_type=MESH)
    for o in range(1, n_hi):
        pl.semaphore_signal(barrier, inc=1, device_id=hi_peer(o), device_id_type=MESH)
    for o in range(1, n_sec):
        pl.semaphore_signal(
            barrier, inc=1, device_id={"sec": lax.rem(sec + o, n_sec), "col": col},
            device_id_type=MESH,
        )

    slot_of_lane = lax.broadcasted_iota(jnp.int32, (1, lanes), 1)
    for k in range(blocks):
        found = jnp.full((1, lanes), noff, jnp.int32)
        for p in range(noff):
            dest = slot_ref[0, targets_ref[k, p]]
            found = jnp.where(slot_of_lane == dest, p, found)
        idx_vec[OWN, k:k + 1, :] = found
    to_scalar = pltpu.make_async_copy(idx_vec.at[OWN], idx_ref.at[OWN], in_sem.at[4])
    to_scalar.start()

    packs = (pack_own, pack_mirror)
    for pack_ref in packs:
        for q in range(pairs):
            pack_ref[q, noff] = jnp.zeros((width, 2 * width), jnp.bfloat16)
    for load in loads:
        load.wait()

    def pack(p, carry):
        for q in range(pairs):
            pack_own[q, p] = jnp.concatenate([off_ref[2 * q, p], off_ref[2 * q + 1, p]], axis=1)
        return carry

    lax.fori_loop(0, noff, pack, 0)
    to_scalar.wait()
    pl.semaphore_wait(barrier, n_lo - 1 + n_hi - 1 + n_sec - 1)

    def factor_copies():
        ends = [
            (idx_vec.at[OWN], idx_vec.at[MIRROR]),
            (diag_ref.at[OWN], diag_ref.at[MIRROR]),
            (rin.at[OTHER], rin.at[MIRROR]),
        ] + [
            (pack_own.at[q, pl.ds(0, noff)], pack_mirror.at[q, pl.ds(0, noff)])
            for q in range(pairs)
        ]
        return [
            pltpu.make_async_remote_copy(
                src_ref=src, dst_ref=dst, send_sem=fs_sem.at[n], recv_sem=fr_sem.at[n],
                device_id=mirror, device_id_type=MESH,
            )
            for n, (src, dst) in enumerate(ends)
        ]

    @pl.when(sec != 0)
    def _():
        for copy in factor_copies():
            copy.start()

    def mirror_factor():
        for copy in factor_copies():
            copy.wait_recv()
        to_scalar = pltpu.make_async_copy(idx_vec.at[MIRROR], idx_ref.at[MIRROR], in_sem.at[5])
        to_scalar.start()
        to_scalar.wait()

    def source(role):
        return lax.rem(role + plane, 2)

    left = lax.broadcasted_iota(jnp.int32, (width, 2 * width), 1) < width

    def build_row(role, src, i):
        pack_ref = packs[src]
        for q in range(pairs):
            a_ref[role, i, :, 2 * q * width:2 * (q + 1) * width] = jnp.where(
                left,
                pack_ref[q, idx_ref[src, 2 * q, i]],
                pack_ref[q, idx_ref[src, 2 * q + 1, i]],
            )

    def build_all(role):
        for src in (OWN, MIRROR):
            @pl.when(source(role) == src)
            def _():
                def step(i, carry):
                    build_row(role, src, i)
                    return carry

                lax.fori_loop(0, rows, step, 0)

    def copy1(j, o, oh):
        return pltpu.make_async_remote_copy(
            src_ref=send1.at[j, o - 1, oh], dst_ref=recv1.at[j, o - 1, oh],
            send_sem=s1_sem.at[j, o - 1, oh], recv_sem=r1_sem.at[j, o - 1, oh],
            device_id=lo_peer(o), device_id_type=MESH,
        )

    def copy2(j, oh):
        return pltpu.make_async_remote_copy(
            src_ref=send2.at[j, oh - 1], dst_ref=recv2.at[j, oh - 1],
            send_sem=s2_sem.at[j, oh - 1], recv_sem=r2_sem.at[j, oh - 1],
            device_id=hi_peer(oh), device_id_type=MESH,
        )

    def copyp(j, to_sec, slot):
        return pltpu.make_async_remote_copy(
            src_ref=passed.at[j], dst_ref=inc.at[slot],
            send_sem=sp_sem.at[j], recv_sem=rp_sem.at[slot],
            device_id={"sec": to_sec, "col": col}, device_id_type=MESH,
        )

    def pass_on(j):
        if j == 0:
            return copyp(0, half + 1, 0)
        more = place + 1 < half
        to_sec = plane * half + jnp.where(more, place + 1, 0)
        if j == 1:
            return copyp(1, to_sec, jnp.where(more, 0, 1))
        return copyp(2, to_sec, 1)

    def give_back(which, j):
        return pltpu.make_async_remote_copy(
            src_ref=(x_ref, passed)[which].at[j], dst_ref=ret.at[which],
            send_sem=sr_sem.at[which], recv_sem=rr_sem.at[which],
            device_id=mirror, device_id_type=MESH,
        )

    order = list(range(n_hi - 1, -1, -1))

    def product(j, oh, o):
        role = max(j - 1, 0)
        dest = hi_flip(oh) * n_lo + lax.rem(lo + o, n_lo)
        if j == 0:
            for r in range(blocks):
                build_row(0, OWN, dest * blocks + r)
        a = a_ref[role, pl.ds(dest * blocks, blocks)].reshape(size, size)
        return jnp.dot(a, x_ref[j], preferred_element_type=jnp.float32)

    def first(j, fresh):
        role = max(j - 1, 0)
        src = source(role)
        which = OTHER if j == 0 else src
        if not fresh:
            copyp(j, sec, role).wait_recv()
        for k in range(blocks):
            part = slice(k * width, (k + 1) * width)
            residual = rin[which, k]
            if not fresh:
                residual = (
                    residual.astype(jnp.float32) - inc[role, part, :].astype(jnp.float32)
                ).astype(jnp.bfloat16)
            x_ref[j, part, :] = jnp.dot(
                diag_ref[src, k], residual, preferred_element_type=jnp.float32
            ).astype(jnp.bfloat16)
        for oh in order:
            for o in range(1, n_lo):
                send1[j, o - 1, oh] = product(j, oh, o).astype(jnp.bfloat16)
                copy1(j, o, oh).start()

    def middle(j):
        for oh in order:
            total = product(j, oh, 0)
            for o in range(1, n_lo):
                copy1(j, o, oh).wait_recv()
                total = total + recv1[j, o - 1, oh].astype(jnp.float32)
            if oh == 0:
                acc[j] = total
            else:
                send2[j, oh - 1] = total.astype(jnp.bfloat16)
                copy2(j, oh).start()

    def last(j):
        total = acc[j]
        for oh in range(1, n_hi):
            copy2(j, oh).wait_recv()
            total = total + recv2[j, oh - 1].astype(jnp.float32)
        passed[j] = total.astype(jnp.bfloat16)
        if j < 2:
            pass_on(j).start()
        else:
            @pl.when(place < half - 1)
            def _():
                pass_on(j).start()

        if j > 0:
            @pl.when(source(j - 1) == MIRROR)
            def _():
                give_back(0, j).start()
                give_back(1, j).start()

    def sent(j):
        for oh in range(n_hi):
            for o in range(1, n_lo):
                copy1(j, o, oh).wait_send()
        for oh in range(1, n_hi):
            copy2(j, oh).wait_send()

    @pl.when(sec == 0)
    def _():
        first(0, True)
        middle(0)
        first(1, True)
        last(0)
        middle(1)
        last(1)
        sent(0)
        sent(1)
        pass_on(0).wait_send()
        pass_on(1).wait_send()

    @pl.when(place > 0)
    def _():
        @pl.when(plane == 1)
        def _():
            mirror_factor()

        build_all(0)
        first(1, False)
        middle(1)
        last(1)
        sent(1)
        pass_on(1).wait_send()

    @pl.when(plane == 0)
    def _():
        mirror_factor()

    build_all(1)
    first(2, False)
    middle(2)
    last(2)
    own = 1 + plane
    sol_ref[:, :, columns_of(plane)] = x_ref[own].reshape(blocks, width, nc)
    hand_ref[:, :, columns_of(plane)] = passed[own].reshape(blocks, width, nc)

    @pl.when(sec == 0)
    def _():
        sol_ref[:, :, nc:2 * nc] = x_ref[0].reshape(blocks, width, nc)
        hand_ref[:, :, nc:2 * nc] = passed[0].reshape(blocks, width, nc)

    @pl.when(sec != 0)
    def _():
        give_back(0, 1).wait_recv()
        sol_ref[:, :, columns_of(1 - plane)] = ret[0].reshape(blocks, width, nc)
        give_back(1, 1).wait_recv()
        hand_ref[:, :, columns_of(1 - plane)] = ret[1].reshape(blocks, width, nc)
        for copy in factor_copies():
            copy.wait_send()

    sent(2)

    @pl.when(place < half - 1)
    def _():
        pass_on(2).wait_send()

    @pl.when(sec != half)
    def _():
        give_back(0, 1).wait_send()
        give_back(1, 1).wait_send()


def mirrored(n_sec, n_col, rhs, diag_inv, off_tiles, targets, row_slot):
    blocks, width, columns = rhs.shape
    noff = off_tiles.shape[1]
    rows = row_slot.shape[1]
    n_lo = low_size(n_col)
    n_hi = n_col // n_lo
    nc = columns // 2
    size = blocks * width
    pairs = blocks // 2
    lanes = -(-rows // 128) * 128

    vmem = pl.BlockSpec(memory_space=pltpu.VMEM)
    smem = pl.BlockSpec(memory_space=pltpu.SMEM)
    hbm = pl.BlockSpec(memory_space=pl.ANY)
    out = jax.ShapeDtypeStruct((blocks, width, columns), jnp.bfloat16)
    dma = pltpu.SemaphoreType.DMA
    bf16 = jnp.bfloat16
    return pl.pallas_call(
        functools.partial(kernel, (n_sec, n_hi, n_lo)),
        out_shape=(out, out),
        in_specs=[smem, smem, hbm, hbm, hbm],
        out_specs=(vmem, vmem),
        scratch_shapes=[
            pltpu.VMEM((3, blocks, width, nc), bf16),
            pltpu.VMEM((2, blocks, width, width), bf16),
            pltpu.VMEM((blocks, noff, width, width), bf16),
            pltpu.VMEM((pairs, noff + 1, width, 2 * width), bf16),
            pltpu.VMEM((pairs, noff + 1, width, 2 * width), bf16),
            pltpu.VMEM((2, blocks, lanes), jnp.int32),
            pltpu.SMEM((2, blocks, lanes), jnp.int32),
            pltpu.VMEM((2, rows, width, size), bf16),
            pltpu.VMEM((3, size, nc), bf16),
            pltpu.VMEM((2, size, nc), bf16),
            pltpu.VMEM((3, n_lo - 1, n_hi, size, nc), bf16),
            pltpu.VMEM((3, n_lo - 1, n_hi, size, nc), bf16),
            pltpu.VMEM((3, n_hi - 1, size, nc), bf16),
            pltpu.VMEM((3, n_hi - 1, size, nc), bf16),
            pltpu.VMEM((3, size, nc), jnp.float32),
            pltpu.VMEM((3, size, nc), bf16),
            pltpu.VMEM((2, size, nc), bf16),
            dma((6,)),
            dma((3 + pairs,)),
            dma((3 + pairs,)),
            dma((3, n_lo - 1, n_hi)),
            dma((3, n_lo - 1, n_hi)),
            dma((3, n_hi - 1)),
            dma((3, n_hi - 1)),
            dma((3,)),
            dma((2,)),
            dma((2,)),
            dma((2,)),
        ],
        compiler_params=pltpu.CompilerParams(
            collective_id=0, has_side_effects=True, vmem_limit_bytes=60 * 1024 * 1024
        ),
    )(targets, row_slot, rhs, diag_inv, off_tiles)


def chains_kernel(
    dims, targets_ref, slot_ref, rhs_hbm, diag_hbm, off_hbm, sol_ref, hand_ref,
    rhs_ref, off_ref, pack_0, pack_1, pack_2, pack_3, diag_ref, idx_vec, idx_ref, rin, a_ref, w_ref,
    send1, recv1, send2, recv2, acc, xs, hs, ret,
    in_sem, fs_sem, fr_sem, rs_sem, rr_sem, s1_sem, r1_sem, s2_sem, r2_sem, p_sem, gs_sem, gr_sem,
):
    n_hi, n_lo = dims
    blocks, noff, width = off_hbm.shape[:3]
    lanes = idx_vec.shape[2]
    pairs = blocks // 2
    size = blocks * width
    packed = pairs * width
    wide = 2 * width
    sec = lax.axis_index("sec")
    col = lax.axis_index("col")
    plane, place = sec // 2, sec % 2
    hi, lo = col // n_lo, col % n_lo
    bf16, f32 = jnp.bfloat16, jnp.float32

    own_idx = pltpu.make_async_copy(idx_vec.at[sec], idx_ref.at[sec], in_sem.at[0])
    load_off = pltpu.make_async_copy(off_hbm, off_ref, in_sem.at[1])
    load_diag = pltpu.make_async_copy(diag_hbm, diag_ref.at[sec], in_sem.at[2])
    load_rhs = pltpu.make_async_copy(rhs_hbm, rhs_ref, in_sem.at[3])
    for load in (load_off, load_diag, load_rhs):
        load.start()

    def hi_flip(o):
        value, bit = hi, 1
        while bit < n_hi:
            value = value + ((o // bit) % 2) * (bit - 2 * bit * ((value // bit) % 2))
            bit *= 2
        return value

    def at_sec(to):
        return {"sec": to, "col": col}

    lo_peer = {"sec": sec, "col": hi * n_lo + 1 - lo}

    def hi_peer(o):
        return {"sec": sec, "col": hi_flip(o) * n_lo + lo}

    barrier = pltpu.get_barrier_semaphore()
    peers = [lo_peer] + [hi_peer(o) for o in range(1, n_hi)]
    peers += [at_sec(lax.rem(sec + o, 4)) for o in range(1, 4)]
    for peer in peers:
        pl.semaphore_signal(barrier, inc=1, device_id=peer, device_id_type=MESH)

    slot_of_lane = lax.broadcasted_iota(jnp.int32, (1, lanes), 1)
    for k in range(blocks):
        found = jnp.full((1, lanes), noff, jnp.int32)
        for p in range(noff):
            dest = slot_ref[0, targets_ref[k, p]]
            found = jnp.where(slot_of_lane == dest, p, found)
        idx_vec[sec, k:k + 1, :] = found
    own_idx.start()
    packs = (pack_0, pack_1, pack_2, pack_3)
    for pack_ref in packs:
        for q in range(pairs):
            pack_ref[q, noff] = jnp.zeros((width, wide), bf16)

    left = lax.broadcasted_iota(jnp.int32, (width, wide), 1) < width

    def swap(x):
        return jnp.concatenate([x[:, width:], x[:, :width]], axis=1)

    load_off.wait()

    def pack_into(pack_ref):
        def step(p, carry):
            for q in range(pairs):
                pack_ref[q, p] = jnp.concatenate([off_ref[2 * q, p], off_ref[2 * q + 1, p]], axis=1)
            return carry

        lax.fori_loop(0, noff, step, 0)

    for s in range(4):
        @pl.when(sec == s)
        def _():
            pack_into(packs[s])

    load_diag.wait()
    load_rhs.wait()
    own_idx.wait()
    pl.semaphore_wait(barrier, len(peers))

    every = range(2 + pairs)
    halves = (range(2 + pairs // 2), range(2 + pairs // 2, 2 + pairs))

    def factor(s, to, step, pieces=every):
        ends = [idx_vec.at[s], diag_ref.at[s]]
        ends += [packs[s].at[q, pl.ds(0, noff)] for q in range(pairs)]
        return [
            pltpu.make_async_remote_copy(
                src_ref=ends[n], dst_ref=ends[n], send_sem=fs_sem.at[step, n], recv_sem=fr_sem.at[s, n],
                device_id=at_sec(to), device_id_type=MESH,
            )
            for n in pieces
        ]

    def start(copies):
        for copy in copies:
            copy.start()

    def wait_sent(copies):
        for copy in copies:
            copy.wait_send()

    def to_scalar_memory(s):
        to_scalar = pltpu.make_async_copy(idx_vec.at[s], idx_ref.at[s], in_sem.at[0])
        to_scalar.start()
        to_scalar.wait()

    def factor_here(s):
        for copy in factor(s, 0, 0):
            copy.wait_recv()
        to_scalar_memory(s)

    def by_core(act):
        for core in range(2):
            @pl.when(place == core)
            def _():
                act(core)

    def across(s, act):
        by_core(lambda core: act(factor(s, 2 - s // 2 * 2 + core, s, halves[core])))

    def arrive(s):
        def step(core):
            for copy in factor(s, 0, 0, halves[core]):
                copy.wait_recv()
            start(factor(s, s // 2 * -2 + 3 - core, s, halves[core]))

        by_core(step)

    def relayed(s):
        by_core(lambda core: wait_sent(factor(s, 0, s, halves[core])))

    def arrive_late(s):
        def step(core):
            for copy in factor(s, 0, 0, halves[1 - core]):
                copy.wait_recv()

        by_core(step)
        to_scalar_memory(s)

    def chain_of(device):
        return 2 * (1 - device // 2) + device % 2

    mine = chain_of(sec)

    def rhs_copy(s, chain, to, step, slot):
        return pltpu.make_async_remote_copy(
            src_ref=rin.at[s, chain], dst_ref=rin.at[s, chain],
            send_sem=rs_sem.at[step], recv_sem=rr_sem.at[slot],
            device_id=at_sec(to), device_id_type=MESH,
        )

    def rhs_sends(s):
        if s == 0:
            return [rhs_copy(0, 1, 1, 0, 4), rhs_copy(0, 3, 1, 1, 0)]
        return [
            rhs_copy(s, 2 * (1 - to // 2) + to % 2, to, n, s)
            for n, to in enumerate(to for to in (s ^ 1, s ^ 2, s ^ 3))
        ]

    def rhs_here(s):
        rhs_copy(s, mine, 0, 0, s).wait_recv()

    other = plane * 2 + 1 - place
    for s in range(4):
        @pl.when(sec == s)
        def _():
            start(factor(s, s ^ 1, 0))

    for m in range(2):
        part = slice(m * wide, (m + 1) * wide)
        for q in range(pairs):
            even, odd = rhs_ref[2 * q, :, part], rhs_ref[2 * q + 1, :, part]
            rows = slice(q * width, (q + 1) * width)
            rin[sec, 2 * m, rows] = jnp.where(left, even, swap(odd))
            rin[sec, 2 * m + 1, rows] = jnp.where(left, swap(even), odd)

    for s in range(4):
        @pl.when(sec == s)
        def _():
            start(rhs_sends(s))

    def build(s, d):
        for r in range(blocks):
            i = d * blocks + r
            for q in range(pairs):
                at = (r % 2) * size + q * wide
                a_ref[s, d * pairs + r // 2, :, at:at + wide] = jnp.where(
                    left, packs[s][q, idx_ref[s, 2 * q, i]], packs[s][q, idx_ref[s, 2 * q + 1, i]]
                )

    def build_range(s, low, high):
        def step(d, carry):
            build(s, d)
            return carry

        lax.fori_loop(low, high, step, 0)

    def copy1(j, oh):
        return pltpu.make_async_remote_copy(
            src_ref=send1.at[j, oh], dst_ref=recv1.at[j, oh],
            send_sem=s1_sem.at[j, oh], recv_sem=r1_sem.at[j, oh],
            device_id=lo_peer, device_id_type=MESH,
        )

    def copy2(j, oh):
        return pltpu.make_async_remote_copy(
            src_ref=send2.at[j, oh - 1], dst_ref=recv2.at[j, oh - 1],
            send_sem=s2_sem.at[j, oh - 1], recv_sem=r2_sem.at[j, oh - 1],
            device_id=hi_peer(oh), device_id_type=MESH,
        )

    def give(which, j, s, chain):
        return pltpu.make_async_remote_copy(
            src_ref=(xs, hs)[which].at[j], dst_ref=ret.at[which, chain],
            send_sem=gs_sem.at[which, j], recv_sem=gr_sem.at[which, chain],
            device_id=at_sec(s), device_id_type=MESH,
        )

    def give_out(which, j, s, chain):
        @pl.when(sec == s)
        def _():
            ret[which, chain] = (xs, hs)[which][j]

        @pl.when(sec != s)
        def _():
            give(which, j, s, chain).start()

    def product(s, w, dest):
        a = a_ref[s, pl.ds(dest * pairs, pairs)].reshape(packed, 2 * size)
        return jnp.dot(a, w_ref[w], preferred_element_type=f32)

    def first(s, j, w, chain, h, fresh=False):
        for q in range(pairs):
            rows = slice(q * width, (q + 1) * width)
            residual = rin[s, chain, rows]
            if h is not None:
                residual = (residual.astype(f32) - h[rows].astype(f32)).astype(bf16)
            z = jnp.dot(
                diag_ref[s, 2 * q:2 * q + 2].reshape(wide, width), residual,
                preferred_element_type=f32,
            ).astype(bf16)
            top, low = z[:width], z[width:]
            xs[j, rows] = jnp.where(left, top, low)
            zero = jnp.zeros_like(top)
            at = q * wide
            w_ref[w, at:at + width] = jnp.where(left, top, zero)
            w_ref[w, at + width:at + wide] = jnp.where(left, swap(low), zero)
            w_ref[w, size + at:size + at + width] = jnp.where(left, zero, swap(top))
            w_ref[w, size + at + width:size + at + wide] = jnp.where(left, zero, low)

        def step(t, carry):
            oh = n_hi - 1 - t
            dest = hi_flip(oh) * n_lo + 1 - lo
            if fresh:
                build(s, dest)
            send1[j, oh] = product(s, w, dest).astype(bf16)
            copy1(j, oh).start()
            return carry

        lax.fori_loop(0, n_hi, step, 0)
        give_out(0, j, s, chain)

    def middle(s, j, w, fresh=False, also=None):

        def step(t, carry):
            oh = n_hi - 1 - t
            dest = hi_flip(oh) * n_lo + lo
            if fresh:
                build(s, dest)
            total = product(s, w, dest)
            copy1(j, oh).wait_recv()
            total = total + recv1[j, oh].astype(f32)

            @pl.when(oh > 0)
            def _():
                send2[j, oh - 1] = total.astype(bf16)
                copy2(j, oh).start()

            @pl.when(oh == 0)
            def _():
                acc[w] = total

            if also is not None:
                @pl.when(plane == 0)
                def _():
                    build(also, 2 * t)
                    build(also, 2 * t + 1)
            return carry

        lax.fori_loop(0, n_hi, step, 0)

    def last(j, w):
        total = acc[w]
        for oh in range(n_hi - 1, 0, -1):
            copy2(j, oh).wait_recv()
            total = total + recv2[j, oh - 1].astype(f32)
        hs[j] = total.astype(bf16)

    def sent(j, s):
        for oh in range(n_hi):
            copy1(j, oh).wait_send()
        for oh in range(1, n_hi):
            copy2(j, oh).wait_send()

        @pl.when(sec != s)
        def _():
            give(0, j, s, mine).wait_send()
            give(1, j, s, mine).wait_send()

    def pass_on():
        return pltpu.make_async_remote_copy(
            src_ref=hs.at[4], dst_ref=hs.at[0], send_sem=p_sem.at[0], recv_sem=p_sem.at[1],
            device_id=at_sec(2 + place), device_id_type=MESH,
        )

    def here(s):
        factor_here(s)
        if s > 0:
            rhs_here(s)

    @pl.when(plane == 0)
    def _():
        @pl.when(place == 1)
        def _():
            across(1, start)
            here(0)
            rhs_copy(0, 1, 0, 0, 4).wait_recv()
            rhs_copy(0, 3, 0, 0, 0).wait_recv()

        first(0, 4, 0, place, None, fresh=True)

        @pl.when(place == 0)
        def _():
            here(1)
            across(1, start)

        first(0, 0, 1, mine, None)
        middle(0, 4, 0, fresh=True)
        middle(0, 0, 1)
        last(4, 0)
        pass_on().start()
        give_out(1, 4, 0, place)
        last(0, 1)
        arrive(2)

    @pl.when(plane == 1)
    def _():
        for s in (2, 3):
            @pl.when(sec != s)
            def _():
                here(s)

        across(2, start)
        build_range(2, 0, n_hi * n_lo)
        build_range(3, 0, n_hi * n_lo)
        arrive(1)
        arrive_late(1)
        rhs_here(1)
        across(2, wait_sent)
        across(3, start)
        pass_on().wait_recv()

    first(1, 1, 1, mine, hs.at[0], fresh=True)

    @pl.when(plane == 0)
    def _():
        give_out(1, 0, 0, mine)
        arrive_late(2)
        rhs_here(2)

    middle(1, 1, 1, fresh=True, also=2)
    last(1, 1)
    first(2, 2, 1, mine, hs.at[1])
    give_out(1, 1, 1, mine)

    @pl.when(plane == 0)
    def _():
        arrive(3)
        arrive_late(3)
        rhs_here(3)

    middle(2, 2, 1, also=3)
    last(2, 1)
    first(3, 3, 1, mine, hs.at[2])
    give_out(1, 2, 2, mine)
    middle(3, 3, 1)
    last(3, 1)
    give_out(1, 3, 3, mine)

    def returned(which, chain):
        return pltpu.make_async_remote_copy(
            src_ref=xs.at[0], dst_ref=ret.at[which, chain],
            send_sem=gs_sem.at[which, 0], recv_sem=gr_sem.at[which, chain],
            device_id=at_sec(other), device_id_type=MESH,
        )

    for which, out in ((0, sol_ref), (1, hand_ref)):
        for m in range(2):
            returned(which, 2 * m + 1 - place).wait_recv()

            @pl.when((sec != 0) & (plane == m))
            def _():
                returned(which, 2 * m + place).wait_recv()

            part = slice(m * wide, (m + 1) * wide)
            for q in range(pairs):
                rows = slice(q * width, (q + 1) * width)
                one, two = ret[which, 2 * m, rows], ret[which, 2 * m + 1, rows]
                out[2 * q, :, part] = jnp.where(left, one, swap(two))
                out[2 * q + 1, :, part] = jnp.where(left, swap(one), two)

    for s in range(1, 4):
        sent(s, s)
    wait_sent(factor(0, other, 0))
    for s in range(4):
        @pl.when(sec == s)
        def _():
            wait_sent(rhs_sends(s))

    @pl.when(plane == 0)
    def _():
        sent(0, 0)
        for oh in range(n_hi):
            copy1(4, oh).wait_send()
        for oh in range(1, n_hi):
            copy2(4, oh).wait_send()

        @pl.when(sec != 0)
        def _():
            give(0, 4, 0, place).wait_send()
            give(1, 4, 0, place).wait_send()

        pass_on().wait_send()
        across(1, wait_sent)
        relayed(2)
        relayed(3)

    @pl.when(plane == 1)
    def _():
        across(3, wait_sent)
        relayed(1)


def chains(n_col, rhs, diag_inv, off_tiles, targets, row_slot):
    blocks, width, columns = rhs.shape
    noff = off_tiles.shape[1]
    rows = row_slot.shape[1]
    n_lo = 2
    n_hi = n_col // n_lo
    size = blocks * width
    pairs = blocks // 2
    packed = pairs * width
    wide = 2 * width
    lanes = -(-rows // 128) * 128
    vmem = pl.BlockSpec(memory_space=pltpu.VMEM)
    smem = pl.BlockSpec(memory_space=pltpu.SMEM)
    hbm = pl.BlockSpec(memory_space=pl.ANY)
    out = jax.ShapeDtypeStruct((blocks, width, columns), jnp.bfloat16)
    dma = pltpu.SemaphoreType.DMA
    bf16 = jnp.bfloat16
    return pl.pallas_call(
        functools.partial(chains_kernel, (n_hi, n_lo)),
        out_shape=(out, out),
        in_specs=[smem, smem, hbm, hbm, hbm],
        out_specs=(vmem, vmem),
        scratch_shapes=[
            pltpu.VMEM((blocks, width, columns), bf16),
            pltpu.VMEM((blocks, noff, width, width), bf16),
            pltpu.VMEM((pairs, noff + 1, width, wide), bf16),
            pltpu.VMEM((pairs, noff + 1, width, wide), bf16),
            pltpu.VMEM((pairs, noff + 1, width, wide), bf16),
            pltpu.VMEM((pairs, noff + 1, width, wide), bf16),
            pltpu.VMEM((4, blocks, width, width), bf16),
            pltpu.VMEM((4, blocks, lanes), jnp.int32),
            pltpu.SMEM((4, blocks, lanes), jnp.int32),
            pltpu.VMEM((4, 4, packed, wide), bf16),
            pltpu.VMEM((4, rows // 2, width, 2 * size), bf16),
            pltpu.VMEM((2, 2 * size, wide), bf16),
            pltpu.VMEM((5, n_hi, packed, wide), bf16),
            pltpu.VMEM((5, n_hi, packed, wide), bf16),
            pltpu.VMEM((5, n_hi - 1, packed, wide), bf16),
            pltpu.VMEM((5, n_hi - 1, packed, wide), bf16),
            pltpu.VMEM((2, packed, wide), jnp.float32),
            pltpu.VMEM((5, packed, wide), bf16),
            pltpu.VMEM((5, packed, wide), bf16),
            pltpu.VMEM((2, 4, packed, wide), bf16),
            dma((4,)),
            dma((4, 2 + pairs)),
            dma((4, 2 + pairs)),
            dma((3,)),
            dma((5,)),
            dma((5, n_hi)),
            dma((5, n_hi)),
            dma((5, n_hi - 1)),
            dma((5, n_hi - 1)),
            dma((2,)),
            dma((2, 5)),
            dma((2, 4)),
        ],
        compiler_params=pltpu.CompilerParams(
            collective_id=1, has_side_effects=True, vmem_limit_bytes=60 * 1024 * 1024
        ),
    )(targets, row_slot, rhs, diag_inv, off_tiles)


def fits_chains(n_sec, n_col, rhs, row_slot):
    blocks, width, columns = rhs.shape
    n_hi = n_col // 2
    return (
        n_sec == 4 and n_col % 2 == 0 and n_hi & (n_hi - 1) == 0 and columns == 4 * width and width == 64
        and blocks % 2 == 0 and row_slot.shape[1] == blocks * n_col
    )


def shards(n_sec, n_col, rhs, diag_inv, off_tiles, targets, row_slot):
    if fits_chains(n_sec, n_col, rhs, row_slot):
        return chains(n_col, rhs, diag_inv, off_tiles, targets, row_slot)
    return mirrored(n_sec, n_col, rhs, diag_inv, off_tiles, targets, row_slot)


def solution(mesh):
    return jax.shard_map(
        functools.partial(shards, mesh.shape["sec"], mesh.shape["col"]),
        mesh=mesh,
        in_specs=(
            P(("sec", "col"), None, None),
            P(("sec", "col"), None, None),
            P(("sec", "col"), None, None, None),
            P(("sec", "col"), None),
            P("sec", None),
        ),
        out_specs=(P(("sec", "col"), None, None), P(("sec", "col"), None, None)),
        check_vma=False,
    )
```

```python
import functools

import jax
import jax.numpy as jnp
from jax import lax
from jax.experimental import pallas as pl
from jax.experimental.pallas import tpu as pltpu
from jax.sharding import PartitionSpec as P

MESH = pl.DeviceIdType.MESH
OWN, MIRROR, OTHER = 0, 1, 2


def low_size(n_col):
    low = 1
    while (2 * low) ** 2 <= n_col:
        low *= 2
    return low


def kernel(
    dims, targets_ref, slot_ref, rhs_hbm, diag_hbm, off_hbm, sol_ref, hand_ref,
    rin, diag_ref, off_ref, pack_own, pack_mirror, idx_vec, idx_ref,
    a_ref, x_ref, inc, send1, recv1, send2, recv2, acc, passed, ret,
    in_sem, fs_sem, fr_sem, s1_sem, r1_sem, s2_sem, r2_sem, sp_sem, rp_sem, sr_sem, rr_sem,
):
    n_sec, n_hi, n_lo = dims
    half = n_sec // 2
    blocks, width = off_hbm.shape[0], off_hbm.shape[2]
    noff = off_hbm.shape[1]
    rows = slot_ref.shape[1]
    lanes = idx_vec.shape[2]
    nc = rin.shape[3]
    size = blocks * width
    pairs = blocks // 2
    sec = lax.axis_index("sec")
    col = lax.axis_index("col")
    plane, place = sec // half, sec % half
    hi, lo = col // n_lo, col % n_lo
    mirror = {"sec": lax.rem(sec + half, n_sec), "col": col}

    def columns_of(which):
        return pl.ds(pl.multiple_of(which * nc, nc), nc)

    loads = [
        pltpu.make_async_copy(off_hbm, off_ref, in_sem.at[0]),
        pltpu.make_async_copy(diag_hbm, diag_ref.at[OWN], in_sem.at[1]),
        pltpu.make_async_copy(rhs_hbm.at[:, :, columns_of(plane)], rin.at[OWN], in_sem.at[2]),
        pltpu.make_async_copy(rhs_hbm.at[:, :, columns_of(1 - plane)], rin.at[OTHER], in_sem.at[3]),
    ]
    for load in loads:
        load.start()

    def lo_peer(o):
        return {"sec": sec, "col": hi * n_lo + lax.rem(lo + o, n_lo)}

    def hi_flip(o):
        value, bit = hi, 1
        while bit < n_hi:
            if o & bit:
                value = value + bit - 2 * bit * ((value // bit) % 2)
            bit *= 2
        return value

    def hi_peer(o):
        return {"sec": sec, "col": hi_flip(o) * n_lo + lo}

    barrier = pltpu.get_barrier_semaphore()
    for o in range(1, n_lo):
        pl.semaphore_signal(barrier, inc=1, device_id=lo_peer(o), device_id_type=MESH)
    for o in range(1, n_hi):
        pl.semaphore_signal(barrier, inc=1, device_id=hi_peer(o), device_id_type=MESH)
    for o in range(1, n_sec):
        pl.semaphore_signal(
            barrier, inc=1, device_id={"sec": lax.rem(sec + o, n_sec), "col": col},
            device_id_type=MESH,
        )

    slot_of_lane = lax.broadcasted_iota(jnp.int32, (1, lanes), 1)
    for k in range(blocks):
        found = jnp.full((1, lanes), noff, jnp.int32)
        for p in range(noff):
            dest = slot_ref[0, targets_ref[k, p]]
            found = jnp.where(slot_of_lane == dest, p, found)
        idx_vec[OWN, k:k + 1, :] = found
    to_scalar = pltpu.make_async_copy(idx_vec.at[OWN], idx_ref.at[OWN], in_sem.at[4])
    to_scalar.start()

    packs = (pack_own, pack_mirror)
    for pack_ref in packs:
        for q in range(pairs):
            pack_ref[q, noff] = jnp.zeros((width, 2 * width), jnp.bfloat16)
    for load in loads:
        load.wait()

    def pack(p, carry):
        for q in range(pairs):
            pack_own[q, p] = jnp.concatenate([off_ref[2 * q, p], off_ref[2 * q + 1, p]], axis=1)
        return carry

    lax.fori_loop(0, noff, pack, 0)
    to_scalar.wait()
    pl.semaphore_wait(barrier, n_lo - 1 + n_hi - 1 + n_sec - 1)

    def factor_copies():
        ends = [
            (idx_vec.at[OWN], idx_vec.at[MIRROR]),
            (diag_ref.at[OWN], diag_ref.at[MIRROR]),
            (rin.at[OTHER], rin.at[MIRROR]),
        ] + [
            (pack_own.at[q, pl.ds(0, noff)], pack_mirror.at[q, pl.ds(0, noff)])
            for q in range(pairs)
        ]
        return [
            pltpu.make_async_remote_copy(
                src_ref=src, dst_ref=dst, send_sem=fs_sem.at[n], recv_sem=fr_sem.at[n],
                device_id=mirror, device_id_type=MESH,
            )
            for n, (src, dst) in enumerate(ends)
        ]

    @pl.when(sec != 0)
    def _():
        for copy in factor_copies():
            copy.start()

    def mirror_factor():
        for copy in factor_copies():
            copy.wait_recv()
        to_scalar = pltpu.make_async_copy(idx_vec.at[MIRROR], idx_ref.at[MIRROR], in_sem.at[5])
        to_scalar.start()
        to_scalar.wait()

    def source(role):
        return lax.rem(role + plane, 2)

    left = lax.broadcasted_iota(jnp.int32, (width, 2 * width), 1) < width

    def build_row(role, src, i):
        pack_ref = packs[src]
        for q in range(pairs):
            a_ref[role, i, :, 2 * q * width:2 * (q + 1) * width] = jnp.where(
                left,
                pack_ref[q, idx_ref[src, 2 * q, i]],
                pack_ref[q, idx_ref[src, 2 * q + 1, i]],
            )

    def build_all(role):
        for src in (OWN, MIRROR):
            @pl.when(source(role) == src)
            def _():
                def step(i, carry):
                    build_row(role, src, i)
                    return carry

                lax.fori_loop(0, rows, step, 0)

    def copy1(j, o, oh):
        return pltpu.make_async_remote_copy(
            src_ref=send1.at[j, o - 1, oh], dst_ref=recv1.at[j, o - 1, oh],
            send_sem=s1_sem.at[j, o - 1, oh], recv_sem=r1_sem.at[j, o - 1, oh],
            device_id=lo_peer(o), device_id_type=MESH,
        )

    def copy2(j, oh):
        return pltpu.make_async_remote_copy(
            src_ref=send2.at[j, oh - 1], dst_ref=recv2.at[j, oh - 1],
            send_sem=s2_sem.at[j, oh - 1], recv_sem=r2_sem.at[j, oh - 1],
            device_id=hi_peer(oh), device_id_type=MESH,
        )

    def copyp(j, to_sec, slot):
        return pltpu.make_async_remote_copy(
            src_ref=passed.at[j], dst_ref=inc.at[slot],
            send_sem=sp_sem.at[j], recv_sem=rp_sem.at[slot],
            device_id={"sec": to_sec, "col": col}, device_id_type=MESH,
        )

    def pass_on(j):
        if j == 0:
            return copyp(0, half + 1, 0)
        more = place + 1 < half
        to_sec = plane * half + jnp.where(more, place + 1, 0)
        if j == 1:
            return copyp(1, to_sec, jnp.where(more, 0, 1))
        return copyp(2, to_sec, 1)

    def give_back(which, j):
        return pltpu.make_async_remote_copy(
            src_ref=(x_ref, passed)[which].at[j], dst_ref=ret.at[which],
            send_sem=sr_sem.at[which], recv_sem=rr_sem.at[which],
            device_id=mirror, device_id_type=MESH,
        )

    order = list(range(n_hi - 1, -1, -1))

    def product(j, oh, o):
        role = max(j - 1, 0)
        dest = hi_flip(oh) * n_lo + lax.rem(lo + o, n_lo)
        if j == 0:
            for r in range(blocks):
                build_row(0, OWN, dest * blocks + r)
        a = a_ref[role, pl.ds(dest * blocks, blocks)].reshape(size, size)
        return jnp.dot(a, x_ref[j], preferred_element_type=jnp.float32)

    def first(j, fresh):
        role = max(j - 1, 0)
        src = source(role)
        which = OTHER if j == 0 else src
        if not fresh:
            copyp(j, sec, role).wait_recv()
        for k in range(blocks):
            part = slice(k * width, (k + 1) * width)
            residual = rin[which, k]
            if not fresh:
                residual = (
                    residual.astype(jnp.float32) - inc[role, part, :].astype(jnp.float32)
                ).astype(jnp.bfloat16)
            x_ref[j, part, :] = jnp.dot(
                diag_ref[src, k], residual, preferred_element_type=jnp.float32
            ).astype(jnp.bfloat16)
        for oh in order:
            for o in range(1, n_lo):
                send1[j, o - 1, oh] = product(j, oh, o).astype(jnp.bfloat16)
                copy1(j, o, oh).start()

    def middle(j):
        for oh in order:
            total = product(j, oh, 0)
            for o in range(1, n_lo):
                copy1(j, o, oh).wait_recv()
                total = total + recv1[j, o - 1, oh].astype(jnp.float32)
            if oh == 0:
                acc[j] = total
            else:
                send2[j, oh - 1] = total.astype(jnp.bfloat16)
                copy2(j, oh).start()

    def last(j):
        total = acc[j]
        for oh in range(1, n_hi):
            copy2(j, oh).wait_recv()
            total = total + recv2[j, oh - 1].astype(jnp.float32)
        passed[j] = total.astype(jnp.bfloat16)
        if j < 2:
            pass_on(j).start()
        else:
            @pl.when(place < half - 1)
            def _():
                pass_on(j).start()

        if j > 0:
            @pl.when(source(j - 1) == MIRROR)
            def _():
                give_back(0, j).start()
                give_back(1, j).start()

    def sent(j):
        for oh in range(n_hi):
            for o in range(1, n_lo):
                copy1(j, o, oh).wait_send()
        for oh in range(1, n_hi):
            copy2(j, oh).wait_send()

    @pl.when(sec == 0)
    def _():
        first(0, True)
        middle(0)
        first(1, True)
        last(0)
        middle(1)
        last(1)
        sent(0)
        sent(1)
        pass_on(0).wait_send()
        pass_on(1).wait_send()

    @pl.when(place > 0)
    def _():
        @pl.when(plane == 1)
        def _():
            mirror_factor()

        build_all(0)
        first(1, False)
        middle(1)
        last(1)
        sent(1)
        pass_on(1).wait_send()

    @pl.when(plane == 0)
    def _():
        mirror_factor()

    build_all(1)
    first(2, False)
    middle(2)
    last(2)
    own = 1 + plane
    sol_ref[:, :, columns_of(plane)] = x_ref[own].reshape(blocks, width, nc)
    hand_ref[:, :, columns_of(plane)] = passed[own].reshape(blocks, width, nc)

    @pl.when(sec == 0)
    def _():
        sol_ref[:, :, nc:2 * nc] = x_ref[0].reshape(blocks, width, nc)
        hand_ref[:, :, nc:2 * nc] = passed[0].reshape(blocks, width, nc)

    @pl.when(sec != 0)
    def _():
        give_back(0, 1).wait_recv()
        sol_ref[:, :, columns_of(1 - plane)] = ret[0].reshape(blocks, width, nc)
        give_back(1, 1).wait_recv()
        hand_ref[:, :, columns_of(1 - plane)] = ret[1].reshape(blocks, width, nc)
        for copy in factor_copies():
            copy.wait_send()

    sent(2)

    @pl.when(place < half - 1)
    def _():
        pass_on(2).wait_send()

    @pl.when(sec != half)
    def _():
        give_back(0, 1).wait_send()
        give_back(1, 1).wait_send()


def mirrored(n_sec, n_col, rhs, diag_inv, off_tiles, targets, row_slot):
    blocks, width, columns = rhs.shape
    noff = off_tiles.shape[1]
    rows = row_slot.shape[1]
    n_lo = low_size(n_col)
    n_hi = n_col // n_lo
    nc = columns // 2
    size = blocks * width
    pairs = blocks // 2
    lanes = -(-rows // 128) * 128

    vmem = pl.BlockSpec(memory_space=pltpu.VMEM)
    smem = pl.BlockSpec(memory_space=pltpu.SMEM)
    hbm = pl.BlockSpec(memory_space=pl.ANY)
    out = jax.ShapeDtypeStruct((blocks, width, columns), jnp.bfloat16)
    dma = pltpu.SemaphoreType.DMA
    bf16 = jnp.bfloat16
    return pl.pallas_call(
        functools.partial(kernel, (n_sec, n_hi, n_lo)),
        out_shape=(out, out),
        in_specs=[smem, smem, hbm, hbm, hbm],
        out_specs=(vmem, vmem),
        scratch_shapes=[
            pltpu.VMEM((3, blocks, width, nc), bf16),
            pltpu.VMEM((2, blocks, width, width), bf16),
            pltpu.VMEM((blocks, noff, width, width), bf16),
            pltpu.VMEM((pairs, noff + 1, width, 2 * width), bf16),
            pltpu.VMEM((pairs, noff + 1, width, 2 * width), bf16),
            pltpu.VMEM((2, blocks, lanes), jnp.int32),
            pltpu.SMEM((2, blocks, lanes), jnp.int32),
            pltpu.VMEM((2, rows, width, size), bf16),
            pltpu.VMEM((3, size, nc), bf16),
            pltpu.VMEM((2, size, nc), bf16),
            pltpu.VMEM((3, n_lo - 1, n_hi, size, nc), bf16),
            pltpu.VMEM((3, n_lo - 1, n_hi, size, nc), bf16),
            pltpu.VMEM((3, n_hi - 1, size, nc), bf16),
            pltpu.VMEM((3, n_hi - 1, size, nc), bf16),
            pltpu.VMEM((3, size, nc), jnp.float32),
            pltpu.VMEM((3, size, nc), bf16),
            pltpu.VMEM((2, size, nc), bf16),
            dma((6,)),
            dma((3 + pairs,)),
            dma((3 + pairs,)),
            dma((3, n_lo - 1, n_hi)),
            dma((3, n_lo - 1, n_hi)),
            dma((3, n_hi - 1)),
            dma((3, n_hi - 1)),
            dma((3,)),
            dma((2,)),
            dma((2,)),
            dma((2,)),
        ],
        compiler_params=pltpu.CompilerParams(
            collective_id=0, has_side_effects=True, vmem_limit_bytes=60 * 1024 * 1024
        ),
    )(targets, row_slot, rhs, diag_inv, off_tiles)


def chains_kernel(
    dims, targets_ref, slot_ref, rhs_hbm, diag_hbm, off_hbm, sol_ref, hand_ref,
    rhs_ref, off_ref, pack_0, pack_1, pack_2, pack_3, diag_ref, idx_vec, idx_ref, rin, a_ref, w_ref,
    send1, recv1, send2, recv2, acc, xs, hs, ret,
    in_sem, fs_sem, fr_sem, rs_sem, rr_sem, s1_sem, r1_sem, s2_sem, r2_sem, p_sem, gs_sem, gr_sem,
):
    n_hi, n_lo = dims
    blocks, noff, width = off_hbm.shape[:3]
    lanes = idx_vec.shape[2]
    pairs = blocks // 2
    size = blocks * width
    packed = pairs * width
    wide = 2 * width
    sec = lax.axis_index("sec")
    col = lax.axis_index("col")
    plane, place = sec // 2, sec % 2
    hi, lo = col // n_lo, col % n_lo
    bf16, f32 = jnp.bfloat16, jnp.float32

    own_idx = pltpu.make_async_copy(idx_vec.at[sec], idx_ref.at[sec], in_sem.at[0])
    load_off = pltpu.make_async_copy(off_hbm, off_ref, in_sem.at[1])
    load_diag = pltpu.make_async_copy(diag_hbm, diag_ref.at[sec], in_sem.at[2])
    load_rhs = pltpu.make_async_copy(rhs_hbm, rhs_ref, in_sem.at[3])
    for load in (load_off, load_diag, load_rhs):
        load.start()

    def hi_flip(o):
        value, bit = hi, 1
        while bit < n_hi:
            value = value + ((o // bit) % 2) * (bit - 2 * bit * ((value // bit) % 2))
            bit *= 2
        return value

    def at_sec(to):
        return {"sec": to, "col": col}

    lo_peer = {"sec": sec, "col": hi * n_lo + 1 - lo}

    def hi_peer(o):
        return {"sec": sec, "col": hi_flip(o) * n_lo + lo}

    barrier = pltpu.get_barrier_semaphore()
    peers = [lo_peer] + [hi_peer(o) for o in range(1, n_hi)]
    peers += [at_sec(lax.rem(sec + o, 4)) for o in range(1, 4)]
    for peer in peers:
        pl.semaphore_signal(barrier, inc=1, device_id=peer, device_id_type=MESH)

    slot_of_lane = lax.broadcasted_iota(jnp.int32, (1, lanes), 1)
    for k in range(blocks):
        found = jnp.full((1, lanes), noff, jnp.int32)
        for p in range(noff):
            dest = slot_ref[0, targets_ref[k, p]]
            found = jnp.where(slot_of_lane == dest, p, found)
        idx_vec[sec, k:k + 1, :] = found
    own_idx.start()
    packs = (pack_0, pack_1, pack_2, pack_3)
    for pack_ref in packs:
        for q in range(pairs):
            pack_ref[q, noff] = jnp.zeros((width, wide), bf16)

    left = lax.broadcasted_iota(jnp.int32, (width, wide), 1) < width

    def swap(x):
        return jnp.concatenate([x[:, width:], x[:, :width]], axis=1)

    load_off.wait()

    def pack_into(pack_ref):
        def step(p, carry):
            for q in range(pairs):
                pack_ref[q, p] = jnp.concatenate([off_ref[2 * q, p], off_ref[2 * q + 1, p]], axis=1)
            return carry

        lax.fori_loop(0, noff, step, 0)

    for s in range(4):
        @pl.when(sec == s)
        def _():
            pack_into(packs[s])

    load_diag.wait()
    load_rhs.wait()
    own_idx.wait()
    pl.semaphore_wait(barrier, len(peers))

    every = range(2 + pairs)
    halves = (range(2 + pairs // 2), range(2 + pairs // 2, 2 + pairs))

    def factor(s, to, step, pieces=every):
        ends = [idx_vec.at[s], diag_ref.at[s]]
        ends += [packs[s].at[q, pl.ds(0, noff)] for q in range(pairs)]
        return [
            pltpu.make_async_remote_copy(
                src_ref=ends[n], dst_ref=ends[n], send_sem=fs_sem.at[step, n], recv_sem=fr_sem.at[s, n],
                device_id=at_sec(to), device_id_type=MESH,
            )
            for n in pieces
        ]

    def start(copies):
        for copy in copies:
            copy.start()

    def wait_sent(copies):
        for copy in copies:
            copy.wait_send()

    def to_scalar_memory(s):
        to_scalar = pltpu.make_async_copy(idx_vec.at[s], idx_ref.at[s], in_sem.at[0])
        to_scalar.start()
        to_scalar.wait()

    def factor_here(s):
        for copy in factor(s, 0, 0):
            copy.wait_recv()
        to_scalar_memory(s)

    def by_core(act):
        for core in range(2):
            @pl.when(place == core)
            def _():
                act(core)

    def across(s, act):
        by_core(lambda core: act(factor(s, 2 - s // 2 * 2 + core, s, halves[core])))

    def arrive(s):
        def step(core):
            for copy in factor(s, 0, 0, halves[core]):
                copy.wait_recv()
            start(factor(s, s // 2 * -2 + 3 - core, s, halves[core]))

        by_core(step)

    def relayed(s):
        by_core(lambda core: wait_sent(factor(s, 0, s, halves[core])))

    def arrive_late(s):
        def step(core):
            for copy in factor(s, 0, 0, halves[1 - core]):
                copy.wait_recv()

        by_core(step)
        to_scalar_memory(s)

    def chain_of(device):
        return 2 * (1 - device // 2) + device % 2

    mine = chain_of(sec)

    def rhs_copy(s, chain, to, step, slot):
        return pltpu.make_async_remote_copy(
            src_ref=rin.at[s, chain], dst_ref=rin.at[s, chain],
            send_sem=rs_sem.at[step], recv_sem=rr_sem.at[slot],
            device_id=at_sec(to), device_id_type=MESH,
        )

    def rhs_sends(s):
        if s == 0:
            return [rhs_copy(0, 1, 1, 0, 4), rhs_copy(0, 3, 1, 1, 0)]
        return [
            rhs_copy(s, 2 * (1 - to // 2) + to % 2, to, n, s)
            for n, to in enumerate(to for to in (s ^ 1, s ^ 2, s ^ 3))
        ]

    def rhs_here(s):
        rhs_copy(s, mine, 0, 0, s).wait_recv()

    other = plane * 2 + 1 - place
    for s in range(4):
        @pl.when(sec == s)
        def _():
            start(factor(s, s ^ 1, 0))

    for m in range(2):
        part = slice(m * wide, (m + 1) * wide)
        for q in range(pairs):
            even, odd = rhs_ref[2 * q, :, part], rhs_ref[2 * q + 1, :, part]
            rows = slice(q * width, (q + 1) * width)
            rin[sec, 2 * m, rows] = jnp.where(left, even, swap(odd))
            rin[sec, 2 * m + 1, rows] = jnp.where(left, swap(even), odd)

    for s in range(4):
        @pl.when(sec == s)
        def _():
            start(rhs_sends(s))

    def build(s, d):
        for r in range(blocks):
            i = d * blocks + r
            for q in range(pairs):
                at = (r % 2) * size + q * wide
                a_ref[s, d * pairs + r // 2, :, at:at + wide] = jnp.where(
                    left, packs[s][q, idx_ref[s, 2 * q, i]], packs[s][q, idx_ref[s, 2 * q + 1, i]]
                )

    def build_range(s, low, high):
        def step(d, carry):
            build(s, d)
            return carry

        lax.fori_loop(low, high, step, 0)

    def copy1(j, oh):
        return pltpu.make_async_remote_copy(
            src_ref=send1.at[j, oh], dst_ref=recv1.at[j, oh],
            send_sem=s1_sem.at[j, oh], recv_sem=r1_sem.at[j, oh],
            device_id=lo_peer, device_id_type=MESH,
        )

    def copy2(j, oh):
        return pltpu.make_async_remote_copy(
            src_ref=send2.at[j, oh - 1], dst_ref=recv2.at[j, oh - 1],
            send_sem=s2_sem.at[j, oh - 1], recv_sem=r2_sem.at[j, oh - 1],
            device_id=hi_peer(oh), device_id_type=MESH,
        )

    def give(which, j, s, chain):
        return pltpu.make_async_remote_copy(
            src_ref=(xs, hs)[which].at[j], dst_ref=ret.at[which, chain],
            send_sem=gs_sem.at[which, j], recv_sem=gr_sem.at[which, chain],
            device_id=at_sec(s), device_id_type=MESH,
        )

    def give_out(which, j, s, chain):
        @pl.when(sec == s)
        def _():
            ret[which, chain] = (xs, hs)[which][j]

        @pl.when(sec != s)
        def _():
            give(which, j, s, chain).start()

    def product(s, w, dest):
        a = a_ref[s, pl.ds(dest * pairs, pairs)].reshape(packed, 2 * size)
        return jnp.dot(a, w_ref[w], preferred_element_type=f32)

    def first(s, j, w, chain, h, fresh=None):
        for q in range(pairs):
            rows = slice(q * width, (q + 1) * width)
            residual = rin[s, chain, rows]
            if h is not None:
                residual = (residual.astype(f32) - h[rows].astype(f32)).astype(bf16)
            z = jnp.dot(
                diag_ref[s, 2 * q:2 * q + 2].reshape(wide, width), residual,
                preferred_element_type=f32,
            ).astype(bf16)
            top, low = z[:width], z[width:]
            xs[j, rows] = jnp.where(left, top, low)
            zero = jnp.zeros_like(top)
            at = q * wide
            w_ref[w, at:at + width] = jnp.where(left, top, zero)
            w_ref[w, at + width:at + wide] = jnp.where(left, swap(low), zero)
            w_ref[w, size + at:size + at + width] = jnp.where(left, zero, swap(top))
            w_ref[w, size + at + width:size + at + wide] = jnp.where(left, zero, low)

        def step(t, carry):
            oh = n_hi - 1 - t
            dest = hi_flip(oh) * n_lo + 1 - lo
            if fresh is not None:
                @pl.when(plane <= fresh)
                def _():
                    build(s, dest)

            send1[j, oh] = product(s, w, dest).astype(bf16)
            copy1(j, oh).start()
            return carry

        lax.fori_loop(0, n_hi, step, 0)
        give_out(0, j, s, chain)

    def middle(s, j, w, fresh=None, also=None):

        def step(t, carry):
            oh = n_hi - 1 - t
            dest = hi_flip(oh) * n_lo + lo
            if fresh is not None:
                @pl.when(plane <= fresh)
                def _():
                    build(s, dest)

            total = product(s, w, dest)
            copy1(j, oh).wait_recv()
            total = total + recv1[j, oh].astype(f32)

            @pl.when(oh > 0)
            def _():
                send2[j, oh - 1] = total.astype(bf16)
                copy2(j, oh).start()

            @pl.when(oh == 0)
            def _():
                acc[w] = total

            if also is not None:
                @pl.when(plane == 0)
                def _():
                    build(also, 2 * t)
                    build(also, 2 * t + 1)
            return carry

        lax.fori_loop(0, n_hi, step, 0)

    def last(j, w):
        total = acc[w]
        for oh in range(n_hi - 1, 0, -1):
            copy2(j, oh).wait_recv()
            total = total + recv2[j, oh - 1].astype(f32)
        hs[j] = total.astype(bf16)

    def sent(j, s):
        for oh in range(n_hi):
            copy1(j, oh).wait_send()
        for oh in range(1, n_hi):
            copy2(j, oh).wait_send()

        @pl.when(sec != s)
        def _():
            give(0, j, s, mine).wait_send()
            give(1, j, s, mine).wait_send()

    def pass_on():
        return pltpu.make_async_remote_copy(
            src_ref=hs.at[4], dst_ref=hs.at[0], send_sem=p_sem.at[0], recv_sem=p_sem.at[1],
            device_id=at_sec(2 + place), device_id_type=MESH,
        )

    def here(s):
        factor_here(s)
        if s > 0:
            rhs_here(s)

    @pl.when(plane == 0)
    def _():
        @pl.when(place == 1)
        def _():
            across(1, start)
            here(0)
            rhs_copy(0, 1, 0, 0, 4).wait_recv()
            rhs_copy(0, 3, 0, 0, 0).wait_recv()

        first(0, 0, 1, mine, None, fresh=1)

        @pl.when(place == 0)
        def _():
            here(1)
            across(1, start)

        first(0, 4, 0, place, None)
        middle(0, 0, 1, fresh=1)
        middle(0, 4, 0)
        last(0, 1)

    @pl.when(plane == 1)
    def _():
        for s in (2, 3):
            @pl.when(sec != s)
            def _():
                here(s)

        across(2, start)
        build_range(2, 0, n_hi * n_lo)
        build_range(3, 0, n_hi * n_lo)
        arrive(1)
        arrive_late(1)
        rhs_here(1)
        across(2, wait_sent)
        across(3, start)
        pass_on().wait_recv()

    first(1, 1, 1, mine, hs.at[0], fresh=1)

    @pl.when(plane == 0)
    def _():
        last(4, 0)
        pass_on().start()
        give_out(1, 0, 0, mine)
        give_out(1, 4, 0, place)

    middle(1, 1, 1, fresh=1)

    @pl.when(plane == 0)
    def _():
        arrive(2)

    last(1, 1)

    @pl.when(plane == 0)
    def _():
        arrive_late(2)
        rhs_here(2)

    first(2, 2, 1, mine, hs.at[1], fresh=0)
    give_out(1, 1, 1, mine)

    middle(2, 2, 1, fresh=0)

    @pl.when(plane == 0)
    def _():
        arrive(3)

    last(2, 1)

    @pl.when(plane == 0)
    def _():
        arrive_late(3)
        rhs_here(3)

    first(3, 3, 1, mine, hs.at[2], fresh=0)
    give_out(1, 2, 2, mine)
    middle(3, 3, 1, fresh=0)
    last(3, 1)
    give_out(1, 3, 3, mine)

    def returned(which, chain):
        return pltpu.make_async_remote_copy(
            src_ref=xs.at[0], dst_ref=ret.at[which, chain],
            send_sem=gs_sem.at[which, 0], recv_sem=gr_sem.at[which, chain],
            device_id=at_sec(other), device_id_type=MESH,
        )

    for which, out in ((0, sol_ref), (1, hand_ref)):
        for m in range(2):
            returned(which, 2 * m + 1 - place).wait_recv()

            @pl.when((sec != 0) & (plane == m))
            def _():
                returned(which, 2 * m + place).wait_recv()

            part = slice(m * wide, (m + 1) * wide)
            for q in range(pairs):
                rows = slice(q * width, (q + 1) * width)
                one, two = ret[which, 2 * m, rows], ret[which, 2 * m + 1, rows]
                out[2 * q, :, part] = jnp.where(left, one, swap(two))
                out[2 * q + 1, :, part] = jnp.where(left, swap(one), two)

    for s in range(1, 4):
        sent(s, s)
    wait_sent(factor(0, other, 0))
    for s in range(4):
        @pl.when(sec == s)
        def _():
            wait_sent(rhs_sends(s))

    @pl.when(plane == 0)
    def _():
        sent(0, 0)
        for oh in range(n_hi):
            copy1(4, oh).wait_send()
        for oh in range(1, n_hi):
            copy2(4, oh).wait_send()

        @pl.when(sec != 0)
        def _():
            give(0, 4, 0, place).wait_send()
            give(1, 4, 0, place).wait_send()

        pass_on().wait_send()
        across(1, wait_sent)
        relayed(2)
        relayed(3)

    @pl.when(plane == 1)
    def _():
        across(3, wait_sent)
        relayed(1)


def chains(n_col, rhs, diag_inv, off_tiles, targets, row_slot):
    blocks, width, columns = rhs.shape
    noff = off_tiles.shape[1]
    rows = row_slot.shape[1]
    n_lo = 2
    n_hi = n_col // n_lo
    size = blocks * width
    pairs = blocks // 2
    packed = pairs * width
    wide = 2 * width
    lanes = -(-rows // 128) * 128
    vmem = pl.BlockSpec(memory_space=pltpu.VMEM)
    smem = pl.BlockSpec(memory_space=pltpu.SMEM)
    hbm = pl.BlockSpec(memory_space=pl.ANY)
    out = jax.ShapeDtypeStruct((blocks, width, columns), jnp.bfloat16)
    dma = pltpu.SemaphoreType.DMA
    bf16 = jnp.bfloat16
    return pl.pallas_call(
        functools.partial(chains_kernel, (n_hi, n_lo)),
        out_shape=(out, out),
        in_specs=[smem, smem, hbm, hbm, hbm],
        out_specs=(vmem, vmem),
        scratch_shapes=[
            pltpu.VMEM((blocks, width, columns), bf16),
            pltpu.VMEM((blocks, noff, width, width), bf16),
            pltpu.VMEM((pairs, noff + 1, width, wide), bf16),
            pltpu.VMEM((pairs, noff + 1, width, wide), bf16),
            pltpu.VMEM((pairs, noff + 1, width, wide), bf16),
            pltpu.VMEM((pairs, noff + 1, width, wide), bf16),
            pltpu.VMEM((4, blocks, width, width), bf16),
            pltpu.VMEM((4, blocks, lanes), jnp.int32),
            pltpu.SMEM((4, blocks, lanes), jnp.int32),
            pltpu.VMEM((4, 4, packed, wide), bf16),
            pltpu.VMEM((4, rows // 2, width, 2 * size), bf16),
            pltpu.VMEM((2, 2 * size, wide), bf16),
            pltpu.VMEM((5, n_hi, packed, wide), bf16),
            pltpu.VMEM((5, n_hi, packed, wide), bf16),
            pltpu.VMEM((5, n_hi - 1, packed, wide), bf16),
            pltpu.VMEM((5, n_hi - 1, packed, wide), bf16),
            pltpu.VMEM((2, packed, wide), jnp.float32),
            pltpu.VMEM((5, packed, wide), bf16),
            pltpu.VMEM((5, packed, wide), bf16),
            pltpu.VMEM((2, 4, packed, wide), bf16),
            dma((4,)),
            dma((4, 2 + pairs)),
            dma((4, 2 + pairs)),
            dma((3,)),
            dma((5,)),
            dma((5, n_hi)),
            dma((5, n_hi)),
            dma((5, n_hi - 1)),
            dma((5, n_hi - 1)),
            dma((2,)),
            dma((2, 5)),
            dma((2, 4)),
        ],
        compiler_params=pltpu.CompilerParams(
            collective_id=1, has_side_effects=True, vmem_limit_bytes=56 * 1024 * 1024
        ),
    )(targets, row_slot, rhs, diag_inv, off_tiles)


def fits_chains(n_sec, n_col, rhs, row_slot):
    blocks, width, columns = rhs.shape
    n_hi = n_col // 2
    return (
        n_sec == 4 and n_col % 2 == 0 and n_hi & (n_hi - 1) == 0 and columns == 4 * width and width == 64
        and blocks % 2 == 0 and row_slot.shape[1] == blocks * n_col
    )


def shards(n_sec, n_col, rhs, diag_inv, off_tiles, targets, row_slot):
    if fits_chains(n_sec, n_col, rhs, row_slot):
        return chains(n_col, rhs, diag_inv, off_tiles, targets, row_slot)
    return mirrored(n_sec, n_col, rhs, diag_inv, off_tiles, targets, row_slot)


def solution(mesh):
    return jax.shard_map(
        functools.partial(shards, mesh.shape["sec"], mesh.shape["col"]),
        mesh=mesh,
        in_specs=(
            P(("sec", "col"), None, None),
            P(("sec", "col"), None, None),
            P(("sec", "col"), None, None, None),
            P(("sec", "col"), None),
            P("sec", None),
        ),
        out_specs=(P(("sec", "col"), None, None), P(("sec", "col"), None, None)),
        check_vma=False,
    )
```

```python
import functools

import jax
import jax.numpy as jnp
from jax import lax
from jax.experimental import pallas as pl
from jax.experimental.pallas import tpu as pltpu
from jax.sharding import PartitionSpec as P

MESH = pl.DeviceIdType.MESH
OWN, MIRROR, OTHER = 0, 1, 2


def low_size(n_col):
    low = 1
    while (2 * low) ** 2 <= n_col:
        low *= 2
    return low


def kernel(
    dims, targets_ref, slot_ref, rhs_hbm, diag_hbm, off_hbm, sol_ref, hand_ref,
    rin, diag_ref, off_ref, pack_own, pack_mirror, idx_vec, idx_ref,
    a_ref, x_ref, inc, send1, recv1, send2, recv2, acc, passed, ret,
    in_sem, fs_sem, fr_sem, s1_sem, r1_sem, s2_sem, r2_sem, sp_sem, rp_sem, sr_sem, rr_sem,
):
    n_sec, n_hi, n_lo = dims
    half = n_sec // 2
    blocks, width = off_hbm.shape[0], off_hbm.shape[2]
    noff = off_hbm.shape[1]
    rows = slot_ref.shape[1]
    lanes = idx_vec.shape[2]
    nc = rin.shape[3]
    size = blocks * width
    pairs = blocks // 2
    sec = lax.axis_index("sec")
    col = lax.axis_index("col")
    plane, place = sec // half, sec % half
    hi, lo = col // n_lo, col % n_lo
    mirror = {"sec": lax.rem(sec + half, n_sec), "col": col}

    def columns_of(which):
        return pl.ds(pl.multiple_of(which * nc, nc), nc)

    loads = [
        pltpu.make_async_copy(off_hbm, off_ref, in_sem.at[0]),
        pltpu.make_async_copy(diag_hbm, diag_ref.at[OWN], in_sem.at[1]),
        pltpu.make_async_copy(rhs_hbm.at[:, :, columns_of(plane)], rin.at[OWN], in_sem.at[2]),
        pltpu.make_async_copy(rhs_hbm.at[:, :, columns_of(1 - plane)], rin.at[OTHER], in_sem.at[3]),
    ]
    for load in loads:
        load.start()

    def lo_peer(o):
        return {"sec": sec, "col": hi * n_lo + lax.rem(lo + o, n_lo)}

    def hi_flip(o):
        value, bit = hi, 1
        while bit < n_hi:
            if o & bit:
                value = value + bit - 2 * bit * ((value // bit) % 2)
            bit *= 2
        return value

    def hi_peer(o):
        return {"sec": sec, "col": hi_flip(o) * n_lo + lo}

    barrier = pltpu.get_barrier_semaphore()
    for o in range(1, n_lo):
        pl.semaphore_signal(barrier, inc=1, device_id=lo_peer(o), device_id_type=MESH)
    for o in range(1, n_hi):
        pl.semaphore_signal(barrier, inc=1, device_id=hi_peer(o), device_id_type=MESH)
    for o in range(1, n_sec):
        pl.semaphore_signal(
            barrier, inc=1, device_id={"sec": lax.rem(sec + o, n_sec), "col": col},
            device_id_type=MESH,
        )

    slot_of_lane = lax.broadcasted_iota(jnp.int32, (1, lanes), 1)
    for k in range(blocks):
        found = jnp.full((1, lanes), noff, jnp.int32)
        for p in range(noff):
            dest = slot_ref[0, targets_ref[k, p]]
            found = jnp.where(slot_of_lane == dest, p, found)
        idx_vec[OWN, k:k + 1, :] = found
    to_scalar = pltpu.make_async_copy(idx_vec.at[OWN], idx_ref.at[OWN], in_sem.at[4])
    to_scalar.start()

    packs = (pack_own, pack_mirror)
    for pack_ref in packs:
        for q in range(pairs):
            pack_ref[q, noff] = jnp.zeros((width, 2 * width), jnp.bfloat16)
    for load in loads:
        load.wait()

    def pack(p, carry):
        for q in range(pairs):
            pack_own[q, p] = jnp.concatenate([off_ref[2 * q, p], off_ref[2 * q + 1, p]], axis=1)
        return carry

    lax.fori_loop(0, noff, pack, 0)
    to_scalar.wait()
    pl.semaphore_wait(barrier, n_lo - 1 + n_hi - 1 + n_sec - 1)

    def factor_copies():
        ends = [
            (idx_vec.at[OWN], idx_vec.at[MIRROR]),
            (diag_ref.at[OWN], diag_ref.at[MIRROR]),
            (rin.at[OTHER], rin.at[MIRROR]),
        ] + [
            (pack_own.at[q, pl.ds(0, noff)], pack_mirror.at[q, pl.ds(0, noff)])
            for q in range(pairs)
        ]
        return [
            pltpu.make_async_remote_copy(
                src_ref=src, dst_ref=dst, send_sem=fs_sem.at[n], recv_sem=fr_sem.at[n],
                device_id=mirror, device_id_type=MESH,
            )
            for n, (src, dst) in enumerate(ends)
        ]

    @pl.when(sec != 0)
    def _():
        for copy in factor_copies():
            copy.start()

    def mirror_factor():
        for copy in factor_copies():
            copy.wait_recv()
        to_scalar = pltpu.make_async_copy(idx_vec.at[MIRROR], idx_ref.at[MIRROR], in_sem.at[5])
        to_scalar.start()
        to_scalar.wait()

    def source(role):
        return lax.rem(role + plane, 2)

    left = lax.broadcasted_iota(jnp.int32, (width, 2 * width), 1) < width

    def build_row(role, src, i):
        pack_ref = packs[src]
        for q in range(pairs):
            a_ref[role, i, :, 2 * q * width:2 * (q + 1) * width] = jnp.where(
                left,
                pack_ref[q, idx_ref[src, 2 * q, i]],
                pack_ref[q, idx_ref[src, 2 * q + 1, i]],
            )

    def build_all(role):
        for src in (OWN, MIRROR):
            @pl.when(source(role) == src)
            def _():
                def step(i, carry):
                    build_row(role, src, i)
                    return carry

                lax.fori_loop(0, rows, step, 0)

    def copy1(j, o, oh):
        return pltpu.make_async_remote_copy(
            src_ref=send1.at[j, o - 1, oh], dst_ref=recv1.at[j, o - 1, oh],
            send_sem=s1_sem.at[j, o - 1, oh], recv_sem=r1_sem.at[j, o - 1, oh],
            device_id=lo_peer(o), device_id_type=MESH,
        )

    def copy2(j, oh):
        return pltpu.make_async_remote_copy(
            src_ref=send2.at[j, oh - 1], dst_ref=recv2.at[j, oh - 1],
            send_sem=s2_sem.at[j, oh - 1], recv_sem=r2_sem.at[j, oh - 1],
            device_id=hi_peer(oh), device_id_type=MESH,
        )

    def copyp(j, to_sec, slot):
        return pltpu.make_async_remote_copy(
            src_ref=passed.at[j], dst_ref=inc.at[slot],
            send_sem=sp_sem.at[j], recv_sem=rp_sem.at[slot],
            device_id={"sec": to_sec, "col": col}, device_id_type=MESH,
        )

    def pass_on(j):
        if j == 0:
            return copyp(0, half + 1, 0)
        more = place + 1 < half
        to_sec = plane * half + jnp.where(more, place + 1, 0)
        if j == 1:
            return copyp(1, to_sec, jnp.where(more, 0, 1))
        return copyp(2, to_sec, 1)

    def give_back(which, j):
        return pltpu.make_async_remote_copy(
            src_ref=(x_ref, passed)[which].at[j], dst_ref=ret.at[which],
            send_sem=sr_sem.at[which], recv_sem=rr_sem.at[which],
            device_id=mirror, device_id_type=MESH,
        )

    order = list(range(n_hi - 1, -1, -1))

    def product(j, oh, o):
        role = max(j - 1, 0)
        dest = hi_flip(oh) * n_lo + lax.rem(lo + o, n_lo)
        if j == 0:
            for r in range(blocks):
                build_row(0, OWN, dest * blocks + r)
        a = a_ref[role, pl.ds(dest * blocks, blocks)].reshape(size, size)
        return jnp.dot(a, x_ref[j], preferred_element_type=jnp.float32)

    def first(j, fresh):
        role = max(j - 1, 0)
        src = source(role)
        which = OTHER if j == 0 else src
        if not fresh:
            copyp(j, sec, role).wait_recv()
        for k in range(blocks):
            part = slice(k * width, (k + 1) * width)
            residual = rin[which, k]
            if not fresh:
                residual = (
                    residual.astype(jnp.float32) - inc[role, part, :].astype(jnp.float32)
                ).astype(jnp.bfloat16)
            x_ref[j, part, :] = jnp.dot(
                diag_ref[src, k], residual, preferred_element_type=jnp.float32
            ).astype(jnp.bfloat16)
        for oh in order:
            for o in range(1, n_lo):
                send1[j, o - 1, oh] = product(j, oh, o).astype(jnp.bfloat16)
                copy1(j, o, oh).start()

    def middle(j):
        for oh in order:
            total = product(j, oh, 0)
            for o in range(1, n_lo):
                copy1(j, o, oh).wait_recv()
                total = total + recv1[j, o - 1, oh].astype(jnp.float32)
            if oh == 0:
                acc[j] = total
            else:
                send2[j, oh - 1] = total.astype(jnp.bfloat16)
                copy2(j, oh).start()

    def last(j):
        total = acc[j]
        for oh in range(1, n_hi):
            copy2(j, oh).wait_recv()
            total = total + recv2[j, oh - 1].astype(jnp.float32)
        passed[j] = total.astype(jnp.bfloat16)
        if j < 2:
            pass_on(j).start()
        else:
            @pl.when(place < half - 1)
            def _():
                pass_on(j).start()

        if j > 0:
            @pl.when(source(j - 1) == MIRROR)
            def _():
                give_back(0, j).start()
                give_back(1, j).start()

    def sent(j):
        for oh in range(n_hi):
            for o in range(1, n_lo):
                copy1(j, o, oh).wait_send()
        for oh in range(1, n_hi):
            copy2(j, oh).wait_send()

    @pl.when(sec == 0)
    def _():
        first(0, True)
        middle(0)
        first(1, True)
        last(0)
        middle(1)
        last(1)
        sent(0)
        sent(1)
        pass_on(0).wait_send()
        pass_on(1).wait_send()

    @pl.when(place > 0)
    def _():
        @pl.when(plane == 1)
        def _():
            mirror_factor()

        build_all(0)
        first(1, False)
        middle(1)
        last(1)
        sent(1)
        pass_on(1).wait_send()

    @pl.when(plane == 0)
    def _():
        mirror_factor()

    build_all(1)
    first(2, False)
    middle(2)
    last(2)
    own = 1 + plane
    sol_ref[:, :, columns_of(plane)] = x_ref[own].reshape(blocks, width, nc)
    hand_ref[:, :, columns_of(plane)] = passed[own].reshape(blocks, width, nc)

    @pl.when(sec == 0)
    def _():
        sol_ref[:, :, nc:2 * nc] = x_ref[0].reshape(blocks, width, nc)
        hand_ref[:, :, nc:2 * nc] = passed[0].reshape(blocks, width, nc)

    @pl.when(sec != 0)
    def _():
        give_back(0, 1).wait_recv()
        sol_ref[:, :, columns_of(1 - plane)] = ret[0].reshape(blocks, width, nc)
        give_back(1, 1).wait_recv()
        hand_ref[:, :, columns_of(1 - plane)] = ret[1].reshape(blocks, width, nc)
        for copy in factor_copies():
            copy.wait_send()

    sent(2)

    @pl.when(place < half - 1)
    def _():
        pass_on(2).wait_send()

    @pl.when(sec != half)
    def _():
        give_back(0, 1).wait_send()
        give_back(1, 1).wait_send()


def mirrored(n_sec, n_col, rhs, diag_inv, off_tiles, targets, row_slot):
    blocks, width, columns = rhs.shape
    noff = off_tiles.shape[1]
    rows = row_slot.shape[1]
    n_lo = low_size(n_col)
    n_hi = n_col // n_lo
    nc = columns // 2
    size = blocks * width
    pairs = blocks // 2
    lanes = -(-rows // 128) * 128

    vmem = pl.BlockSpec(memory_space=pltpu.VMEM)
    smem = pl.BlockSpec(memory_space=pltpu.SMEM)
    hbm = pl.BlockSpec(memory_space=pl.ANY)
    out = jax.ShapeDtypeStruct((blocks, width, columns), jnp.bfloat16)
    dma = pltpu.SemaphoreType.DMA
    bf16 = jnp.bfloat16
    return pl.pallas_call(
        functools.partial(kernel, (n_sec, n_hi, n_lo)),
        out_shape=(out, out),
        in_specs=[smem, smem, hbm, hbm, hbm],
        out_specs=(vmem, vmem),
        scratch_shapes=[
            pltpu.VMEM((3, blocks, width, nc), bf16),
            pltpu.VMEM((2, blocks, width, width), bf16),
            pltpu.VMEM((blocks, noff, width, width), bf16),
            pltpu.VMEM((pairs, noff + 1, width, 2 * width), bf16),
            pltpu.VMEM((pairs, noff + 1, width, 2 * width), bf16),
            pltpu.VMEM((2, blocks, lanes), jnp.int32),
            pltpu.SMEM((2, blocks, lanes), jnp.int32),
            pltpu.VMEM((2, rows, width, size), bf16),
            pltpu.VMEM((3, size, nc), bf16),
            pltpu.VMEM((2, size, nc), bf16),
            pltpu.VMEM((3, n_lo - 1, n_hi, size, nc), bf16),
            pltpu.VMEM((3, n_lo - 1, n_hi, size, nc), bf16),
            pltpu.VMEM((3, n_hi - 1, size, nc), bf16),
            pltpu.VMEM((3, n_hi - 1, size, nc), bf16),
            pltpu.VMEM((3, size, nc), jnp.float32),
            pltpu.VMEM((3, size, nc), bf16),
            pltpu.VMEM((2, size, nc), bf16),
            dma((6,)),
            dma((3 + pairs,)),
            dma((3 + pairs,)),
            dma((3, n_lo - 1, n_hi)),
            dma((3, n_lo - 1, n_hi)),
            dma((3, n_hi - 1)),
            dma((3, n_hi - 1)),
            dma((3,)),
            dma((2,)),
            dma((2,)),
            dma((2,)),
        ],
        compiler_params=pltpu.CompilerParams(
            collective_id=0, has_side_effects=True, vmem_limit_bytes=60 * 1024 * 1024
        ),
    )(targets, row_slot, rhs, diag_inv, off_tiles)


def chains_kernel(
    dims, targets_ref, slot_ref, rhs_hbm, diag_hbm, off_hbm, sol_ref, hand_ref,
    rhs_ref, off_ref, pack_0, pack_1, pack_2, pack_3, diag_ref, idx_vec, idx_ref, rin, a_ref, w_ref,
    send1, recv1, send2, recv2, acc, xs, hs, ret,
    in_sem, fs_sem, fr_sem, rs_sem, rr_sem, s1_sem, r1_sem, s2_sem, r2_sem, p_sem, gs_sem, gr_sem,
):
    n_hi, n_lo = dims
    blocks, noff, width = off_hbm.shape[:3]
    lanes = idx_vec.shape[2]
    pairs = blocks // 2
    size = blocks * width
    packed = pairs * width
    wide = 2 * width
    sec = lax.axis_index("sec")
    col = lax.axis_index("col")
    plane, place = sec // 2, sec % 2
    hi, lo = col // n_lo, col % n_lo
    bf16, f32 = jnp.bfloat16, jnp.float32

    own_idx = pltpu.make_async_copy(idx_vec.at[sec], idx_ref.at[sec], in_sem.at[0])
    load_off = pltpu.make_async_copy(off_hbm, off_ref, in_sem.at[1])
    load_diag = pltpu.make_async_copy(diag_hbm, diag_ref.at[sec], in_sem.at[2])
    load_rhs = pltpu.make_async_copy(rhs_hbm, rhs_ref, in_sem.at[3])
    for load in (load_off, load_diag, load_rhs):
        load.start()

    def hi_flip(o):
        value, bit = hi, 1
        while bit < n_hi:
            value = value + ((o // bit) % 2) * (bit - 2 * bit * ((value // bit) % 2))
            bit *= 2
        return value

    def at_sec(to):
        return {"sec": to, "col": col}

    lo_peer = {"sec": sec, "col": hi * n_lo + 1 - lo}

    def hi_peer(o):
        return {"sec": sec, "col": hi_flip(o) * n_lo + lo}

    barrier = pltpu.get_barrier_semaphore()
    peers = [lo_peer] + [hi_peer(o) for o in range(1, n_hi)]
    peers += [at_sec(lax.rem(sec + o, 4)) for o in range(1, 4)]
    for peer in peers:
        pl.semaphore_signal(barrier, inc=1, device_id=peer, device_id_type=MESH)

    slot_of_lane = lax.broadcasted_iota(jnp.int32, (1, lanes), 1)
    for k in range(blocks):
        found = jnp.full((1, lanes), noff, jnp.int32)
        for p in range(noff):
            dest = slot_ref[0, targets_ref[k, p]]
            found = jnp.where(slot_of_lane == dest, p, found)
        idx_vec[sec, k:k + 1, :] = found
    own_idx.start()
    packs = (pack_0, pack_1, pack_2, pack_3)
    for pack_ref in packs:
        for q in range(pairs):
            pack_ref[q, noff] = jnp.zeros((width, wide), bf16)

    left = lax.broadcasted_iota(jnp.int32, (width, wide), 1) < width

    def swap(x):
        return jnp.concatenate([x[:, width:], x[:, :width]], axis=1)

    load_off.wait()

    def pack_into(pack_ref):
        def step(p, carry):
            for q in range(pairs):
                pack_ref[q, p] = jnp.concatenate([off_ref[2 * q, p], off_ref[2 * q + 1, p]], axis=1)
            return carry

        lax.fori_loop(0, noff, step, 0)

    for s in range(4):
        @pl.when(sec == s)
        def _():
            pack_into(packs[s])

    load_diag.wait()
    load_rhs.wait()
    own_idx.wait()
    pl.semaphore_wait(barrier, len(peers))

    every = range(2 + pairs)
    halves = (range(2 + pairs // 2), range(2 + pairs // 2, 2 + pairs))

    def factor(s, to, step, pieces=every):
        ends = [idx_vec.at[s], diag_ref.at[s]]
        ends += [packs[s].at[q, pl.ds(0, noff)] for q in range(pairs)]
        return [
            pltpu.make_async_remote_copy(
                src_ref=ends[n], dst_ref=ends[n], send_sem=fs_sem.at[step, n], recv_sem=fr_sem.at[s, n],
                device_id=at_sec(to), device_id_type=MESH,
            )
            for n in pieces
        ]

    def start(copies):
        for copy in copies:
            copy.start()

    def wait_sent(copies):
        for copy in copies:
            copy.wait_send()

    def to_scalar_memory(s):
        to_scalar = pltpu.make_async_copy(idx_vec.at[s], idx_ref.at[s], in_sem.at[0])
        to_scalar.start()
        to_scalar.wait()

    def factor_here(s):
        for copy in factor(s, 0, 0):
            copy.wait_recv()
        to_scalar_memory(s)

    def by_core(act):
        for core in range(2):
            @pl.when(place == core)
            def _():
                act(core)

    def across(s, act):
        by_core(lambda core: act(factor(s, 2 - s // 2 * 2 + core, s, halves[core])))

    def arrive(s):
        def step(core):
            for copy in factor(s, 0, 0, halves[core]):
                copy.wait_recv()
            start(factor(s, s // 2 * -2 + 3 - core, s, halves[core]))

        by_core(step)

    def relayed(s):
        by_core(lambda core: wait_sent(factor(s, 0, s, halves[core])))

    def arrive_late(s):
        def step(core):
            for copy in factor(s, 0, 0, halves[1 - core]):
                copy.wait_recv()

        by_core(step)
        to_scalar_memory(s)

    def chain_of(device):
        return 2 * (1 - device // 2) + device % 2

    mine = chain_of(sec)

    def rhs_copy(s, chain, to, step, slot):
        return pltpu.make_async_remote_copy(
            src_ref=rin.at[s, chain], dst_ref=rin.at[s, chain],
            send_sem=rs_sem.at[step], recv_sem=rr_sem.at[slot],
            device_id=at_sec(to), device_id_type=MESH,
        )

    def rhs_sends(s):
        if s == 0:
            return [rhs_copy(0, 1, 1, 0, 4), rhs_copy(0, 3, 1, 1, 0)]
        return [
            rhs_copy(s, 2 * (1 - to // 2) + to % 2, to, n, s)
            for n, to in enumerate(to for to in (s ^ 1, s ^ 2, s ^ 3))
        ]

    def rhs_here(s):
        rhs_copy(s, mine, 0, 0, s).wait_recv()

    other = plane * 2 + 1 - place
    for s in range(4):
        @pl.when(sec == s)
        def _():
            start(factor(s, s ^ 1, 0))

    for m in range(2):
        part = slice(m * wide, (m + 1) * wide)
        for q in range(pairs):
            even, odd = rhs_ref[2 * q, :, part], rhs_ref[2 * q + 1, :, part]
            rows = slice(q * width, (q + 1) * width)
            rin[sec, 2 * m, rows] = jnp.where(left, even, swap(odd))
            rin[sec, 2 * m + 1, rows] = jnp.where(left, swap(even), odd)

    for s in range(4):
        @pl.when(sec == s)
        def _():
            start(rhs_sends(s))

    def build(s, d):
        for r in range(blocks):
            i = d * blocks + r
            for q in range(pairs):
                at = (r % 2) * size + q * wide
                a_ref[s, d * pairs + r // 2, :, at:at + wide] = jnp.where(
                    left, packs[s][q, idx_ref[s, 2 * q, i]], packs[s][q, idx_ref[s, 2 * q + 1, i]]
                )

    def build_range(s, low, high):
        def step(d, carry):
            build(s, d)
            return carry

        lax.fori_loop(low, high, step, 0)

    def copy1(j, oh):
        return pltpu.make_async_remote_copy(
            src_ref=send1.at[j, oh], dst_ref=recv1.at[j, oh],
            send_sem=s1_sem.at[j, oh], recv_sem=r1_sem.at[j, oh],
            device_id=lo_peer, device_id_type=MESH,
        )

    def copy2(j, oh):
        return pltpu.make_async_remote_copy(
            src_ref=send2.at[j, oh - 1], dst_ref=recv2.at[j, oh - 1],
            send_sem=s2_sem.at[j, oh - 1], recv_sem=r2_sem.at[j, oh - 1],
            device_id=hi_peer(oh), device_id_type=MESH,
        )

    def give(which, j, s, chain):
        return pltpu.make_async_remote_copy(
            src_ref=(xs, hs)[which].at[j], dst_ref=ret.at[which, chain],
            send_sem=gs_sem.at[which, j], recv_sem=gr_sem.at[which, chain],
            device_id=at_sec(s), device_id_type=MESH,
        )

    def give_out(which, j, s, chain):
        @pl.when(sec == s)
        def _():
            ret[which, chain] = (xs, hs)[which][j]

        @pl.when(sec != s)
        def _():
            give(which, j, s, chain).start()

    def product(s, w, dest):
        a = a_ref[s, pl.ds(dest * pairs, pairs)].reshape(packed, 2 * size)
        return jnp.dot(a, w_ref[w], preferred_element_type=f32)

    def first(s, j, w, chain, h, fresh=None):
        for q in range(pairs):
            rows = slice(q * width, (q + 1) * width)
            residual = rin[s, chain, rows]
            if h is not None:
                residual = (residual.astype(f32) - h[rows].astype(f32)).astype(bf16)
            z = jnp.dot(
                diag_ref[s, 2 * q:2 * q + 2].reshape(wide, width), residual,
                preferred_element_type=f32,
            ).astype(bf16)
            top, low = z[:width], z[width:]
            xs[j, rows] = jnp.where(left, top, low)
            zero = jnp.zeros_like(top)
            at = q * wide
            w_ref[w, at:at + width] = jnp.where(left, top, zero)
            w_ref[w, at + width:at + wide] = jnp.where(left, swap(low), zero)
            w_ref[w, size + at:size + at + width] = jnp.where(left, zero, swap(top))
            w_ref[w, size + at + width:size + at + wide] = jnp.where(left, zero, low)

        def step(t, carry):
            oh = n_hi - 1 - t
            dest = hi_flip(oh) * n_lo + 1 - lo
            if fresh is not None:
                @pl.when(plane <= fresh)
                def _():
                    build(s, dest)

            send1[j, oh] = product(s, w, dest).astype(bf16)
            copy1(j, oh).start()
            return carry

        lax.fori_loop(0, n_hi, step, 0)
        give_out(0, j, s, chain)

    def middle(s, j, w, fresh=None, also=None):

        def step(t, carry):
            oh = n_hi - 1 - t
            dest = hi_flip(oh) * n_lo + lo
            if fresh is not None:
                @pl.when(plane <= fresh)
                def _():
                    build(s, dest)

            total = product(s, w, dest)
            copy1(j, oh).wait_recv()
            total = total + recv1[j, oh].astype(f32)

            @pl.when(oh > 0)
            def _():
                send2[j, oh - 1] = total.astype(bf16)
                copy2(j, oh).start()

            @pl.when(oh == 0)
            def _():
                acc[w] = total

            if also is not None:
                @pl.when(plane == 0)
                def _():
                    build(also, 2 * t)
                    build(also, 2 * t + 1)
            return carry

        lax.fori_loop(0, n_hi, step, 0)

    def last(j, w):
        total = acc[w]
        for oh in range(n_hi - 1, 0, -1):
            copy2(j, oh).wait_recv()
            total = total + recv2[j, oh - 1].astype(f32)
        hs[j] = total.astype(bf16)

    def sent(j, s):
        for oh in range(n_hi):
            copy1(j, oh).wait_send()
        for oh in range(1, n_hi):
            copy2(j, oh).wait_send()

        @pl.when(sec != s)
        def _():
            give(0, j, s, mine).wait_send()
            give(1, j, s, mine).wait_send()

    def pass_on():
        return pltpu.make_async_remote_copy(
            src_ref=hs.at[4], dst_ref=hs.at[0], send_sem=p_sem.at[0], recv_sem=p_sem.at[1],
            device_id=at_sec(2 + place), device_id_type=MESH,
        )

    def here(s):
        factor_here(s)
        if s > 0:
            rhs_here(s)

    @pl.when(plane == 0)
    def _():
        @pl.when(place == 0)
        def _():
            first(0, 0, 1, mine, None, fresh=1)
            here(1)
            across(1, start)
            first(0, 4, 0, place, None)
            middle(0, 0, 1, fresh=1)
            middle(0, 4, 0)
            last(0, 1)

        @pl.when(place == 1)
        def _():
            across(1, start)
            here(0)
            rhs_copy(0, 1, 0, 0, 4).wait_recv()
            rhs_copy(0, 3, 0, 0, 0).wait_recv()
            first(0, 4, 0, place, None, fresh=1)
            first(0, 0, 1, mine, None)
            middle(0, 4, 0, fresh=1)
            middle(0, 0, 1)
            last(4, 0)
            pass_on().start()
            give_out(1, 4, 0, place)
            last(0, 1)

    @pl.when(plane == 1)
    def _():
        for s in (2, 3):
            @pl.when(sec != s)
            def _():
                here(s)

        across(2, start)
        build_range(2, 0, n_hi * n_lo)
        build_range(3, 0, n_hi * n_lo)
        arrive(1)
        arrive_late(1)
        rhs_here(1)
        across(2, wait_sent)
        across(3, start)
        pass_on().wait_recv()

    first(1, 1, 1, mine, hs.at[0], fresh=1)

    @pl.when(plane == 0)
    def _():
        @pl.when(place == 0)
        def _():
            last(4, 0)
            pass_on().start()
            give_out(1, 4, 0, place)

        give_out(1, 0, 0, mine)

    @pl.when((plane == 0) & (place == 1))
    def _():
        arrive(2)

    middle(1, 1, 1, fresh=1)

    @pl.when((plane == 0) & (place == 0))
    def _():
        arrive(2)

    last(1, 1)

    @pl.when(plane == 0)
    def _():
        arrive_late(2)
        rhs_here(2)

    first(2, 2, 1, mine, hs.at[1], fresh=0)
    give_out(1, 1, 1, mine)

    @pl.when((plane == 0) & (place == 1))
    def _():
        arrive(3)

    middle(2, 2, 1, fresh=0)

    @pl.when((plane == 0) & (place == 0))
    def _():
        arrive(3)

    last(2, 1)

    @pl.when(plane == 0)
    def _():
        arrive_late(3)
        rhs_here(3)

    first(3, 3, 1, mine, hs.at[2], fresh=0)
    give_out(1, 2, 2, mine)
    middle(3, 3, 1, fresh=0)
    last(3, 1)
    give_out(1, 3, 3, mine)

    def returned(which, chain):
        return pltpu.make_async_remote_copy(
            src_ref=xs.at[0], dst_ref=ret.at[which, chain],
            send_sem=gs_sem.at[which, 0], recv_sem=gr_sem.at[which, chain],
            device_id=at_sec(other), device_id_type=MESH,
        )

    for which, out in ((0, sol_ref), (1, hand_ref)):
        for m in range(2):
            returned(which, 2 * m + 1 - place).wait_recv()

            @pl.when((sec != 0) & (plane == m))
            def _():
                returned(which, 2 * m + place).wait_recv()

            part = slice(m * wide, (m + 1) * wide)
            for q in range(pairs):
                rows = slice(q * width, (q + 1) * width)
                one, two = ret[which, 2 * m, rows], ret[which, 2 * m + 1, rows]
                out[2 * q, :, part] = jnp.where(left, one, swap(two))
                out[2 * q + 1, :, part] = jnp.where(left, swap(one), two)

    for s in range(1, 4):
        sent(s, s)
    wait_sent(factor(0, other, 0))
    for s in range(4):
        @pl.when(sec == s)
        def _():
            wait_sent(rhs_sends(s))

    @pl.when(plane == 0)
    def _():
        sent(0, 0)
        for oh in range(n_hi):
            copy1(4, oh).wait_send()
        for oh in range(1, n_hi):
            copy2(4, oh).wait_send()

        @pl.when(sec != 0)
        def _():
            give(0, 4, 0, place).wait_send()
            give(1, 4, 0, place).wait_send()

        pass_on().wait_send()
        across(1, wait_sent)
        relayed(2)
        relayed(3)

    @pl.when(plane == 1)
    def _():
        across(3, wait_sent)
        relayed(1)


def chains(n_col, rhs, diag_inv, off_tiles, targets, row_slot):
    blocks, width, columns = rhs.shape
    noff = off_tiles.shape[1]
    rows = row_slot.shape[1]
    n_lo = 2
    n_hi = n_col // n_lo
    size = blocks * width
    pairs = blocks // 2
    packed = pairs * width
    wide = 2 * width
    lanes = -(-rows // 128) * 128
    vmem = pl.BlockSpec(memory_space=pltpu.VMEM)
    smem = pl.BlockSpec(memory_space=pltpu.SMEM)
    hbm = pl.BlockSpec(memory_space=pl.ANY)
    out = jax.ShapeDtypeStruct((blocks, width, columns), jnp.bfloat16)
    dma = pltpu.SemaphoreType.DMA
    bf16 = jnp.bfloat16
    return pl.pallas_call(
        functools.partial(chains_kernel, (n_hi, n_lo)),
        out_shape=(out, out),
        in_specs=[smem, smem, hbm, hbm, hbm],
        out_specs=(vmem, vmem),
        scratch_shapes=[
            pltpu.VMEM((blocks, width, columns), bf16),
            pltpu.VMEM((blocks, noff, width, width), bf16),
            pltpu.VMEM((pairs, noff + 1, width, wide), bf16),
            pltpu.VMEM((pairs, noff + 1, width, wide), bf16),
            pltpu.VMEM((pairs, noff + 1, width, wide), bf16),
            pltpu.VMEM((pairs, noff + 1, width, wide), bf16),
            pltpu.VMEM((4, blocks, width, width), bf16),
            pltpu.VMEM((4, blocks, lanes), jnp.int32),
            pltpu.SMEM((4, blocks, lanes), jnp.int32),
            pltpu.VMEM((4, 4, packed, wide), bf16),
            pltpu.VMEM((4, rows // 2, width, 2 * size), bf16),
            pltpu.VMEM((2, 2 * size, wide), bf16),
            pltpu.VMEM((5, n_hi, packed, wide), bf16),
            pltpu.VMEM((5, n_hi, packed, wide), bf16),
            pltpu.VMEM((5, n_hi - 1, packed, wide), bf16),
            pltpu.VMEM((5, n_hi - 1, packed, wide), bf16),
            pltpu.VMEM((2, packed, wide), jnp.float32),
            pltpu.VMEM((5, packed, wide), bf16),
            pltpu.VMEM((5, packed, wide), bf16),
            pltpu.VMEM((2, 4, packed, wide), bf16),
            dma((4,)),
            dma((4, 2 + pairs)),
            dma((4, 2 + pairs)),
            dma((3,)),
            dma((5,)),
            dma((5, n_hi)),
            dma((5, n_hi)),
            dma((5, n_hi - 1)),
            dma((5, n_hi - 1)),
            dma((2,)),
            dma((2, 5)),
            dma((2, 4)),
        ],
        compiler_params=pltpu.CompilerParams(
            collective_id=1, has_side_effects=True, vmem_limit_bytes=48 * 1024 * 1024
        ),
    )(*[pltpu.with_memory_space_constraint(x, pltpu.MemorySpace.HBM) for x in (targets, row_slot, rhs, diag_inv, off_tiles)])


def fits_chains(n_sec, n_col, rhs, row_slot):
    blocks, width, columns = rhs.shape
    n_hi = n_col // 2
    return (
        n_sec == 4 and n_col % 2 == 0 and n_hi & (n_hi - 1) == 0 and columns == 4 * width and width == 64
        and blocks % 2 == 0 and row_slot.shape[1] == blocks * n_col
    )


def shards(n_sec, n_col, rhs, diag_inv, off_tiles, targets, row_slot):
    if fits_chains(n_sec, n_col, rhs, row_slot):
        return chains(n_col, rhs, diag_inv, off_tiles, targets, row_slot)
    return mirrored(n_sec, n_col, rhs, diag_inv, off_tiles, targets, row_slot)


def solution(mesh):
    return jax.shard_map(
        functools.partial(shards, mesh.shape["sec"], mesh.shape["col"]),
        mesh=mesh,
        in_specs=(
            P(("sec", "col"), None, None),
            P(("sec", "col"), None, None),
            P(("sec", "col"), None, None, None),
            P(("sec", "col"), None),
            P("sec", None),
        ),
        out_specs=(P(("sec", "col"), None, None), P(("sec", "col"), None, None)),
        check_vma=False,
    )
```

```python
import functools

import jax
import jax.numpy as jnp
from jax import lax
from jax.experimental import pallas as pl
from jax.experimental.pallas import tpu as pltpu
from jax.sharding import PartitionSpec as P

MESH = pl.DeviceIdType.MESH
OWN, MIRROR, OTHER = 0, 1, 2


def low_size(n_col):
    low = 1
    while (2 * low) ** 2 <= n_col:
        low *= 2
    return low


def kernel(
    dims, targets_ref, slot_ref, rhs_hbm, diag_hbm, off_hbm, sol_ref, hand_ref,
    rin, diag_ref, off_ref, pack_own, pack_mirror, idx_vec, idx_ref,
    a_ref, x_ref, inc, send1, recv1, send2, recv2, acc, passed, ret,
    in_sem, fs_sem, fr_sem, s1_sem, r1_sem, s2_sem, r2_sem, sp_sem, rp_sem, sr_sem, rr_sem,
):
    n_sec, n_hi, n_lo = dims
    half = n_sec // 2
    blocks, width = off_hbm.shape[0], off_hbm.shape[2]
    noff = off_hbm.shape[1]
    rows = slot_ref.shape[1]
    lanes = idx_vec.shape[2]
    nc = rin.shape[3]
    size = blocks * width
    pairs = blocks // 2
    sec = lax.axis_index("sec")
    col = lax.axis_index("col")
    plane, place = sec // half, sec % half
    hi, lo = col // n_lo, col % n_lo
    mirror = {"sec": lax.rem(sec + half, n_sec), "col": col}

    def columns_of(which):
        return pl.ds(pl.multiple_of(which * nc, nc), nc)

    loads = [
        pltpu.make_async_copy(off_hbm, off_ref, in_sem.at[0]),
        pltpu.make_async_copy(diag_hbm, diag_ref.at[OWN], in_sem.at[1]),
        pltpu.make_async_copy(rhs_hbm.at[:, :, columns_of(plane)], rin.at[OWN], in_sem.at[2]),
        pltpu.make_async_copy(rhs_hbm.at[:, :, columns_of(1 - plane)], rin.at[OTHER], in_sem.at[3]),
    ]
    for load in loads:
        load.start()

    def lo_peer(o):
        return {"sec": sec, "col": hi * n_lo + lax.rem(lo + o, n_lo)}

    def hi_flip(o):
        value, bit = hi, 1
        while bit < n_hi:
            if o & bit:
                value = value + bit - 2 * bit * ((value // bit) % 2)
            bit *= 2
        return value

    def hi_peer(o):
        return {"sec": sec, "col": hi_flip(o) * n_lo + lo}

    barrier = pltpu.get_barrier_semaphore()
    for o in range(1, n_lo):
        pl.semaphore_signal(barrier, inc=1, device_id=lo_peer(o), device_id_type=MESH)
    for o in range(1, n_hi):
        pl.semaphore_signal(barrier, inc=1, device_id=hi_peer(o), device_id_type=MESH)
    for o in range(1, n_sec):
        pl.semaphore_signal(
            barrier, inc=1, device_id={"sec": lax.rem(sec + o, n_sec), "col": col},
            device_id_type=MESH,
        )

    slot_of_lane = lax.broadcasted_iota(jnp.int32, (1, lanes), 1)
    for k in range(blocks):
        found = jnp.full((1, lanes), noff, jnp.int32)
        for p in range(noff):
            dest = slot_ref[0, targets_ref[k, p]]
            found = jnp.where(slot_of_lane == dest, p, found)
        idx_vec[OWN, k:k + 1, :] = found
    to_scalar = pltpu.make_async_copy(idx_vec.at[OWN], idx_ref.at[OWN], in_sem.at[4])
    to_scalar.start()

    packs = (pack_own, pack_mirror)
    for pack_ref in packs:
        for q in range(pairs):
            pack_ref[q, noff] = jnp.zeros((width, 2 * width), jnp.bfloat16)
    for load in loads:
        load.wait()

    def pack(p, carry):
        for q in range(pairs):
            pack_own[q, p] = jnp.concatenate([off_ref[2 * q, p], off_ref[2 * q + 1, p]], axis=1)
        return carry

    lax.fori_loop(0, noff, pack, 0)
    to_scalar.wait()
    pl.semaphore_wait(barrier, n_lo - 1 + n_hi - 1 + n_sec - 1)

    def factor_copies():
        ends = [
            (idx_vec.at[OWN], idx_vec.at[MIRROR]),
            (diag_ref.at[OWN], diag_ref.at[MIRROR]),
            (rin.at[OTHER], rin.at[MIRROR]),
        ] + [
            (pack_own.at[q, pl.ds(0, noff)], pack_mirror.at[q, pl.ds(0, noff)])
            for q in range(pairs)
        ]
        return [
            pltpu.make_async_remote_copy(
                src_ref=src, dst_ref=dst, send_sem=fs_sem.at[n], recv_sem=fr_sem.at[n],
                device_id=mirror, device_id_type=MESH,
            )
            for n, (src, dst) in enumerate(ends)
        ]

    @pl.when(sec != 0)
    def _():
        for copy in factor_copies():
            copy.start()

    def mirror_factor():
        for copy in factor_copies():
            copy.wait_recv()
        to_scalar = pltpu.make_async_copy(idx_vec.at[MIRROR], idx_ref.at[MIRROR], in_sem.at[5])
        to_scalar.start()
        to_scalar.wait()

    def source(role):
        return lax.rem(role + plane, 2)

    left = lax.broadcasted_iota(jnp.int32, (width, 2 * width), 1) < width

    def build_row(role, src, i):
        pack_ref = packs[src]
        for q in range(pairs):
            a_ref[role, i, :, 2 * q * width:2 * (q + 1) * width] = jnp.where(
                left,
                pack_ref[q, idx_ref[src, 2 * q, i]],
                pack_ref[q, idx_ref[src, 2 * q + 1, i]],
            )

    def build_all(role):
        for src in (OWN, MIRROR):
            @pl.when(source(role) == src)
            def _():
                def step(i, carry):
                    build_row(role, src, i)
                    return carry

                lax.fori_loop(0, rows, step, 0)

    def copy1(j, o, oh):
        return pltpu.make_async_remote_copy(
            src_ref=send1.at[j, o - 1, oh], dst_ref=recv1.at[j, o - 1, oh],
            send_sem=s1_sem.at[j, o - 1, oh], recv_sem=r1_sem.at[j, o - 1, oh],
            device_id=lo_peer(o), device_id_type=MESH,
        )

    def copy2(j, oh):
        return pltpu.make_async_remote_copy(
            src_ref=send2.at[j, oh - 1], dst_ref=recv2.at[j, oh - 1],
            send_sem=s2_sem.at[j, oh - 1], recv_sem=r2_sem.at[j, oh - 1],
            device_id=hi_peer(oh), device_id_type=MESH,
        )

    def copyp(j, to_sec, slot):
        return pltpu.make_async_remote_copy(
            src_ref=passed.at[j], dst_ref=inc.at[slot],
            send_sem=sp_sem.at[j], recv_sem=rp_sem.at[slot],
            device_id={"sec": to_sec, "col": col}, device_id_type=MESH,
        )

    def pass_on(j):
        if j == 0:
            return copyp(0, half + 1, 0)
        more = place + 1 < half
        to_sec = plane * half + jnp.where(more, place + 1, 0)
        if j == 1:
            return copyp(1, to_sec, jnp.where(more, 0, 1))
        return copyp(2, to_sec, 1)

    def give_back(which, j):
        return pltpu.make_async_remote_copy(
            src_ref=(x_ref, passed)[which].at[j], dst_ref=ret.at[which],
            send_sem=sr_sem.at[which], recv_sem=rr_sem.at[which],
            device_id=mirror, device_id_type=MESH,
        )

    order = list(range(n_hi - 1, -1, -1))

    def product(j, oh, o):
        role = max(j - 1, 0)
        dest = hi_flip(oh) * n_lo + lax.rem(lo + o, n_lo)
        if j == 0:
            for r in range(blocks):
                build_row(0, OWN, dest * blocks + r)
        a = a_ref[role, pl.ds(dest * blocks, blocks)].reshape(size, size)
        return jnp.dot(a, x_ref[j], preferred_element_type=jnp.float32)

    def first(j, fresh):
        role = max(j - 1, 0)
        src = source(role)
        which = OTHER if j == 0 else src
        if not fresh:
            copyp(j, sec, role).wait_recv()
        for k in range(blocks):
            part = slice(k * width, (k + 1) * width)
            residual = rin[which, k]
            if not fresh:
                residual = (
                    residual.astype(jnp.float32) - inc[role, part, :].astype(jnp.float32)
                ).astype(jnp.bfloat16)
            x_ref[j, part, :] = jnp.dot(
                diag_ref[src, k], residual, preferred_element_type=jnp.float32
            ).astype(jnp.bfloat16)
        for oh in order:
            for o in range(1, n_lo):
                send1[j, o - 1, oh] = product(j, oh, o).astype(jnp.bfloat16)
                copy1(j, o, oh).start()

    def middle(j):
        for oh in order:
            total = product(j, oh, 0)
            for o in range(1, n_lo):
                copy1(j, o, oh).wait_recv()
                total = total + recv1[j, o - 1, oh].astype(jnp.float32)
            if oh == 0:
                acc[j] = total
            else:
                send2[j, oh - 1] = total.astype(jnp.bfloat16)
                copy2(j, oh).start()

    def last(j):
        total = acc[j]
        for oh in range(1, n_hi):
            copy2(j, oh).wait_recv()
            total = total + recv2[j, oh - 1].astype(jnp.float32)
        passed[j] = total.astype(jnp.bfloat16)
        if j < 2:
            pass_on(j).start()
        else:
            @pl.when(place < half - 1)
            def _():
                pass_on(j).start()

        if j > 0:
            @pl.when(source(j - 1) == MIRROR)
            def _():
                give_back(0, j).start()
                give_back(1, j).start()

    def sent(j):
        for oh in range(n_hi):
            for o in range(1, n_lo):
                copy1(j, o, oh).wait_send()
        for oh in range(1, n_hi):
            copy2(j, oh).wait_send()

    @pl.when(sec == 0)
    def _():
        first(0, True)
        middle(0)
        first(1, True)
        last(0)
        middle(1)
        last(1)
        sent(0)
        sent(1)
        pass_on(0).wait_send()
        pass_on(1).wait_send()

    @pl.when(place > 0)
    def _():
        @pl.when(plane == 1)
        def _():
            mirror_factor()

        build_all(0)
        first(1, False)
        middle(1)
        last(1)
        sent(1)
        pass_on(1).wait_send()

    @pl.when(plane == 0)
    def _():
        mirror_factor()

    build_all(1)
    first(2, False)
    middle(2)
    last(2)
    own = 1 + plane
    sol_ref[:, :, columns_of(plane)] = x_ref[own].reshape(blocks, width, nc)
    hand_ref[:, :, columns_of(plane)] = passed[own].reshape(blocks, width, nc)

    @pl.when(sec == 0)
    def _():
        sol_ref[:, :, nc:2 * nc] = x_ref[0].reshape(blocks, width, nc)
        hand_ref[:, :, nc:2 * nc] = passed[0].reshape(blocks, width, nc)

    @pl.when(sec != 0)
    def _():
        give_back(0, 1).wait_recv()
        sol_ref[:, :, columns_of(1 - plane)] = ret[0].reshape(blocks, width, nc)
        give_back(1, 1).wait_recv()
        hand_ref[:, :, columns_of(1 - plane)] = ret[1].reshape(blocks, width, nc)
        for copy in factor_copies():
            copy.wait_send()

    sent(2)

    @pl.when(place < half - 1)
    def _():
        pass_on(2).wait_send()

    @pl.when(sec != half)
    def _():
        give_back(0, 1).wait_send()
        give_back(1, 1).wait_send()


def mirrored(n_sec, n_col, rhs, diag_inv, off_tiles, targets, row_slot):
    blocks, width, columns = rhs.shape
    noff = off_tiles.shape[1]
    rows = row_slot.shape[1]
    n_lo = low_size(n_col)
    n_hi = n_col // n_lo
    nc = columns // 2
    size = blocks * width
    pairs = blocks // 2
    lanes = -(-rows // 128) * 128

    vmem = pl.BlockSpec(memory_space=pltpu.VMEM)
    smem = pl.BlockSpec(memory_space=pltpu.SMEM)
    hbm = pl.BlockSpec(memory_space=pl.ANY)
    out = jax.ShapeDtypeStruct((blocks, width, columns), jnp.bfloat16)
    dma = pltpu.SemaphoreType.DMA
    bf16 = jnp.bfloat16
    return pl.pallas_call(
        functools.partial(kernel, (n_sec, n_hi, n_lo)),
        out_shape=(out, out),
        in_specs=[smem, smem, hbm, hbm, hbm],
        out_specs=(vmem, vmem),
        scratch_shapes=[
            pltpu.VMEM((3, blocks, width, nc), bf16),
            pltpu.VMEM((2, blocks, width, width), bf16),
            pltpu.VMEM((blocks, noff, width, width), bf16),
            pltpu.VMEM((pairs, noff + 1, width, 2 * width), bf16),
            pltpu.VMEM((pairs, noff + 1, width, 2 * width), bf16),
            pltpu.VMEM((2, blocks, lanes), jnp.int32),
            pltpu.SMEM((2, blocks, lanes), jnp.int32),
            pltpu.VMEM((2, rows, width, size), bf16),
            pltpu.VMEM((3, size, nc), bf16),
            pltpu.VMEM((2, size, nc), bf16),
            pltpu.VMEM((3, n_lo - 1, n_hi, size, nc), bf16),
            pltpu.VMEM((3, n_lo - 1, n_hi, size, nc), bf16),
            pltpu.VMEM((3, n_hi - 1, size, nc), bf16),
            pltpu.VMEM((3, n_hi - 1, size, nc), bf16),
            pltpu.VMEM((3, size, nc), jnp.float32),
            pltpu.VMEM((3, size, nc), bf16),
            pltpu.VMEM((2, size, nc), bf16),
            dma((6,)),
            dma((3 + pairs,)),
            dma((3 + pairs,)),
            dma((3, n_lo - 1, n_hi)),
            dma((3, n_lo - 1, n_hi)),
            dma((3, n_hi - 1)),
            dma((3, n_hi - 1)),
            dma((3,)),
            dma((2,)),
            dma((2,)),
            dma((2,)),
        ],
        compiler_params=pltpu.CompilerParams(
            collective_id=0, has_side_effects=True, vmem_limit_bytes=60 * 1024 * 1024
        ),
    )(targets, row_slot, rhs, diag_inv, off_tiles)


def chains_kernel(
    dims, targets_ref, slot_ref, rhs_hbm, diag_hbm, off_hbm, sol_ref, hand_ref,
    rhs_ref, off_ref, pack_0, pack_1, pack_2, pack_3, diag_ref, idx_vec, idx_ref, rin, a_ref, w_ref,
    send1, recv1, send2, recv2, acc, xs, hs, ret,
    in_sem, fs_sem, fr_sem, rs_sem, rr_sem, s1_sem, r1_sem, s2_sem, r2_sem, p_sem, gs_sem, gr_sem,
):
    n_hi, n_lo = dims
    blocks, noff, width = off_hbm.shape[:3]
    lanes = idx_vec.shape[2]
    pairs = blocks // 2
    size = blocks * width
    packed = pairs * width
    wide = 2 * width
    sec = lax.axis_index("sec")
    col = lax.axis_index("col")
    plane, place = sec // 2, sec % 2
    hi, lo = col // n_lo, col % n_lo
    bf16, f32 = jnp.bfloat16, jnp.float32

    own_idx = pltpu.make_async_copy(idx_vec.at[sec], idx_ref.at[sec], in_sem.at[0])
    load_off = [
        pltpu.make_async_copy(
            off_hbm.at[pl.ds(2 * q, 2)], off_ref.at[pl.ds(2 * q, 2)], in_sem.at[3 + q]
        )
        for q in range(pairs)
    ]
    load_diag = pltpu.make_async_copy(diag_hbm, diag_ref.at[sec], in_sem.at[2])
    load_rhs = pltpu.make_async_copy(rhs_hbm, rhs_ref, in_sem.at[1])
    for load in (*load_off, load_diag, load_rhs):
        load.start()

    def hi_flip(o):
        value, bit = hi, 1
        while bit < n_hi:
            value = value + ((o // bit) % 2) * (bit - 2 * bit * ((value // bit) % 2))
            bit *= 2
        return value

    def at_sec(to):
        return {"sec": to, "col": col}

    lo_peer = {"sec": sec, "col": hi * n_lo + 1 - lo}

    def hi_peer(o):
        return {"sec": sec, "col": hi_flip(o) * n_lo + lo}

    barrier = pltpu.get_barrier_semaphore()
    peers = [lo_peer] + [hi_peer(o) for o in range(1, n_hi)]
    peers += [at_sec(lax.rem(sec + o, 4)) for o in range(1, 4)]
    for peer in peers:
        pl.semaphore_signal(barrier, inc=1, device_id=peer, device_id_type=MESH)

    slot_of_lane = lax.broadcasted_iota(jnp.int32, (1, lanes), 1)
    for k in range(blocks):
        found = jnp.full((1, lanes), noff, jnp.int32)
        for p in range(noff):
            dest = slot_ref[0, targets_ref[k, p]]
            found = jnp.where(slot_of_lane == dest, p, found)
        idx_vec[sec, k:k + 1, :] = found
    own_idx.start()
    packs = (pack_0, pack_1, pack_2, pack_3)
    for pack_ref in packs:
        for q in range(pairs):
            pack_ref[q, noff] = jnp.zeros((width, wide), bf16)

    left = lax.broadcasted_iota(jnp.int32, (width, wide), 1) < width

    def swap(x):
        return jnp.concatenate([x[:, width:], x[:, :width]], axis=1)

    def pack_into(pack_ref):
        for q in range(pairs):
            load_off[q].wait()

            def step(p, carry):
                pack_ref[q, p] = jnp.concatenate([off_ref[2 * q, p], off_ref[2 * q + 1, p]], axis=1)
                return carry

            lax.fori_loop(0, noff, step, 0, unroll=4)

    for s in range(4):
        @pl.when(sec == s)
        def _():
            pack_into(packs[s])

    load_diag.wait()
    load_rhs.wait()
    own_idx.wait()
    for m in range(2):
        part = slice(m * wide, (m + 1) * wide)
        for q in range(pairs):
            even, odd = rhs_ref[2 * q, :, part], rhs_ref[2 * q + 1, :, part]
            rows = slice(q * width, (q + 1) * width)
            rin[sec, 2 * m, rows] = jnp.where(left, even, swap(odd))
            rin[sec, 2 * m + 1, rows] = jnp.where(left, swap(even), odd)

    pl.semaphore_wait(barrier, len(peers))

    every = range(2 + pairs)
    def shares(s):
        cut = 3 if s == 1 else 2 + pairs // 2
        return range(cut), range(cut, 2 + pairs)


    def factor(s, to, step, pieces=every):
        ends = [idx_vec.at[s], diag_ref.at[s]]
        ends += [packs[s].at[q, pl.ds(0, noff)] for q in range(pairs)]
        return [
            pltpu.make_async_remote_copy(
                src_ref=ends[n], dst_ref=ends[n], send_sem=fs_sem.at[step, n], recv_sem=fr_sem.at[s, n],
                device_id=at_sec(to), device_id_type=MESH,
            )
            for n in pieces
        ]

    def start(copies):
        for copy in copies:
            copy.start()

    def wait_sent(copies):
        for copy in copies:
            copy.wait_send()

    def to_scalar_memory(s):
        to_scalar = pltpu.make_async_copy(idx_vec.at[s], idx_ref.at[s], in_sem.at[0])
        to_scalar.start()
        to_scalar.wait()

    def factor_here(s):
        for copy in factor(s, 0, 0):
            copy.wait_recv()
        to_scalar_memory(s)

    def by_core(act):
        for core in range(2):
            @pl.when(place == core)
            def _():
                act(core)

    def across(s, act):
        by_core(lambda core: act(factor(s, 2 - s // 2 * 2 + core, s, shares(s)[core])))

    def arrive(s):
        def step(core):
            onward = factor(s, s // 2 * -2 + 3 - core, s, shares(s)[core])
            for here_now, copy in zip(factor(s, 0, 0, shares(s)[core]), onward):
                here_now.wait_recv()
                copy.start()

        by_core(step)

    def relayed(s):
        by_core(lambda core: wait_sent(factor(s, 0, s, shares(s)[core])))

    def arrive_late(s):
        def step(core):
            for copy in factor(s, 0, 0, shares(s)[1 - core]):
                copy.wait_recv()

        by_core(step)
        to_scalar_memory(s)

    def chain_of(device):
        return 2 * (1 - device // 2) + device % 2

    mine = chain_of(sec)

    def rhs_copy(s, chain, to, step, slot):
        return pltpu.make_async_remote_copy(
            src_ref=rin.at[s, chain], dst_ref=rin.at[s, chain],
            send_sem=rs_sem.at[step], recv_sem=rr_sem.at[slot],
            device_id=at_sec(to), device_id_type=MESH,
        )

    def rhs_sends(s):
        if s == 0:
            return [rhs_copy(0, 1, 1, 0, 4), rhs_copy(0, 3, 1, 1, 0)]
        return [
            rhs_copy(s, 2 * (1 - to // 2) + to % 2, to, n, s)
            for n, to in enumerate(to for to in (s ^ 1, s ^ 2, s ^ 3))
        ]

    def rhs_here(s):
        rhs_copy(s, mine, 0, 0, s).wait_recv()

    other = plane * 2 + 1 - place
    for s in range(4):
        @pl.when(sec == s)
        def _():
            start(factor(s, s ^ 1, 0))

    for s in range(4):
        @pl.when(sec == s)
        def _():
            start(rhs_sends(s))

    def build(s, d):
        for r in range(blocks):
            i = d * blocks + r
            for q in range(pairs):
                at = (r % 2) * size + q * wide
                a_ref[s, d * pairs + r // 2, :, at:at + wide] = jnp.where(
                    left, packs[s][q, idx_ref[s, 2 * q, i]], packs[s][q, idx_ref[s, 2 * q + 1, i]]
                )

    def build_range(s, low, high):
        def step(d, carry):
            build(s, d)
            return carry

        lax.fori_loop(low, high, step, 0)

    def copy1(j, oh):
        return pltpu.make_async_remote_copy(
            src_ref=send1.at[j, oh], dst_ref=recv1.at[j, oh],
            send_sem=s1_sem.at[j, oh], recv_sem=r1_sem.at[j, oh],
            device_id=lo_peer, device_id_type=MESH,
        )

    def copy2(j, oh):
        return pltpu.make_async_remote_copy(
            src_ref=send2.at[j, oh - 1], dst_ref=recv2.at[j, oh - 1],
            send_sem=s2_sem.at[j, oh - 1], recv_sem=r2_sem.at[j, oh - 1],
            device_id=hi_peer(oh), device_id_type=MESH,
        )

    def give(which, j, s, chain):
        return pltpu.make_async_remote_copy(
            src_ref=(xs, hs)[which].at[j], dst_ref=ret.at[which, chain],
            send_sem=gs_sem.at[which, j], recv_sem=gr_sem.at[which, chain],
            device_id=at_sec(s), device_id_type=MESH,
        )

    def give_out(which, j, s, chain):
        @pl.when(sec == s)
        def _():
            ret[which, chain] = (xs, hs)[which][j]

        @pl.when(sec != s)
        def _():
            give(which, j, s, chain).start()

    def product(s, w, dest):
        a = a_ref[s, pl.ds(dest * pairs, pairs)].reshape(packed, 2 * size)
        return jnp.dot(a, w_ref[w], preferred_element_type=f32)

    def first(s, j, w, chain, h, fresh=None):
        for q in range(pairs):
            rows = slice(q * width, (q + 1) * width)
            residual = rin[s, chain, rows]
            if h is not None:
                residual = (residual.astype(f32) - h[rows].astype(f32)).astype(bf16)
            z = jnp.dot(
                diag_ref[s, 2 * q:2 * q + 2].reshape(wide, width), residual,
                preferred_element_type=f32,
            ).astype(bf16)
            top, low = z[:width], z[width:]
            xs[j, rows] = jnp.where(left, top, low)
            zero = jnp.zeros_like(top)
            at = q * wide
            w_ref[w, at:at + width] = jnp.where(left, top, zero)
            w_ref[w, at + width:at + wide] = jnp.where(left, swap(low), zero)
            w_ref[w, size + at:size + at + width] = jnp.where(left, zero, swap(top))
            w_ref[w, size + at + width:size + at + wide] = jnp.where(left, zero, low)

        def step(t, carry):
            oh = n_hi - 1 - t
            dest = hi_flip(oh) * n_lo + 1 - lo
            if fresh is not None:
                @pl.when(plane <= fresh)
                def _():
                    build(s, dest)

            send1[j, oh] = product(s, w, dest).astype(bf16)
            copy1(j, oh).start()
            return carry

        lax.fori_loop(0, n_hi, step, 0)
        give_out(0, j, s, chain)

    def middle(s, j, w, fresh=None, also=None):

        def step(t, carry):
            oh = n_hi - 1 - t
            dest = hi_flip(oh) * n_lo + lo
            if fresh is not None:
                @pl.when(plane <= fresh)
                def _():
                    build(s, dest)

            total = product(s, w, dest)
            copy1(j, oh).wait_recv()
            total = total + recv1[j, oh].astype(f32)

            @pl.when(oh > 0)
            def _():
                send2[j, oh - 1] = total.astype(bf16)
                copy2(j, oh).start()

            @pl.when(oh == 0)
            def _():
                acc[w] = total

            if also is not None:
                @pl.when(plane == 0)
                def _():
                    build(also, 2 * t)
                    build(also, 2 * t + 1)
            return carry

        lax.fori_loop(0, n_hi, step, 0)

    def last(j, w):
        total = acc[w]
        for oh in range(n_hi - 1, 0, -1):
            copy2(j, oh).wait_recv()
            total = total + recv2[j, oh - 1].astype(f32)
        hs[j] = total.astype(bf16)

    def sent(j, s):
        for oh in range(n_hi):
            copy1(j, oh).wait_send()
        for oh in range(1, n_hi):
            copy2(j, oh).wait_send()

        @pl.when(sec != s)
        def _():
            give(0, j, s, mine).wait_send()
            give(1, j, s, mine).wait_send()

    def pass_on():
        return pltpu.make_async_remote_copy(
            src_ref=hs.at[4], dst_ref=hs.at[0], send_sem=p_sem.at[0], recv_sem=p_sem.at[1],
            device_id=at_sec(2 + place), device_id_type=MESH,
        )

    def here(s):
        factor_here(s)
        if s > 0:
            rhs_here(s)

    @pl.when(plane == 0)
    def _():
        @pl.when(place == 0)
        def _():
            first(0, 0, 1, mine, None, fresh=1)
            first(0, 4, 0, place, None)
            here(1)
            across(1, start)
            middle(0, 0, 1, fresh=1)
            middle(0, 4, 0)
            last(0, 1)

        @pl.when(place == 1)
        def _():
            across(1, start)
            here(0)
            rhs_copy(0, 1, 0, 0, 4).wait_recv()
            rhs_copy(0, 3, 0, 0, 0).wait_recv()
            first(0, 4, 0, place, None, fresh=1)
            first(0, 0, 1, mine, None)
            middle(0, 4, 0, fresh=1)
            middle(0, 0, 1)
            last(4, 0)
            pass_on().start()
            give_out(1, 4, 0, place)
            last(0, 1)

    @pl.when(plane == 1)
    def _():
        @pl.when(place == 0)
        def _():
            across(2, start)
            here(3)

        @pl.when(place == 1)
        def _():
            here(2)
            across(2, start)

        build_range(2, 0, n_hi * n_lo)
        build_range(3, 0, n_hi * n_lo)
        arrive(1)
        arrive_late(1)
        rhs_here(1)
        across(2, wait_sent)
        across(3, start)
        pass_on().wait_recv()

    first(1, 1, 1, mine, hs.at[0], fresh=1)

    @pl.when(plane == 0)
    def _():
        @pl.when(place == 0)
        def _():
            last(4, 0)
            pass_on().start()
            give_out(1, 4, 0, place)

        give_out(1, 0, 0, mine)

    @pl.when((plane == 0) & (place == 1))
    def _():
        arrive(2)

    middle(1, 1, 1, fresh=1)

    @pl.when((plane == 0) & (place == 0))
    def _():
        arrive(2)

    last(1, 1)

    @pl.when(plane == 0)
    def _():
        arrive_late(2)
        rhs_here(2)

    first(2, 2, 1, mine, hs.at[1], fresh=0)
    give_out(1, 1, 1, mine)

    @pl.when((plane == 0) & (place == 1))
    def _():
        arrive(3)

    middle(2, 2, 1, fresh=0)

    @pl.when((plane == 0) & (place == 0))
    def _():
        arrive(3)

    last(2, 1)

    @pl.when(plane == 0)
    def _():
        arrive_late(3)
        rhs_here(3)

    def returned(which, chain):
        return pltpu.make_async_remote_copy(
            src_ref=xs.at[0], dst_ref=ret.at[which, chain],
            send_sem=gs_sem.at[which, 0], recv_sem=gr_sem.at[which, chain],
            device_id=at_sec(other), device_id_type=MESH,
        )

    def assemble(which, out):
        for m in range(2):
            returned(which, 2 * m + 1 - place).wait_recv()

            @pl.when((sec != 0) & (plane == m))
            def _():
                returned(which, 2 * m + place).wait_recv()

            part = slice(m * wide, (m + 1) * wide)
            for q in range(pairs):
                rows = slice(q * width, (q + 1) * width)
                one, two = ret[which, 2 * m, rows], ret[which, 2 * m + 1, rows]
                out[2 * q, :, part] = jnp.where(left, one, swap(two))
                out[2 * q + 1, :, part] = jnp.where(left, swap(one), two)

    first(3, 3, 1, mine, hs.at[2], fresh=0)
    give_out(1, 2, 2, mine)
    sent(1, 1)
    wait_sent(factor(0, other, 0))
    for s in range(4):
        @pl.when(sec == s)
        def _():
            wait_sent(rhs_sends(s))

    @pl.when(plane == 0)
    def _():
        sent(0, 0)
        for oh in range(n_hi):
            copy1(4, oh).wait_send()
        for oh in range(1, n_hi):
            copy2(4, oh).wait_send()

        @pl.when(sec != 0)
        def _():
            give(0, 4, 0, place).wait_send()
            give(1, 4, 0, place).wait_send()

        pass_on().wait_send()
        across(1, wait_sent)
        relayed(2)
        relayed(3)

    @pl.when(plane == 1)
    def _():
        across(3, wait_sent)
        relayed(1)

    middle(3, 3, 1, fresh=0)
    assemble(0, sol_ref)
    sent(2, 2)
    last(3, 1)
    give_out(1, 3, 3, mine)
    assemble(1, hand_ref)
    sent(3, 3)


def chains(n_col, rhs, diag_inv, off_tiles, targets, row_slot):
    blocks, width, columns = rhs.shape
    noff = off_tiles.shape[1]
    rows = row_slot.shape[1]
    n_lo = 2
    n_hi = n_col // n_lo
    size = blocks * width
    pairs = blocks // 2
    packed = pairs * width
    wide = 2 * width
    lanes = -(-rows // 128) * 128
    vmem = pl.BlockSpec(memory_space=pltpu.VMEM)
    smem = pl.BlockSpec(memory_space=pltpu.SMEM)
    hbm = pl.BlockSpec(memory_space=pl.ANY)
    out = jax.ShapeDtypeStruct((blocks, width, columns), jnp.bfloat16)
    dma = pltpu.SemaphoreType.DMA
    bf16 = jnp.bfloat16
    return pl.pallas_call(
        functools.partial(chains_kernel, (n_hi, n_lo)),
        out_shape=(out, out),
        in_specs=[smem, smem, hbm, hbm, hbm],
        out_specs=(vmem, vmem),
        scratch_shapes=[
            pltpu.VMEM((blocks, width, columns), bf16),
            pltpu.VMEM((blocks, noff, width, width), bf16),
            pltpu.VMEM((pairs, noff + 1, width, wide), bf16),
            pltpu.VMEM((pairs, noff + 1, width, wide), bf16),
            pltpu.VMEM((pairs, noff + 1, width, wide), bf16),
            pltpu.VMEM((pairs, noff + 1, width, wide), bf16),
            pltpu.VMEM((4, blocks, width, width), bf16),
            pltpu.VMEM((4, blocks, lanes), jnp.int32),
            pltpu.SMEM((4, blocks, lanes), jnp.int32),
            pltpu.VMEM((4, 4, packed, wide), bf16),
            pltpu.VMEM((4, rows // 2, width, 2 * size), bf16),
            pltpu.VMEM((2, 2 * size, wide), bf16),
            pltpu.VMEM((5, n_hi, packed, wide), bf16),
            pltpu.VMEM((5, n_hi, packed, wide), bf16),
            pltpu.VMEM((5, n_hi - 1, packed, wide), bf16),
            pltpu.VMEM((5, n_hi - 1, packed, wide), bf16),
            pltpu.VMEM((2, packed, wide), jnp.float32),
            pltpu.VMEM((5, packed, wide), bf16),
            pltpu.VMEM((5, packed, wide), bf16),
            pltpu.VMEM((2, 4, packed, wide), bf16),
            dma((3 + pairs,)),
            dma((4, 2 + pairs)),
            dma((4, 2 + pairs)),
            dma((3,)),
            dma((5,)),
            dma((5, n_hi)),
            dma((5, n_hi)),
            dma((5, n_hi - 1)),
            dma((5, n_hi - 1)),
            dma((2,)),
            dma((2, 5)),
            dma((2, 4)),
        ],
        compiler_params=pltpu.CompilerParams(
            collective_id=1, has_side_effects=True, vmem_limit_bytes=48 * 1024 * 1024
        ),
    )(*[pltpu.with_memory_space_constraint(x, pltpu.MemorySpace.HBM) for x in (targets, row_slot, rhs, diag_inv, off_tiles)])


def fits_chains(n_sec, n_col, rhs, row_slot):
    blocks, width, columns = rhs.shape
    n_hi = n_col // 2
    return (
        n_sec == 4 and n_col % 2 == 0 and n_hi & (n_hi - 1) == 0 and columns == 4 * width and width == 64
        and blocks % 2 == 0 and row_slot.shape[1] == blocks * n_col
    )


def shards(n_sec, n_col, rhs, diag_inv, off_tiles, targets, row_slot):
    if fits_chains(n_sec, n_col, rhs, row_slot):
        return chains(n_col, rhs, diag_inv, off_tiles, targets, row_slot)
    return mirrored(n_sec, n_col, rhs, diag_inv, off_tiles, targets, row_slot)


def solution(mesh):
    return jax.shard_map(
        functools.partial(shards, mesh.shape["sec"], mesh.shape["col"]),
        mesh=mesh,
        in_specs=(
            P(("sec", "col"), None, None),
            P(("sec", "col"), None, None),
            P(("sec", "col"), None, None, None),
            P(("sec", "col"), None),
            P("sec", None),
        ),
        out_specs=(P(("sec", "col"), None, None), P(("sec", "col"), None, None)),
        check_vma=False,
    )
```

```python
import functools

import jax
import jax.numpy as jnp
from jax import lax
from jax.experimental import pallas as pl
from jax.experimental.pallas import tpu as pltpu
from jax.sharding import PartitionSpec as P

MESH = pl.DeviceIdType.MESH
OWN, MIRROR, OTHER = 0, 1, 2


def low_size(n_col):
    low = 1
    while (2 * low) ** 2 <= n_col:
        low *= 2
    return low


def kernel(
    dims, targets_ref, slot_ref, rhs_hbm, diag_hbm, off_hbm, sol_ref, hand_ref,
    rin, diag_ref, off_ref, pack_own, pack_mirror, idx_vec, idx_ref,
    a_ref, x_ref, inc, send1, recv1, send2, recv2, acc, passed, ret,
    in_sem, fs_sem, fr_sem, s1_sem, r1_sem, s2_sem, r2_sem, sp_sem, rp_sem, sr_sem, rr_sem,
):
    n_sec, n_hi, n_lo = dims
    half = n_sec // 2
    blocks, width = off_hbm.shape[0], off_hbm.shape[2]
    noff = off_hbm.shape[1]
    rows = slot_ref.shape[1]
    lanes = idx_vec.shape[2]
    nc = rin.shape[3]
    size = blocks * width
    pairs = blocks // 2
    sec = lax.axis_index("sec")
    col = lax.axis_index("col")
    plane, place = sec // half, sec % half
    hi, lo = col // n_lo, col % n_lo
    mirror = {"sec": lax.rem(sec + half, n_sec), "col": col}

    def columns_of(which):
        return pl.ds(pl.multiple_of(which * nc, nc), nc)

    loads = [
        pltpu.make_async_copy(off_hbm, off_ref, in_sem.at[0]),
        pltpu.make_async_copy(diag_hbm, diag_ref.at[OWN], in_sem.at[1]),
        pltpu.make_async_copy(rhs_hbm.at[:, :, columns_of(plane)], rin.at[OWN], in_sem.at[2]),
        pltpu.make_async_copy(rhs_hbm.at[:, :, columns_of(1 - plane)], rin.at[OTHER], in_sem.at[3]),
    ]
    for load in loads:
        load.start()

    def lo_peer(o):
        return {"sec": sec, "col": hi * n_lo + lax.rem(lo + o, n_lo)}

    def hi_flip(o):
        value, bit = hi, 1
        while bit < n_hi:
            if o & bit:
                value = value + bit - 2 * bit * ((value // bit) % 2)
            bit *= 2
        return value

    def hi_peer(o):
        return {"sec": sec, "col": hi_flip(o) * n_lo + lo}

    barrier = pltpu.get_barrier_semaphore()
    for o in range(1, n_lo):
        pl.semaphore_signal(barrier, inc=1, device_id=lo_peer(o), device_id_type=MESH)
    for o in range(1, n_hi):
        pl.semaphore_signal(barrier, inc=1, device_id=hi_peer(o), device_id_type=MESH)
    for o in range(1, n_sec):
        pl.semaphore_signal(
            barrier, inc=1, device_id={"sec": lax.rem(sec + o, n_sec), "col": col},
            device_id_type=MESH,
        )

    slot_of_lane = lax.broadcasted_iota(jnp.int32, (1, lanes), 1)
    for k in range(blocks):
        found = jnp.full((1, lanes), noff, jnp.int32)
        for p in range(noff):
            dest = slot_ref[0, targets_ref[k, p]]
            found = jnp.where(slot_of_lane == dest, p, found)
        idx_vec[OWN, k:k + 1, :] = found
    to_scalar = pltpu.make_async_copy(idx_vec.at[OWN], idx_ref.at[OWN], in_sem.at[4])
    to_scalar.start()

    packs = (pack_own, pack_mirror)
    for pack_ref in packs:
        for q in range(pairs):
            pack_ref[q, noff] = jnp.zeros((width, 2 * width), jnp.bfloat16)
    for load in loads:
        load.wait()

    def pack(p, carry):
        for q in range(pairs):
            pack_own[q, p] = jnp.concatenate([off_ref[2 * q, p], off_ref[2 * q + 1, p]], axis=1)
        return carry

    lax.fori_loop(0, noff, pack, 0)
    to_scalar.wait()
    pl.semaphore_wait(barrier, n_lo - 1 + n_hi - 1 + n_sec - 1)

    def factor_copies():
        ends = [
            (idx_vec.at[OWN], idx_vec.at[MIRROR]),
            (diag_ref.at[OWN], diag_ref.at[MIRROR]),
            (rin.at[OTHER], rin.at[MIRROR]),
        ] + [
            (pack_own.at[q, pl.ds(0, noff)], pack_mirror.at[q, pl.ds(0, noff)])
            for q in range(pairs)
        ]
        return [
            pltpu.make_async_remote_copy(
                src_ref=src, dst_ref=dst, send_sem=fs_sem.at[n], recv_sem=fr_sem.at[n],
                device_id=mirror, device_id_type=MESH,
            )
            for n, (src, dst) in enumerate(ends)
        ]

    @pl.when(sec != 0)
    def _():
        for copy in factor_copies():
            copy.start()

    def mirror_factor():
        for copy in factor_copies():
            copy.wait_recv()
        to_scalar = pltpu.make_async_copy(idx_vec.at[MIRROR], idx_ref.at[MIRROR], in_sem.at[5])
        to_scalar.start()
        to_scalar.wait()

    def source(role):
        return lax.rem(role + plane, 2)

    left = lax.broadcasted_iota(jnp.int32, (width, 2 * width), 1) < width

    def build_row(role, src, i):
        pack_ref = packs[src]
        for q in range(pairs):
            a_ref[role, i, :, 2 * q * width:2 * (q + 1) * width] = jnp.where(
                left,
                pack_ref[q, idx_ref[src, 2 * q, i]],
                pack_ref[q, idx_ref[src, 2 * q + 1, i]],
            )

    def build_all(role):
        for src in (OWN, MIRROR):
            @pl.when(source(role) == src)
            def _():
                def step(i, carry):
                    build_row(role, src, i)
                    return carry

                lax.fori_loop(0, rows, step, 0)

    def copy1(j, o, oh):
        return pltpu.make_async_remote_copy(
            src_ref=send1.at[j, o - 1, oh], dst_ref=recv1.at[j, o - 1, oh],
            send_sem=s1_sem.at[j, o - 1, oh], recv_sem=r1_sem.at[j, o - 1, oh],
            device_id=lo_peer(o), device_id_type=MESH,
        )

    def copy2(j, oh):
        return pltpu.make_async_remote_copy(
            src_ref=send2.at[j, oh - 1], dst_ref=recv2.at[j, oh - 1],
            send_sem=s2_sem.at[j, oh - 1], recv_sem=r2_sem.at[j, oh - 1],
            device_id=hi_peer(oh), device_id_type=MESH,
        )

    def copyp(j, to_sec, slot):
        return pltpu.make_async_remote_copy(
            src_ref=passed.at[j], dst_ref=inc.at[slot],
            send_sem=sp_sem.at[j], recv_sem=rp_sem.at[slot],
            device_id={"sec": to_sec, "col": col}, device_id_type=MESH,
        )

    def pass_on(j):
        if j == 0:
            return copyp(0, half + 1, 0)
        more = place + 1 < half
        to_sec = plane * half + jnp.where(more, place + 1, 0)
        if j == 1:
            return copyp(1, to_sec, jnp.where(more, 0, 1))
        return copyp(2, to_sec, 1)

    def give_back(which, j):
        return pltpu.make_async_remote_copy(
            src_ref=(x_ref, passed)[which].at[j], dst_ref=ret.at[which],
            send_sem=sr_sem.at[which], recv_sem=rr_sem.at[which],
            device_id=mirror, device_id_type=MESH,
        )

    order = list(range(n_hi - 1, -1, -1))

    def product(j, oh, o):
        role = max(j - 1, 0)
        dest = hi_flip(oh) * n_lo + lax.rem(lo + o, n_lo)
        if j == 0:
            for r in range(blocks):
                build_row(0, OWN, dest * blocks + r)
        a = a_ref[role, pl.ds(dest * blocks, blocks)].reshape(size, size)
        return jnp.dot(a, x_ref[j], preferred_element_type=jnp.float32)

    def first(j, fresh):
        role = max(j - 1, 0)
        src = source(role)
        which = OTHER if j == 0 else src
        if not fresh:
            copyp(j, sec, role).wait_recv()
        for k in range(blocks):
            part = slice(k * width, (k + 1) * width)
            residual = rin[which, k]
            if not fresh:
                residual = (
                    residual.astype(jnp.float32) - inc[role, part, :].astype(jnp.float32)
                ).astype(jnp.bfloat16)
            x_ref[j, part, :] = jnp.dot(
                diag_ref[src, k], residual, preferred_element_type=jnp.float32
            ).astype(jnp.bfloat16)
        for oh in order:
            for o in range(1, n_lo):
                send1[j, o - 1, oh] = product(j, oh, o).astype(jnp.bfloat16)
                copy1(j, o, oh).start()

    def middle(j):
        for oh in order:
            total = product(j, oh, 0)
            for o in range(1, n_lo):
                copy1(j, o, oh).wait_recv()
                total = total + recv1[j, o - 1, oh].astype(jnp.float32)
            if oh == 0:
                acc[j] = total
            else:
                send2[j, oh - 1] = total.astype(jnp.bfloat16)
                copy2(j, oh).start()

    def last(j):
        total = acc[j]
        for oh in range(1, n_hi):
            copy2(j, oh).wait_recv()
            total = total + recv2[j, oh - 1].astype(jnp.float32)
        passed[j] = total.astype(jnp.bfloat16)
        if j < 2:
            pass_on(j).start()
        else:
            @pl.when(place < half - 1)
            def _():
                pass_on(j).start()

        if j > 0:
            @pl.when(source(j - 1) == MIRROR)
            def _():
                give_back(0, j).start()
                give_back(1, j).start()

    def sent(j):
        for oh in range(n_hi):
            for o in range(1, n_lo):
                copy1(j, o, oh).wait_send()
        for oh in range(1, n_hi):
            copy2(j, oh).wait_send()

    @pl.when(sec == 0)
    def _():
        first(0, True)
        middle(0)
        first(1, True)
        last(0)
        middle(1)
        last(1)
        sent(0)
        sent(1)
        pass_on(0).wait_send()
        pass_on(1).wait_send()

    @pl.when(place > 0)
    def _():
        @pl.when(plane == 1)
        def _():
            mirror_factor()

        build_all(0)
        first(1, False)
        middle(1)
        last(1)
        sent(1)
        pass_on(1).wait_send()

    @pl.when(plane == 0)
    def _():
        mirror_factor()

    build_all(1)
    first(2, False)
    middle(2)
    last(2)
    own = 1 + plane
    sol_ref[:, :, columns_of(plane)] = x_ref[own].reshape(blocks, width, nc)
    hand_ref[:, :, columns_of(plane)] = passed[own].reshape(blocks, width, nc)

    @pl.when(sec == 0)
    def _():
        sol_ref[:, :, nc:2 * nc] = x_ref[0].reshape(blocks, width, nc)
        hand_ref[:, :, nc:2 * nc] = passed[0].reshape(blocks, width, nc)

    @pl.when(sec != 0)
    def _():
        give_back(0, 1).wait_recv()
        sol_ref[:, :, columns_of(1 - plane)] = ret[0].reshape(blocks, width, nc)
        give_back(1, 1).wait_recv()
        hand_ref[:, :, columns_of(1 - plane)] = ret[1].reshape(blocks, width, nc)
        for copy in factor_copies():
            copy.wait_send()

    sent(2)

    @pl.when(place < half - 1)
    def _():
        pass_on(2).wait_send()

    @pl.when(sec != half)
    def _():
        give_back(0, 1).wait_send()
        give_back(1, 1).wait_send()


def mirrored(n_sec, n_col, rhs, diag_inv, off_tiles, targets, row_slot):
    blocks, width, columns = rhs.shape
    noff = off_tiles.shape[1]
    rows = row_slot.shape[1]
    n_lo = low_size(n_col)
    n_hi = n_col // n_lo
    nc = columns // 2
    size = blocks * width
    pairs = blocks // 2
    lanes = -(-rows // 128) * 128

    vmem = pl.BlockSpec(memory_space=pltpu.VMEM)
    smem = pl.BlockSpec(memory_space=pltpu.SMEM)
    hbm = pl.BlockSpec(memory_space=pl.ANY)
    out = jax.ShapeDtypeStruct((blocks, width, columns), jnp.bfloat16)
    dma = pltpu.SemaphoreType.DMA
    bf16 = jnp.bfloat16
    return pl.pallas_call(
        functools.partial(kernel, (n_sec, n_hi, n_lo)),
        out_shape=(out, out),
        in_specs=[smem, smem, hbm, hbm, hbm],
        out_specs=(vmem, vmem),
        scratch_shapes=[
            pltpu.VMEM((3, blocks, width, nc), bf16),
            pltpu.VMEM((2, blocks, width, width), bf16),
            pltpu.VMEM((blocks, noff, width, width), bf16),
            pltpu.VMEM((pairs, noff + 1, width, 2 * width), bf16),
            pltpu.VMEM((pairs, noff + 1, width, 2 * width), bf16),
            pltpu.VMEM((2, blocks, lanes), jnp.int32),
            pltpu.SMEM((2, blocks, lanes), jnp.int32),
            pltpu.VMEM((2, rows, width, size), bf16),
            pltpu.VMEM((3, size, nc), bf16),
            pltpu.VMEM((2, size, nc), bf16),
            pltpu.VMEM((3, n_lo - 1, n_hi, size, nc), bf16),
            pltpu.VMEM((3, n_lo - 1, n_hi, size, nc), bf16),
            pltpu.VMEM((3, n_hi - 1, size, nc), bf16),
            pltpu.VMEM((3, n_hi - 1, size, nc), bf16),
            pltpu.VMEM((3, size, nc), jnp.float32),
            pltpu.VMEM((3, size, nc), bf16),
            pltpu.VMEM((2, size, nc), bf16),
            dma((6,)),
            dma((3 + pairs,)),
            dma((3 + pairs,)),
            dma((3, n_lo - 1, n_hi)),
            dma((3, n_lo - 1, n_hi)),
            dma((3, n_hi - 1)),
            dma((3, n_hi - 1)),
            dma((3,)),
            dma((2,)),
            dma((2,)),
            dma((2,)),
        ],
        compiler_params=pltpu.CompilerParams(
            collective_id=0, has_side_effects=True, vmem_limit_bytes=60 * 1024 * 1024
        ),
    )(targets, row_slot, rhs, diag_inv, off_tiles)


def chains_kernel(
    dims, targets_ref, slot_ref, rhs_hbm, diag_hbm, off_hbm, sol_ref, hand_ref,
    rhs_ref, off_ref, pack_0, pack_1, pack_2, pack_3, diag_ref, idx_vec, idx_ref, rin, a_ref, w_ref,
    send1, recv1, send2, recv2, acc, xs, hs, ret,
    in_sem, fs_sem, fr_sem, rs_sem, rr_sem, s1_sem, r1_sem, s2_sem, r2_sem, p_sem, gs_sem, gr_sem,
):
    n_hi, n_lo = dims
    blocks, noff, width = off_hbm.shape[:3]
    lanes = idx_vec.shape[2]
    pairs = blocks // 2
    size = blocks * width
    packed = pairs * width
    wide = 2 * width
    sec = lax.axis_index("sec")
    col = lax.axis_index("col")
    plane, place = sec // 2, sec % 2
    hi, lo = col // n_lo, col % n_lo
    bf16, f32 = jnp.bfloat16, jnp.float32

    own_idx = pltpu.make_async_copy(idx_vec.at[sec], idx_ref.at[sec], in_sem.at[0])
    load_off = [
        pltpu.make_async_copy(
            off_hbm.at[pl.ds(2 * q, 2)], off_ref.at[pl.ds(2 * q, 2)], in_sem.at[3 + q]
        )
        for q in range(pairs)
    ]
    load_diag = pltpu.make_async_copy(diag_hbm, diag_ref.at[sec], in_sem.at[2])
    load_rhs = pltpu.make_async_copy(rhs_hbm, rhs_ref, in_sem.at[1])
    for load in (*load_off, load_diag, load_rhs):
        load.start()

    def hi_flip(o):
        value, bit = hi, 1
        while bit < n_hi:
            value = value + ((o // bit) % 2) * (bit - 2 * bit * ((value // bit) % 2))
            bit *= 2
        return value

    def at_sec(to):
        return {"sec": to, "col": col}

    lo_peer = {"sec": sec, "col": hi * n_lo + 1 - lo}

    def hi_peer(o):
        return {"sec": sec, "col": hi_flip(o) * n_lo + lo}

    barrier = pltpu.get_barrier_semaphore()
    peers = [lo_peer] + [hi_peer(o) for o in range(1, n_hi)]
    peers += [at_sec(lax.rem(sec + o, 4)) for o in range(1, 4)]
    for peer in peers:
        pl.semaphore_signal(barrier, inc=1, device_id=peer, device_id_type=MESH)

    slot_of_lane = lax.broadcasted_iota(jnp.int32, (1, lanes), 1)
    for k in range(blocks):
        found = jnp.full((1, lanes), noff, jnp.int32)
        for p in range(noff):
            dest = slot_ref[0, targets_ref[k, p]]
            found = jnp.where(slot_of_lane == dest, p, found)
        idx_vec[sec, k:k + 1, :] = found
    own_idx.start()
    packs = (pack_0, pack_1, pack_2, pack_3)
    for pack_ref in packs:
        for q in range(pairs):
            pack_ref[q, noff] = jnp.zeros((width, wide), bf16)

    left = lax.broadcasted_iota(jnp.int32, (width, wide), 1) < width

    def swap(x):
        return jnp.concatenate([x[:, width:], x[:, :width]], axis=1)

    def pack_into(pack_ref):
        for q in range(pairs):
            load_off[q].wait()

            def step(p, carry):
                pack_ref[q, p] = jnp.concatenate([off_ref[2 * q, p], off_ref[2 * q + 1, p]], axis=1)
                return carry

            lax.fori_loop(0, noff, step, 0, unroll=4)

    for s in range(4):
        @pl.when(sec == s)
        def _():
            pack_into(packs[s])

    load_diag.wait()
    load_rhs.wait()
    own_idx.wait()
    for m in range(2):
        part = slice(m * wide, (m + 1) * wide)
        for q in range(pairs):
            even, odd = rhs_ref[2 * q, :, part], rhs_ref[2 * q + 1, :, part]
            rows = slice(q * width, (q + 1) * width)
            rin[sec, 2 * m, rows] = jnp.where(left, even, swap(odd))
            rin[sec, 2 * m + 1, rows] = jnp.where(left, swap(even), odd)

    pl.semaphore_wait(barrier, len(peers))

    every = range(2 + pairs)
    def shares(s):
        cut = 3 if s == 1 else 2 + pairs // 2
        return range(cut), range(cut, 2 + pairs)


    def factor(s, to, step, pieces=every):
        ends = [idx_vec.at[s], diag_ref.at[s]]
        ends += [packs[s].at[q, pl.ds(0, noff)] for q in range(pairs)]
        return [
            pltpu.make_async_remote_copy(
                src_ref=ends[n], dst_ref=ends[n], send_sem=fs_sem.at[step, n], recv_sem=fr_sem.at[s, n],
                device_id=at_sec(to), device_id_type=MESH,
            )
            for n in pieces
        ]

    def start(copies):
        for copy in copies:
            copy.start()

    def wait_sent(copies):
        for copy in copies:
            copy.wait_send()

    def to_scalar_memory(s):
        to_scalar = pltpu.make_async_copy(idx_vec.at[s], idx_ref.at[s], in_sem.at[0])
        to_scalar.start()
        to_scalar.wait()

    def factor_here(s):
        for copy in factor(s, 0, 0):
            copy.wait_recv()
        to_scalar_memory(s)

    def by_core(act):
        for core in range(2):
            @pl.when(place == core)
            def _():
                act(core)

    def across(s, act):
        by_core(lambda core: act(factor(s, 2 - s // 2 * 2 + core, s, shares(s)[core])))

    def arrive(s):
        def step(core):
            onward = factor(s, s // 2 * -2 + 3 - core, s, shares(s)[core])
            for here_now, copy in zip(factor(s, 0, 0, shares(s)[core]), onward):
                here_now.wait_recv()
                copy.start()

        by_core(step)

    def relayed(s):
        by_core(lambda core: wait_sent(factor(s, 0, s, shares(s)[core])))

    def arrive_late(s):
        def step(core):
            for copy in factor(s, 0, 0, shares(s)[1 - core]):
                copy.wait_recv()

        by_core(step)
        to_scalar_memory(s)

    def chain_of(device):
        return 2 * (1 - device // 2) + device % 2

    mine = chain_of(sec)

    def rhs_copy(s, chain, to, step, slot):
        return pltpu.make_async_remote_copy(
            src_ref=rin.at[s, chain], dst_ref=rin.at[s, chain],
            send_sem=rs_sem.at[step], recv_sem=rr_sem.at[slot],
            device_id=at_sec(to), device_id_type=MESH,
        )

    def rhs_sends(s):
        if s == 0:
            return [rhs_copy(0, 1, 1, 0, 4), rhs_copy(0, 3, 1, 1, 0)]
        return [
            rhs_copy(s, 2 * (1 - to // 2) + to % 2, to, n, s)
            for n, to in enumerate(to for to in (s ^ 1, s ^ 2, s ^ 3))
        ]

    def rhs_here(s):
        rhs_copy(s, mine, 0, 0, s).wait_recv()

    other = plane * 2 + 1 - place
    for s in range(4):
        @pl.when(sec == s)
        def _():
            start(factor(s, s ^ 1, 0))

    for s in range(4):
        @pl.when(sec == s)
        def _():
            start(rhs_sends(s))

    def build(s, d):
        for r in range(blocks):
            i = d * blocks + r
            for q in range(pairs):
                at = (r % 2) * size + q * wide
                a_ref[s, d * pairs + r // 2, :, at:at + wide] = jnp.where(
                    left, packs[s][q, idx_ref[s, 2 * q, i]], packs[s][q, idx_ref[s, 2 * q + 1, i]]
                )

    def build_range(s, low, high):
        def step(d, carry):
            build(s, d)
            return carry

        lax.fori_loop(low, high, step, 0)

    def copy1(j, oh):
        return pltpu.make_async_remote_copy(
            src_ref=send1.at[j, oh], dst_ref=recv1.at[j, oh],
            send_sem=s1_sem.at[j, oh], recv_sem=r1_sem.at[j, oh],
            device_id=lo_peer, device_id_type=MESH,
        )

    def copy2(j, oh):
        return pltpu.make_async_remote_copy(
            src_ref=send2.at[j, oh - 1], dst_ref=recv2.at[j, oh - 1],
            send_sem=s2_sem.at[j, oh - 1], recv_sem=r2_sem.at[j, oh - 1],
            device_id=hi_peer(oh), device_id_type=MESH,
        )

    def give(which, j, s, chain):
        return pltpu.make_async_remote_copy(
            src_ref=(xs, hs)[which].at[j], dst_ref=ret.at[which, chain],
            send_sem=gs_sem.at[which, j], recv_sem=gr_sem.at[which, chain],
            device_id=at_sec(s), device_id_type=MESH,
        )

    def give_out(which, j, s, chain):
        @pl.when(sec == s)
        def _():
            ret[which, chain] = (xs, hs)[which][j]

        @pl.when(sec != s)
        def _():
            give(which, j, s, chain).start()

    def product(s, w, dest):
        a = a_ref[s, pl.ds(dest * pairs, pairs)].reshape(packed, 2 * size)
        return jnp.dot(a, w_ref[w], preferred_element_type=f32)

    def first(s, j, w, chain, h, fresh=None):
        for q in range(pairs):
            rows = slice(q * width, (q + 1) * width)
            residual = rin[s, chain, rows]
            if h is not None:
                residual = (residual.astype(f32) - h[rows].astype(f32)).astype(bf16)
            z = jnp.dot(
                diag_ref[s, 2 * q:2 * q + 2].reshape(wide, width), residual,
                preferred_element_type=f32,
            ).astype(bf16)
            top, low = z[:width], z[width:]
            xs[j, rows] = jnp.where(left, top, low)
            zero = jnp.zeros_like(top)
            at = q * wide
            w_ref[w, at:at + width] = jnp.where(left, top, zero)
            w_ref[w, at + width:at + wide] = jnp.where(left, swap(low), zero)
            w_ref[w, size + at:size + at + width] = jnp.where(left, zero, swap(top))
            w_ref[w, size + at + width:size + at + wide] = jnp.where(left, zero, low)

        def step(t, carry):
            oh = n_hi - 1 - t
            dest = hi_flip(oh) * n_lo + 1 - lo
            if fresh is not None:
                @pl.when(plane <= fresh)
                def _():
                    build(s, dest)

            send1[j, oh] = product(s, w, dest).astype(bf16)
            copy1(j, oh).start()
            return carry

        lax.fori_loop(0, n_hi, step, 0, unroll=True)
        give_out(0, j, s, chain)

    def middle(s, j, w, fresh=None, also=None):

        def step(t, carry):
            oh = n_hi - 1 - t
            dest = hi_flip(oh) * n_lo + lo
            if fresh is not None:
                @pl.when(plane <= fresh)
                def _():
                    build(s, dest)

            total = product(s, w, dest)
            copy1(j, oh).wait_recv()
            total = total + recv1[j, oh].astype(f32)

            @pl.when(oh > 0)
            def _():
                send2[j, oh - 1] = total.astype(bf16)
                copy2(j, oh).start()

            @pl.when(oh == 0)
            def _():
                acc[w] = total

            if also is not None:
                @pl.when(plane == 0)
                def _():
                    build(also, 2 * t)
                    build(also, 2 * t + 1)
            return carry

        lax.fori_loop(0, n_hi, step, 0, unroll=True)

    def last(j, w):
        total = acc[w]
        for oh in range(n_hi - 1, 0, -1):
            copy2(j, oh).wait_recv()
            total = total + recv2[j, oh - 1].astype(f32)
        hs[j] = total.astype(bf16)

    def sent(j, s):
        for oh in range(n_hi):
            copy1(j, oh).wait_send()
        for oh in range(1, n_hi):
            copy2(j, oh).wait_send()

        @pl.when(sec != s)
        def _():
            give(0, j, s, mine).wait_send()
            give(1, j, s, mine).wait_send()

    def pass_on():
        return pltpu.make_async_remote_copy(
            src_ref=hs.at[4], dst_ref=hs.at[0], send_sem=p_sem.at[0], recv_sem=p_sem.at[1],
            device_id=at_sec(2 + place), device_id_type=MESH,
        )

    def here(s):
        factor_here(s)
        if s > 0:
            rhs_here(s)

    @pl.when(plane == 0)
    def _():
        @pl.when(place == 0)
        def _():
            first(0, 0, 1, mine, None, fresh=1)
            first(0, 4, 0, place, None)
            here(1)
            across(1, start)
            middle(0, 0, 1, fresh=1)
            middle(0, 4, 0)
            last(0, 1)

        @pl.when(place == 1)
        def _():
            across(1, start)
            here(0)
            rhs_copy(0, 1, 0, 0, 4).wait_recv()
            rhs_copy(0, 3, 0, 0, 0).wait_recv()
            first(0, 4, 0, place, None, fresh=1)
            first(0, 0, 1, mine, None)
            middle(0, 4, 0, fresh=1)
            middle(0, 0, 1)
            last(4, 0)
            pass_on().start()
            give_out(1, 4, 0, place)
            last(0, 1)

    @pl.when(plane == 1)
    def _():
        @pl.when(place == 0)
        def _():
            across(2, start)
            here(3)

        @pl.when(place == 1)
        def _():
            here(2)
            across(2, start)

        build_range(2, 0, n_hi * n_lo)
        build_range(3, 0, n_hi * n_lo)
        arrive(1)
        arrive_late(1)
        rhs_here(1)
        across(3, start)
        pass_on().wait_recv()

    first(1, 1, 1, mine, hs.at[0], fresh=1)

    @pl.when(plane == 0)
    def _():
        @pl.when(place == 0)
        def _():
            last(4, 0)
            pass_on().start()
            give_out(1, 4, 0, place)

        give_out(1, 0, 0, mine)

    @pl.when((plane == 0) & (place == 1))
    def _():
        arrive(2)

    middle(1, 1, 1, fresh=1)

    @pl.when((plane == 0) & (place == 0))
    def _():
        arrive(2)

    last(1, 1)

    @pl.when(plane == 0)
    def _():
        arrive_late(2)
        rhs_here(2)

    first(2, 2, 1, mine, hs.at[1], fresh=0)
    give_out(1, 1, 1, mine)

    @pl.when((plane == 0) & (place == 1))
    def _():
        arrive(3)

    middle(2, 2, 1, fresh=0)

    @pl.when((plane == 0) & (place == 0))
    def _():
        arrive(3)

    last(2, 1)

    @pl.when(plane == 0)
    def _():
        arrive_late(3)
        rhs_here(3)

    def returned(which, chain):
        return pltpu.make_async_remote_copy(
            src_ref=xs.at[0], dst_ref=ret.at[which, chain],
            send_sem=gs_sem.at[which, 0], recv_sem=gr_sem.at[which, chain],
            device_id=at_sec(other), device_id_type=MESH,
        )

    def assemble(which, out):
        for m in range(2):
            returned(which, 2 * m + 1 - place).wait_recv()

            @pl.when((sec != 0) & (plane == m))
            def _():
                returned(which, 2 * m + place).wait_recv()

            part = slice(m * wide, (m + 1) * wide)
            for q in range(pairs):
                rows = slice(q * width, (q + 1) * width)
                one, two = ret[which, 2 * m, rows], ret[which, 2 * m + 1, rows]
                out[2 * q, :, part] = jnp.where(left, one, swap(two))
                out[2 * q + 1, :, part] = jnp.where(left, swap(one), two)

    first(3, 3, 1, mine, hs.at[2], fresh=0)
    give_out(1, 2, 2, mine)
    sent(1, 1)
    wait_sent(factor(0, other, 0))
    for s in range(4):
        @pl.when(sec == s)
        def _():
            wait_sent(rhs_sends(s))

    @pl.when(plane == 0)
    def _():
        sent(0, 0)
        for oh in range(n_hi):
            copy1(4, oh).wait_send()
        for oh in range(1, n_hi):
            copy2(4, oh).wait_send()

        @pl.when(sec != 0)
        def _():
            give(0, 4, 0, place).wait_send()
            give(1, 4, 0, place).wait_send()

        pass_on().wait_send()
        across(1, wait_sent)
        relayed(2)
        relayed(3)

    @pl.when(plane == 1)
    def _():
        across(2, wait_sent)
        across(3, wait_sent)
        relayed(1)

    middle(3, 3, 1, fresh=0)
    assemble(0, sol_ref)
    sent(2, 2)
    last(3, 1)
    give_out(1, 3, 3, mine)
    assemble(1, hand_ref)
    sent(3, 3)


def chains(n_col, rhs, diag_inv, off_tiles, targets, row_slot):
    blocks, width, columns = rhs.shape
    noff = off_tiles.shape[1]
    rows = row_slot.shape[1]
    n_lo = 2
    n_hi = n_col // n_lo
    size = blocks * width
    pairs = blocks // 2
    packed = pairs * width
    wide = 2 * width
    lanes = -(-rows // 128) * 128
    vmem = pl.BlockSpec(memory_space=pltpu.VMEM)
    smem = pl.BlockSpec(memory_space=pltpu.SMEM)
    hbm = pl.BlockSpec(memory_space=pl.ANY)
    out = jax.ShapeDtypeStruct((blocks, width, columns), jnp.bfloat16)
    dma = pltpu.SemaphoreType.DMA
    bf16 = jnp.bfloat16
    return pl.pallas_call(
        functools.partial(chains_kernel, (n_hi, n_lo)),
        out_shape=(out, out),
        in_specs=[smem, smem, hbm, hbm, hbm],
        out_specs=(vmem, vmem),
        scratch_shapes=[
            pltpu.VMEM((blocks, width, columns), bf16),
            pltpu.VMEM((blocks, noff, width, width), bf16),
            pltpu.VMEM((pairs, noff + 1, width, wide), bf16),
            pltpu.VMEM((pairs, noff + 1, width, wide), bf16),
            pltpu.VMEM((pairs, noff + 1, width, wide), bf16),
            pltpu.VMEM((pairs, noff + 1, width, wide), bf16),
            pltpu.VMEM((4, blocks, width, width), bf16),
            pltpu.VMEM((4, blocks, lanes), jnp.int32),
            pltpu.SMEM((4, blocks, lanes), jnp.int32),
            pltpu.VMEM((4, 4, packed, wide), bf16),
            pltpu.VMEM((4, rows // 2, width, 2 * size), bf16),
            pltpu.VMEM((2, 2 * size, wide), bf16),
            pltpu.VMEM((5, n_hi, packed, wide), bf16),
            pltpu.VMEM((5, n_hi, packed, wide), bf16),
            pltpu.VMEM((5, n_hi - 1, packed, wide), bf16),
            pltpu.VMEM((5, n_hi - 1, packed, wide), bf16),
            pltpu.VMEM((2, packed, wide), jnp.float32),
            pltpu.VMEM((5, packed, wide), bf16),
            pltpu.VMEM((5, packed, wide), bf16),
            pltpu.VMEM((2, 4, packed, wide), bf16),
            dma((3 + pairs,)),
            dma((4, 2 + pairs)),
            dma((4, 2 + pairs)),
            dma((3,)),
            dma((5,)),
            dma((5, n_hi)),
            dma((5, n_hi)),
            dma((5, n_hi - 1)),
            dma((5, n_hi - 1)),
            dma((2,)),
            dma((2, 5)),
            dma((2, 4)),
        ],
        compiler_params=pltpu.CompilerParams(
            collective_id=1, has_side_effects=True, vmem_limit_bytes=48 * 1024 * 1024
        ),
    )(*[pltpu.with_memory_space_constraint(x, pltpu.MemorySpace.HBM) for x in (targets, row_slot, rhs, diag_inv, off_tiles)])


def fits_chains(n_sec, n_col, rhs, row_slot):
    blocks, width, columns = rhs.shape
    n_hi = n_col // 2
    return (
        n_sec == 4 and n_col % 2 == 0 and n_hi & (n_hi - 1) == 0 and columns == 4 * width and width == 64
        and blocks % 2 == 0 and row_slot.shape[1] == blocks * n_col
    )


def shards(n_sec, n_col, rhs, diag_inv, off_tiles, targets, row_slot):
    if fits_chains(n_sec, n_col, rhs, row_slot):
        return chains(n_col, rhs, diag_inv, off_tiles, targets, row_slot)
    return mirrored(n_sec, n_col, rhs, diag_inv, off_tiles, targets, row_slot)


def solution(mesh):
    return jax.shard_map(
        functools.partial(shards, mesh.shape["sec"], mesh.shape["col"]),
        mesh=mesh,
        in_specs=(
            P(("sec", "col"), None, None),
            P(("sec", "col"), None, None),
            P(("sec", "col"), None, None, None),
            P(("sec", "col"), None),
            P("sec", None),
        ),
        out_specs=(P(("sec", "col"), None, None), P(("sec", "col"), None, None)),
        check_vma=False,
    )
```

```python
import functools

import jax
import jax.numpy as jnp
from jax import lax
from jax.experimental import pallas as pl
from jax.experimental.pallas import tpu as pltpu
from jax.sharding import PartitionSpec as P

MESH = pl.DeviceIdType.MESH
OWN, MIRROR, OTHER = 0, 1, 2


def low_size(n_col):
    low = 1
    while (2 * low) ** 2 <= n_col:
        low *= 2
    return low


def kernel(
    dims, targets_ref, slot_ref, rhs_hbm, diag_hbm, off_hbm, sol_ref, hand_ref,
    rin, diag_ref, off_ref, pack_own, pack_mirror, idx_vec, idx_ref,
    a_ref, x_ref, inc, send1, recv1, send2, recv2, acc, passed, ret,
    in_sem, fs_sem, fr_sem, s1_sem, r1_sem, s2_sem, r2_sem, sp_sem, rp_sem, sr_sem, rr_sem,
):
    n_sec, n_hi, n_lo = dims
    half = n_sec // 2
    blocks, width = off_hbm.shape[0], off_hbm.shape[2]
    noff = off_hbm.shape[1]
    rows = slot_ref.shape[1]
    lanes = idx_vec.shape[2]
    nc = rin.shape[3]
    size = blocks * width
    pairs = blocks // 2
    sec = lax.axis_index("sec")
    col = lax.axis_index("col")
    plane, place = sec // half, sec % half
    hi, lo = col // n_lo, col % n_lo
    mirror = {"sec": lax.rem(sec + half, n_sec), "col": col}

    def columns_of(which):
        return pl.ds(pl.multiple_of(which * nc, nc), nc)

    loads = [
        pltpu.make_async_copy(off_hbm, off_ref, in_sem.at[0]),
        pltpu.make_async_copy(diag_hbm, diag_ref.at[OWN], in_sem.at[1]),
        pltpu.make_async_copy(rhs_hbm.at[:, :, columns_of(plane)], rin.at[OWN], in_sem.at[2]),
        pltpu.make_async_copy(rhs_hbm.at[:, :, columns_of(1 - plane)], rin.at[OTHER], in_sem.at[3]),
    ]
    for load in loads:
        load.start()

    def lo_peer(o):
        return {"sec": sec, "col": hi * n_lo + lax.rem(lo + o, n_lo)}

    def hi_flip(o):
        value, bit = hi, 1
        while bit < n_hi:
            if o & bit:
                value = value + bit - 2 * bit * ((value // bit) % 2)
            bit *= 2
        return value

    def hi_peer(o):
        return {"sec": sec, "col": hi_flip(o) * n_lo + lo}

    barrier = pltpu.get_barrier_semaphore()
    for o in range(1, n_lo):
        pl.semaphore_signal(barrier, inc=1, device_id=lo_peer(o), device_id_type=MESH)
    for o in range(1, n_hi):
        pl.semaphore_signal(barrier, inc=1, device_id=hi_peer(o), device_id_type=MESH)
    for o in range(1, n_sec):
        pl.semaphore_signal(
            barrier, inc=1, device_id={"sec": lax.rem(sec + o, n_sec), "col": col},
            device_id_type=MESH,
        )

    slot_of_lane = lax.broadcasted_iota(jnp.int32, (1, lanes), 1)
    for k in range(blocks):
        found = jnp.full((1, lanes), noff, jnp.int32)
        for p in range(noff):
            dest = slot_ref[0, targets_ref[k, p]]
            found = jnp.where(slot_of_lane == dest, p, found)
        idx_vec[OWN, k:k + 1, :] = found
    to_scalar = pltpu.make_async_copy(idx_vec.at[OWN], idx_ref.at[OWN], in_sem.at[4])
    to_scalar.start()

    packs = (pack_own, pack_mirror)
    for pack_ref in packs:
        for q in range(pairs):
            pack_ref[q, noff] = jnp.zeros((width, 2 * width), jnp.bfloat16)
    for load in loads:
        load.wait()

    def pack(p, carry):
        for q in range(pairs):
            pack_own[q, p] = jnp.concatenate([off_ref[2 * q, p], off_ref[2 * q + 1, p]], axis=1)
        return carry

    lax.fori_loop(0, noff, pack, 0)
    to_scalar.wait()
    pl.semaphore_wait(barrier, n_lo - 1 + n_hi - 1 + n_sec - 1)

    def factor_copies():
        ends = [
            (idx_vec.at[OWN], idx_vec.at[MIRROR]),
            (diag_ref.at[OWN], diag_ref.at[MIRROR]),
            (rin.at[OTHER], rin.at[MIRROR]),
        ] + [
            (pack_own.at[q, pl.ds(0, noff)], pack_mirror.at[q, pl.ds(0, noff)])
            for q in range(pairs)
        ]
        return [
            pltpu.make_async_remote_copy(
                src_ref=src, dst_ref=dst, send_sem=fs_sem.at[n], recv_sem=fr_sem.at[n],
                device_id=mirror, device_id_type=MESH,
            )
            for n, (src, dst) in enumerate(ends)
        ]

    @pl.when(sec != 0)
    def _():
        for copy in factor_copies():
            copy.start()

    def mirror_factor():
        for copy in factor_copies():
            copy.wait_recv()
        to_scalar = pltpu.make_async_copy(idx_vec.at[MIRROR], idx_ref.at[MIRROR], in_sem.at[5])
        to_scalar.start()
        to_scalar.wait()

    def source(role):
        return lax.rem(role + plane, 2)

    left = lax.broadcasted_iota(jnp.int32, (width, 2 * width), 1) < width

    def build_row(role, src, i):
        pack_ref = packs[src]
        for q in range(pairs):
            a_ref[role, i, :, 2 * q * width:2 * (q + 1) * width] = jnp.where(
                left,
                pack_ref[q, idx_ref[src, 2 * q, i]],
                pack_ref[q, idx_ref[src, 2 * q + 1, i]],
            )

    def build_all(role):
        for src in (OWN, MIRROR):
            @pl.when(source(role) == src)
            def _():
                def step(i, carry):
                    build_row(role, src, i)
                    return carry

                lax.fori_loop(0, rows, step, 0)

    def copy1(j, o, oh):
        return pltpu.make_async_remote_copy(
            src_ref=send1.at[j, o - 1, oh], dst_ref=recv1.at[j, o - 1, oh],
            send_sem=s1_sem.at[j, o - 1, oh], recv_sem=r1_sem.at[j, o - 1, oh],
            device_id=lo_peer(o), device_id_type=MESH,
        )

    def copy2(j, oh):
        return pltpu.make_async_remote_copy(
            src_ref=send2.at[j, oh - 1], dst_ref=recv2.at[j, oh - 1],
            send_sem=s2_sem.at[j, oh - 1], recv_sem=r2_sem.at[j, oh - 1],
            device_id=hi_peer(oh), device_id_type=MESH,
        )

    def copyp(j, to_sec, slot):
        return pltpu.make_async_remote_copy(
            src_ref=passed.at[j], dst_ref=inc.at[slot],
            send_sem=sp_sem.at[j], recv_sem=rp_sem.at[slot],
            device_id={"sec": to_sec, "col": col}, device_id_type=MESH,
        )

    def pass_on(j):
        if j == 0:
            return copyp(0, half + 1, 0)
        more = place + 1 < half
        to_sec = plane * half + jnp.where(more, place + 1, 0)
        if j == 1:
            return copyp(1, to_sec, jnp.where(more, 0, 1))
        return copyp(2, to_sec, 1)

    def give_back(which, j):
        return pltpu.make_async_remote_copy(
            src_ref=(x_ref, passed)[which].at[j], dst_ref=ret.at[which],
            send_sem=sr_sem.at[which], recv_sem=rr_sem.at[which],
            device_id=mirror, device_id_type=MESH,
        )

    order = list(range(n_hi - 1, -1, -1))

    def product(j, oh, o):
        role = max(j - 1, 0)
        dest = hi_flip(oh) * n_lo + lax.rem(lo + o, n_lo)
        if j == 0:
            for r in range(blocks):
                build_row(0, OWN, dest * blocks + r)
        a = a_ref[role, pl.ds(dest * blocks, blocks)].reshape(size, size)
        return jnp.dot(a, x_ref[j], preferred_element_type=jnp.float32)

    def first(j, fresh):
        role = max(j - 1, 0)
        src = source(role)
        which = OTHER if j == 0 else src
        if not fresh:
            copyp(j, sec, role).wait_recv()
        for k in range(blocks):
            part = slice(k * width, (k + 1) * width)
            residual = rin[which, k]
            if not fresh:
                residual = (
                    residual.astype(jnp.float32) - inc[role, part, :].astype(jnp.float32)
                ).astype(jnp.bfloat16)
            x_ref[j, part, :] = jnp.dot(
                diag_ref[src, k], residual, preferred_element_type=jnp.float32
            ).astype(jnp.bfloat16)
        for oh in order:
            for o in range(1, n_lo):
                send1[j, o - 1, oh] = product(j, oh, o).astype(jnp.bfloat16)
                copy1(j, o, oh).start()

    def middle(j):
        for oh in order:
            total = product(j, oh, 0)
            for o in range(1, n_lo):
                copy1(j, o, oh).wait_recv()
                total = total + recv1[j, o - 1, oh].astype(jnp.float32)
            if oh == 0:
                acc[j] = total
            else:
                send2[j, oh - 1] = total.astype(jnp.bfloat16)
                copy2(j, oh).start()

    def last(j):
        total = acc[j]
        for oh in range(1, n_hi):
            copy2(j, oh).wait_recv()
            total = total + recv2[j, oh - 1].astype(jnp.float32)
        passed[j] = total.astype(jnp.bfloat16)
        if j < 2:
            pass_on(j).start()
        else:
            @pl.when(place < half - 1)
            def _():
                pass_on(j).start()

        if j > 0:
            @pl.when(source(j - 1) == MIRROR)
            def _():
                give_back(0, j).start()
                give_back(1, j).start()

    def sent(j):
        for oh in range(n_hi):
            for o in range(1, n_lo):
                copy1(j, o, oh).wait_send()
        for oh in range(1, n_hi):
            copy2(j, oh).wait_send()

    @pl.when(sec == 0)
    def _():
        first(0, True)
        middle(0)
        first(1, True)
        last(0)
        middle(1)
        last(1)
        sent(0)
        sent(1)
        pass_on(0).wait_send()
        pass_on(1).wait_send()

    @pl.when(place > 0)
    def _():
        @pl.when(plane == 1)
        def _():
            mirror_factor()

        build_all(0)
        first(1, False)
        middle(1)
        last(1)
        sent(1)
        pass_on(1).wait_send()

    @pl.when(plane == 0)
    def _():
        mirror_factor()

    build_all(1)
    first(2, False)
    middle(2)
    last(2)
    own = 1 + plane
    sol_ref[:, :, columns_of(plane)] = x_ref[own].reshape(blocks, width, nc)
    hand_ref[:, :, columns_of(plane)] = passed[own].reshape(blocks, width, nc)

    @pl.when(sec == 0)
    def _():
        sol_ref[:, :, nc:2 * nc] = x_ref[0].reshape(blocks, width, nc)
        hand_ref[:, :, nc:2 * nc] = passed[0].reshape(blocks, width, nc)

    @pl.when(sec != 0)
    def _():
        give_back(0, 1).wait_recv()
        sol_ref[:, :, columns_of(1 - plane)] = ret[0].reshape(blocks, width, nc)
        give_back(1, 1).wait_recv()
        hand_ref[:, :, columns_of(1 - plane)] = ret[1].reshape(blocks, width, nc)
        for copy in factor_copies():
            copy.wait_send()

    sent(2)

    @pl.when(place < half - 1)
    def _():
        pass_on(2).wait_send()

    @pl.when(sec != half)
    def _():
        give_back(0, 1).wait_send()
        give_back(1, 1).wait_send()


def mirrored(n_sec, n_col, rhs, diag_inv, off_tiles, targets, row_slot):
    blocks, width, columns = rhs.shape
    noff = off_tiles.shape[1]
    rows = row_slot.shape[1]
    n_lo = low_size(n_col)
    n_hi = n_col // n_lo
    nc = columns // 2
    size = blocks * width
    pairs = blocks // 2
    lanes = -(-rows // 128) * 128

    vmem = pl.BlockSpec(memory_space=pltpu.VMEM)
    smem = pl.BlockSpec(memory_space=pltpu.SMEM)
    hbm = pl.BlockSpec(memory_space=pl.ANY)
    out = jax.ShapeDtypeStruct((blocks, width, columns), jnp.bfloat16)
    dma = pltpu.SemaphoreType.DMA
    bf16 = jnp.bfloat16
    return pl.pallas_call(
        functools.partial(kernel, (n_sec, n_hi, n_lo)),
        out_shape=(out, out),
        in_specs=[smem, smem, hbm, hbm, hbm],
        out_specs=(vmem, vmem),
        scratch_shapes=[
            pltpu.VMEM((3, blocks, width, nc), bf16),
            pltpu.VMEM((2, blocks, width, width), bf16),
            pltpu.VMEM((blocks, noff, width, width), bf16),
            pltpu.VMEM((pairs, noff + 1, width, 2 * width), bf16),
            pltpu.VMEM((pairs, noff + 1, width, 2 * width), bf16),
            pltpu.VMEM((2, blocks, lanes), jnp.int32),
            pltpu.SMEM((2, blocks, lanes), jnp.int32),
            pltpu.VMEM((2, rows, width, size), bf16),
            pltpu.VMEM((3, size, nc), bf16),
            pltpu.VMEM((2, size, nc), bf16),
            pltpu.VMEM((3, n_lo - 1, n_hi, size, nc), bf16),
            pltpu.VMEM((3, n_lo - 1, n_hi, size, nc), bf16),
            pltpu.VMEM((3, n_hi - 1, size, nc), bf16),
            pltpu.VMEM((3, n_hi - 1, size, nc), bf16),
            pltpu.VMEM((3, size, nc), jnp.float32),
            pltpu.VMEM((3, size, nc), bf16),
            pltpu.VMEM((2, size, nc), bf16),
            dma((6,)),
            dma((3 + pairs,)),
            dma((3 + pairs,)),
            dma((3, n_lo - 1, n_hi)),
            dma((3, n_lo - 1, n_hi)),
            dma((3, n_hi - 1)),
            dma((3, n_hi - 1)),
            dma((3,)),
            dma((2,)),
            dma((2,)),
            dma((2,)),
        ],
        compiler_params=pltpu.CompilerParams(
            collective_id=0, has_side_effects=True, vmem_limit_bytes=60 * 1024 * 1024
        ),
    )(targets, row_slot, rhs, diag_inv, off_tiles)


def chains_kernel(
    dims, targets_ref, slot_ref, rhs_hbm, diag_hbm, off_hbm, sol_ref, hand_ref,
    rhs_ref, off_ref, pack_0, pack_1, pack_2, pack_3, diag_ref, idx_vec, idx_ref, rin, a_ref, w_ref,
    send1, recv1, send2, recv2, acc, xs, hs, ret,
    in_sem, fs_sem, fr_sem, rs_sem, rr_sem, s1_sem, r1_sem, s2_sem, r2_sem, p_sem, gs_sem, gr_sem,
):
    n_hi, n_lo = dims
    blocks, noff, width = off_hbm.shape[:3]
    lanes = idx_vec.shape[2]
    pairs = blocks // 2
    size = blocks * width
    packed = pairs * width
    wide = 2 * width
    sec = lax.axis_index("sec")
    col = lax.axis_index("col")
    plane, place = sec // 2, sec % 2
    hi, lo = col // n_lo, col % n_lo
    bf16, f32 = jnp.bfloat16, jnp.float32

    own_idx = pltpu.make_async_copy(idx_vec.at[sec], idx_ref.at[sec], in_sem.at[0])
    load_off = [
        pltpu.make_async_copy(
            off_hbm.at[pl.ds(2 * q, 2)], off_ref.at[pl.ds(2 * q, 2)], in_sem.at[3 + q]
        )
        for q in range(pairs)
    ]
    load_diag = pltpu.make_async_copy(diag_hbm, diag_ref.at[sec], in_sem.at[2])
    load_rhs = pltpu.make_async_copy(rhs_hbm, rhs_ref, in_sem.at[1])
    for load in (*load_off, load_diag, load_rhs):
        load.start()

    def hi_flip(o):
        value, bit = hi, 1
        while bit < n_hi:
            value = value + ((o // bit) % 2) * (bit - 2 * bit * ((value // bit) % 2))
            bit *= 2
        return value

    def at_sec(to):
        return {"sec": to, "col": col}

    lo_peer = {"sec": sec, "col": hi * n_lo + 1 - lo}

    def hi_peer(o):
        return {"sec": sec, "col": hi_flip(o) * n_lo + lo}

    barrier = pltpu.get_barrier_semaphore()
    peers = [lo_peer] + [hi_peer(o) for o in range(1, n_hi)]
    peers += [at_sec(lax.rem(sec + o, 4)) for o in range(1, 4)]
    for peer in peers:
        pl.semaphore_signal(barrier, inc=1, device_id=peer, device_id_type=MESH)

    slot_of_lane = lax.broadcasted_iota(jnp.int32, (1, lanes), 1)
    for k in range(blocks):
        found = jnp.full((1, lanes), noff, jnp.int32)
        for p in range(noff):
            dest = slot_ref[0, targets_ref[k, p]]
            found = jnp.where(slot_of_lane == dest, p, found)
        idx_vec[sec, k:k + 1, :] = found
    own_idx.start()
    packs = (pack_0, pack_1, pack_2, pack_3)
    for pack_ref in packs:
        for q in range(pairs):
            pack_ref[q, noff] = jnp.zeros((width, wide), bf16)

    left = lax.broadcasted_iota(jnp.int32, (width, wide), 1) < width

    def swap(x):
        return jnp.concatenate([x[:, width:], x[:, :width]], axis=1)

    def pack_into(pack_ref):
        for q in range(pairs):
            load_off[q].wait()

            def step(p, carry):
                pack_ref[q, p] = jnp.concatenate([off_ref[2 * q, p], off_ref[2 * q + 1, p]], axis=1)
                return carry

            lax.fori_loop(0, noff, step, 0, unroll=4)

    for s in range(4):
        @pl.when(sec == s)
        def _():
            pack_into(packs[s])

    load_diag.wait()
    load_rhs.wait()
    own_idx.wait()
    for m in range(2):
        part = slice(m * wide, (m + 1) * wide)
        for q in range(pairs):
            even, odd = rhs_ref[2 * q, :, part], rhs_ref[2 * q + 1, :, part]
            rows = slice(q * width, (q + 1) * width)
            rin[sec, 2 * m, rows] = jnp.where(left, even, swap(odd))
            rin[sec, 2 * m + 1, rows] = jnp.where(left, swap(even), odd)

    pl.semaphore_wait(barrier, len(peers))

    every = range(2 + pairs)
    def shares(s):
        cut = 3 if s == 1 else 2 + pairs // 2
        return range(cut), range(cut, 2 + pairs)


    def factor(s, to, step, pieces=every):
        ends = [idx_vec.at[s], diag_ref.at[s]]
        ends += [packs[s].at[q, pl.ds(0, noff)] for q in range(pairs)]
        return [
            pltpu.make_async_remote_copy(
                src_ref=ends[n], dst_ref=ends[n], send_sem=fs_sem.at[step, n], recv_sem=fr_sem.at[s, n],
                device_id=at_sec(to), device_id_type=MESH,
            )
            for n in pieces
        ]

    def start(copies):
        for copy in copies:
            copy.start()

    def wait_sent(copies):
        for copy in copies:
            copy.wait_send()

    def to_scalar_memory(s):
        to_scalar = pltpu.make_async_copy(idx_vec.at[s], idx_ref.at[s], in_sem.at[0])
        to_scalar.start()
        to_scalar.wait()

    def factor_here(s):
        for copy in factor(s, 0, 0):
            copy.wait_recv()
        to_scalar_memory(s)

    def by_core(act):
        for core in range(2):
            @pl.when(place == core)
            def _():
                act(core)

    def across(s, act):
        by_core(lambda core: act(factor(s, 2 - s // 2 * 2 + core, s, shares(s)[core])))

    def arrive(s):
        def step(core):
            onward = factor(s, s // 2 * -2 + 3 - core, s, shares(s)[core])
            for here_now, copy in zip(factor(s, 0, 0, shares(s)[core]), onward):
                here_now.wait_recv()
                copy.start()

        by_core(step)

    def relayed(s):
        by_core(lambda core: wait_sent(factor(s, 0, s, shares(s)[core])))

    def arrive_late(s):
        def step(core):
            for copy in factor(s, 0, 0, shares(s)[1 - core]):
                copy.wait_recv()

        by_core(step)
        to_scalar_memory(s)

    def chain_of(device):
        return 2 * (1 - device // 2) + device % 2

    mine = chain_of(sec)

    def rhs_copy(s, chain, to, step, slot):
        return pltpu.make_async_remote_copy(
            src_ref=rin.at[s, chain], dst_ref=rin.at[s, chain],
            send_sem=rs_sem.at[step], recv_sem=rr_sem.at[slot],
            device_id=at_sec(to), device_id_type=MESH,
        )

    def rhs_sends(s):
        if s == 0:
            return [rhs_copy(0, 1, 1, 0, 4), rhs_copy(0, 3, 1, 1, 0)]
        return [
            rhs_copy(s, 2 * (1 - to // 2) + to % 2, to, n, s)
            for n, to in enumerate(to for to in (s ^ 1, s ^ 2, s ^ 3))
        ]

    def rhs_here(s):
        rhs_copy(s, mine, 0, 0, s).wait_recv()

    other = plane * 2 + 1 - place
    for s in range(4):
        @pl.when(sec == s)
        def _():
            start(factor(s, s ^ 1, 0))

    for s in range(4):
        @pl.when(sec == s)
        def _():
            start(rhs_sends(s))

    def build(s, d):
        for r in range(blocks):
            i = d * blocks + r
            for q in range(pairs):
                at = (r % 2) * size + q * wide
                a_ref[s, d * pairs + r // 2, :, at:at + wide] = jnp.where(
                    left, packs[s][q, idx_ref[s, 2 * q, i]], packs[s][q, idx_ref[s, 2 * q + 1, i]]
                )

    def build_range(s, low, high):
        def step(d, carry):
            build(s, d)
            return carry

        lax.fori_loop(low, high, step, 0)

    def copy1(j, oh):
        return pltpu.make_async_remote_copy(
            src_ref=send1.at[j, oh], dst_ref=recv1.at[j, oh],
            send_sem=s1_sem.at[j, oh], recv_sem=r1_sem.at[j, oh],
            device_id=lo_peer, device_id_type=MESH,
        )

    def copy2(j, oh):
        return pltpu.make_async_remote_copy(
            src_ref=send2.at[j, oh - 1], dst_ref=recv2.at[j, oh - 1],
            send_sem=s2_sem.at[j, oh - 1], recv_sem=r2_sem.at[j, oh - 1],
            device_id=hi_peer(oh), device_id_type=MESH,
        )

    def give(which, j, s, chain):
        return pltpu.make_async_remote_copy(
            src_ref=(xs, hs)[which].at[j], dst_ref=ret.at[which, chain],
            send_sem=gs_sem.at[which, j], recv_sem=gr_sem.at[which, chain],
            device_id=at_sec(s), device_id_type=MESH,
        )

    def give_out(which, j, s, chain):
        @pl.when(sec == s)
        def _():
            ret[which, chain] = (xs, hs)[which][j]

        @pl.when(sec != s)
        def _():
            give(which, j, s, chain).start()

    def product(s, w, dest):
        a = a_ref[s, pl.ds(dest * pairs, pairs)].reshape(packed, 2 * size)
        return jnp.dot(a, w_ref[w], preferred_element_type=f32)

    def first(s, j, w, chain, h, fresh=None):
        for q in range(pairs):
            rows = slice(q * width, (q + 1) * width)
            residual = rin[s, chain, rows]
            if h is not None:
                residual = (residual.astype(f32) - h[rows].astype(f32)).astype(bf16)
            z = jnp.dot(
                diag_ref[s, 2 * q:2 * q + 2].reshape(wide, width), residual,
                preferred_element_type=f32,
            ).astype(bf16)
            top, low = z[:width], z[width:]
            xs[j, rows] = jnp.where(left, top, low)
            zero = jnp.zeros_like(top)
            at = q * wide
            w_ref[w, at:at + width] = jnp.where(left, top, zero)
            w_ref[w, at + width:at + wide] = jnp.where(left, swap(low), zero)
            w_ref[w, size + at:size + at + width] = jnp.where(left, zero, swap(top))
            w_ref[w, size + at + width:size + at + wide] = jnp.where(left, zero, low)

        def step(t, carry):
            oh = n_hi - 1 - t
            dest = hi_flip(oh) * n_lo + 1 - lo
            if fresh is not None:
                @pl.when(plane <= fresh)
                def _():
                    build(s, dest)

            send1[j, oh] = product(s, w, dest).astype(bf16)
            copy1(j, oh).start()
            return carry

        lax.fori_loop(0, n_hi, step, 0)
        give_out(0, j, s, chain)

    def middle(s, j, w, fresh=None, also=None):

        def step(t, carry):
            oh = n_hi - 1 - t
            dest = hi_flip(oh) * n_lo + lo
            if fresh is not None:
                @pl.when(plane <= fresh)
                def _():
                    build(s, dest)

            total = product(s, w, dest)
            copy1(j, oh).wait_recv()
            total = total + recv1[j, oh].astype(f32)

            @pl.when(oh > 0)
            def _():
                send2[j, oh - 1] = total.astype(bf16)
                copy2(j, oh).start()

            @pl.when(oh == 0)
            def _():
                acc[w] = total

            if also is not None:
                @pl.when(plane == 0)
                def _():
                    build(also, 2 * t)
                    build(also, 2 * t + 1)
            return carry

        lax.fori_loop(0, n_hi, step, 0)

    def last(j, w):
        total = acc[w]
        for oh in range(n_hi - 1, 0, -1):
            copy2(j, oh).wait_recv()
            total = total + recv2[j, oh - 1].astype(f32)
        hs[j] = total.astype(bf16)

    def sent(j, s):
        for oh in range(n_hi):
            copy1(j, oh).wait_send()
        for oh in range(1, n_hi):
            copy2(j, oh).wait_send()

        @pl.when(sec != s)
        def _():
            give(0, j, s, mine).wait_send()
            give(1, j, s, mine).wait_send()

    def pass_on():
        return pltpu.make_async_remote_copy(
            src_ref=hs.at[4], dst_ref=hs.at[0], send_sem=p_sem.at[0], recv_sem=p_sem.at[1],
            device_id=at_sec(2 + place), device_id_type=MESH,
        )

    def here(s):
        factor_here(s)
        if s > 0:
            rhs_here(s)

    @pl.when(plane == 0)
    def _():
        @pl.when(place == 0)
        def _():
            first(0, 0, 1, mine, None, fresh=1)
            first(0, 4, 0, place, None)
            here(1)
            across(1, start)
            middle(0, 0, 1, fresh=1)
            middle(0, 4, 0)
            last(0, 1)

        @pl.when(place == 1)
        def _():
            across(1, start)
            here(0)
            rhs_copy(0, 1, 0, 0, 4).wait_recv()
            rhs_copy(0, 3, 0, 0, 0).wait_recv()
            first(0, 4, 0, place, None, fresh=1)
            first(0, 0, 1, mine, None)
            middle(0, 4, 0, fresh=1)
            last(4, 0)
            pass_on().start()
            give_out(1, 4, 0, place)
            middle(0, 0, 1)
            last(0, 1)

    @pl.when(plane == 1)
    def _():
        @pl.when(place == 0)
        def _():
            across(2, start)
            here(3)

        @pl.when(place == 1)
        def _():
            here(2)
            across(2, start)

        build_range(2, 0, n_hi * n_lo)
        build_range(3, 0, n_hi * n_lo)
        arrive(1)
        arrive_late(1)
        rhs_here(1)
        across(2, wait_sent)
        across(3, start)
        pass_on().wait_recv()

    first(1, 1, 1, mine, hs.at[0], fresh=1)

    @pl.when(plane == 0)
    def _():
        @pl.when(place == 0)
        def _():
            last(4, 0)
            pass_on().start()
            give_out(1, 4, 0, place)

        give_out(1, 0, 0, mine)

    @pl.when((plane == 0) & (place == 1))
    def _():
        arrive(2)

    middle(1, 1, 1, fresh=1)

    @pl.when((plane == 0) & (place == 0))
    def _():
        arrive(2)

    last(1, 1)

    @pl.when(plane == 0)
    def _():
        arrive_late(2)
        rhs_here(2)

    first(2, 2, 1, mine, hs.at[1], fresh=0)
    give_out(1, 1, 1, mine)

    @pl.when((plane == 0) & (place == 1))
    def _():
        arrive(3)

    middle(2, 2, 1, fresh=0)

    @pl.when((plane == 0) & (place == 0))
    def _():
        arrive(3)

    last(2, 1)

    @pl.when(plane == 0)
    def _():
        arrive_late(3)
        rhs_here(3)

    def returned(which, chain):
        return pltpu.make_async_remote_copy(
            src_ref=xs.at[0], dst_ref=ret.at[which, chain],
            send_sem=gs_sem.at[which, 0], recv_sem=gr_sem.at[which, chain],
            device_id=at_sec(other), device_id_type=MESH,
        )

    def assemble(which, out):
        for m in range(2):
            returned(which, 2 * m + 1 - place).wait_recv()

            @pl.when((sec != 0) & (plane == m))
            def _():
                returned(which, 2 * m + place).wait_recv()

            part = slice(m * wide, (m + 1) * wide)
            for q in range(pairs):
                rows = slice(q * width, (q + 1) * width)
                one, two = ret[which, 2 * m, rows], ret[which, 2 * m + 1, rows]
                out[2 * q, :, part] = jnp.where(left, one, swap(two))
                out[2 * q + 1, :, part] = jnp.where(left, swap(one), two)

    first(3, 3, 1, mine, hs.at[2], fresh=0)
    give_out(1, 2, 2, mine)
    sent(1, 1)
    wait_sent(factor(0, other, 0))
    for s in range(4):
        @pl.when(sec == s)
        def _():
            wait_sent(rhs_sends(s))

    @pl.when(plane == 0)
    def _():
        sent(0, 0)
        for oh in range(n_hi):
            copy1(4, oh).wait_send()
        for oh in range(1, n_hi):
            copy2(4, oh).wait_send()

        @pl.when(sec != 0)
        def _():
            give(0, 4, 0, place).wait_send()
            give(1, 4, 0, place).wait_send()

        pass_on().wait_send()
        across(1, wait_sent)
        relayed(2)
        relayed(3)

    @pl.when(plane == 1)
    def _():
        across(3, wait_sent)
        relayed(1)

    middle(3, 3, 1, fresh=0)
    assemble(0, sol_ref)
    sent(2, 2)
    last(3, 1)
    give_out(1, 3, 3, mine)
    assemble(1, hand_ref)
    sent(3, 3)


def chains(n_col, rhs, diag_inv, off_tiles, targets, row_slot):
    blocks, width, columns = rhs.shape
    noff = off_tiles.shape[1]
    rows = row_slot.shape[1]
    n_lo = 2
    n_hi = n_col // n_lo
    size = blocks * width
    pairs = blocks // 2
    packed = pairs * width
    wide = 2 * width
    lanes = -(-rows // 128) * 128
    vmem = pl.BlockSpec(memory_space=pltpu.VMEM)
    smem = pl.BlockSpec(memory_space=pltpu.SMEM)
    hbm = pl.BlockSpec(memory_space=pl.ANY)
    out = jax.ShapeDtypeStruct((blocks, width, columns), jnp.bfloat16)
    dma = pltpu.SemaphoreType.DMA
    bf16 = jnp.bfloat16
    return pl.pallas_call(
        functools.partial(chains_kernel, (n_hi, n_lo)),
        out_shape=(out, out),
        in_specs=[smem, smem, hbm, hbm, hbm],
        out_specs=(vmem, vmem),
        scratch_shapes=[
            pltpu.VMEM((blocks, width, columns), bf16),
            pltpu.VMEM((blocks, noff, width, width), bf16),
            pltpu.VMEM((pairs, noff + 1, width, wide), bf16),
            pltpu.VMEM((pairs, noff + 1, width, wide), bf16),
            pltpu.VMEM((pairs, noff + 1, width, wide), bf16),
            pltpu.VMEM((pairs, noff + 1, width, wide), bf16),
            pltpu.VMEM((4, blocks, width, width), bf16),
            pltpu.VMEM((4, blocks, lanes), jnp.int32),
            pltpu.SMEM((4, blocks, lanes), jnp.int32),
            pltpu.VMEM((4, 4, packed, wide), bf16),
            pltpu.VMEM((4, rows // 2, width, 2 * size), bf16),
            pltpu.VMEM((2, 2 * size, wide), bf16),
            pltpu.VMEM((5, n_hi, packed, wide), bf16),
            pltpu.VMEM((5, n_hi, packed, wide), bf16),
            pltpu.VMEM((5, n_hi - 1, packed, wide), bf16),
            pltpu.VMEM((5, n_hi - 1, packed, wide), bf16),
            pltpu.VMEM((2, packed, wide), jnp.float32),
            pltpu.VMEM((5, packed, wide), bf16),
            pltpu.VMEM((5, packed, wide), bf16),
            pltpu.VMEM((2, 4, packed, wide), bf16),
            dma((3 + pairs,)),
            dma((4, 2 + pairs)),
            dma((4, 2 + pairs)),
            dma((3,)),
            dma((5,)),
            dma((5, n_hi)),
            dma((5, n_hi)),
            dma((5, n_hi - 1)),
            dma((5, n_hi - 1)),
            dma((2,)),
            dma((2, 5)),
            dma((2, 4)),
        ],
        compiler_params=pltpu.CompilerParams(
            collective_id=1, has_side_effects=True, vmem_limit_bytes=48 * 1024 * 1024
        ),
    )(*[pltpu.with_memory_space_constraint(x, pltpu.MemorySpace.HBM) for x in (targets, row_slot, rhs, diag_inv, off_tiles)])


def fits_chains(n_sec, n_col, rhs, row_slot):
    blocks, width, columns = rhs.shape
    n_hi = n_col // 2
    return (
        n_sec == 4 and n_col % 2 == 0 and n_hi & (n_hi - 1) == 0 and columns == 4 * width and width == 64
        and blocks % 2 == 0 and row_slot.shape[1] == blocks * n_col
    )


def shards(n_sec, n_col, rhs, diag_inv, off_tiles, targets, row_slot):
    if fits_chains(n_sec, n_col, rhs, row_slot):
        return chains(n_col, rhs, diag_inv, off_tiles, targets, row_slot)
    return mirrored(n_sec, n_col, rhs, diag_inv, off_tiles, targets, row_slot)


def solution(mesh):
    return jax.shard_map(
        functools.partial(shards, mesh.shape["sec"], mesh.shape["col"]),
        mesh=mesh,
        in_specs=(
            P(("sec", "col"), None, None),
            P(("sec", "col"), None, None),
            P(("sec", "col"), None, None, None),
            P(("sec", "col"), None),
            P("sec", None),
        ),
        out_specs=(P(("sec", "col"), None, None), P(("sec", "col"), None, None)),
        check_vma=False,
    )
```
